32 devices in a mesh: rollout: 4 (over y, x), context: 4 (over z), head: 2 (over core).
Axes of the slice: x: 2, y: 2, z: 4, core: 2. Of those that a mesh axis runs over, the one named last changes fastest.
Arguments:
- qkv: bfloat16 [3, 4, 512, 32, 128], P(None, 'rollout', 'context', 'head'), may hold values from -18 to 18
- ssd_b: bfloat16 [4, 512, 128], P('rollout', 'context'), may hold values from -5 to 5
- ssd_c: bfloat16 [4, 512, 128], P('rollout', 'context'), may hold values from -0.5 to 0.5
- step_size: float32 [4, 512, 64], P('rollout', 'context', 'head'), may hold values from 0 to 0.3, as said below
- decay_rate: float32 [64], P('head'), may hold values from 0.5 to 2
- value_weight: bfloat16 [4096], P('head'), may hold values from -0.09375 to 0.09375
- returns: float32 [4, 64], P('rollout'), may hold values from -4 to 4
- step_labels: int32 [4, 512], P('rollout', 'context'), may hold values from 0 to 63, never falling along the last dimension, each value on 1 to 128 neighbouring positions
- lengths: int32 [4], replicated, may hold values from 128 to 512, as said below
Outputs:
- loss: float32 [], replicated
- grad_qkv: bfloat16 [3, 4, 512, 32, 128], P(None, 'rollout', 'context', 'head')
- grad_b: float32 [4, 512, 128], P('rollout', 'context')
- grad_c: float32 [4, 512, 128], P('rollout', 'context')
- grad_step: float32 [4, 512, 64], P('rollout', 'context', 'head')
- grad_rate: float32 [64], P('head')
- grad_value: float32 [4096], P('head')
The draws below stay inside these ranges and needn't reach their ends.
Inputs may be any that keep to these rules, and one draw needn't show every extreme that they name: `step_size`: positive. `lengths`: one rollout in every draw is full. `step_labels`: never falling along a rollout.
All inputs are finite; a program needn't handle non-finite values.
Results may differ from the reference program's by a relative error of at most 0.011.
Values may be sent and summed in bfloat16 or wider, within the bound.
No kernel may reach another device: no remote copies, remote signals or barrier semaphores. Data moves between devices by JAX's collectives and lax.ppermute only.
A program may use at most 192 MiB of HBM per device.

```python
import math
import jax
import jax.numpy as jnp
import numpy as np
from jax import lax

TOK_DEV = 128
HA = 32
HD = 128
MH = 64
MP = 64
NS = 128
NSTEPS = 64
ROLLOUT_COUNT = 4
ROLLOUT_LENGTH = 512
STEP_MOST = 128


def draw_qkv(key, part):
    full_shape = (3, ROLLOUT_COUNT, ROLLOUT_LENGTH, HA, HD)
    base_draw = jnp.clip(jax.random.normal(key, full_shape, jnp.float32), -5.0, 5.0)
    return base_draw.astype(jnp.bfloat16)


def draw_step_size(key, part):
    quick_random_key, rate_random_key, jagged_random_key, spike_random_key = jax.random.split(key, 4)
    fast_share = 0.5
    fast_heads = jax.random.uniform(quick_random_key, (MH,), jnp.float32) < fast_share
    level = jax.random.uniform(rate_random_key, (MH,), jnp.float32)
    fast_rate = 1.0 / 50.0 * (50.0 / 30.0) ** level
    slow_rate = 0.05 / ROLLOUT_LENGTH * 6.0 ** level
    head_rate = jnp.where(fast_heads, fast_rate, slow_rate)
    roughness = jax.random.uniform(jagged_random_key, (ROLLOUT_COUNT, ROLLOUT_LENGTH, MH), jnp.float32, 0.5, 1.5)
    per_step_values = head_rate[None, None, :] * roughness
    spike_position = jax.random.randint(spike_random_key, (ROLLOUT_COUNT, 2), 0, ROLLOUT_LENGTH)
    spike_landed = jnp.any(jnp.arange(ROLLOUT_LENGTH)[None, :, None] == spike_position[:, None, :], axis=2)
    return jnp.where(spike_landed[:, :, None], 0.3, per_step_values).astype(jnp.float32)


def draw_lengths(key, part):
    key_len, key_full = jax.random.split(key)
    drawn = jax.random.randint(key_len, (ROLLOUT_COUNT,), ROLLOUT_LENGTH // 4, ROLLOUT_LENGTH + 1)
    chosen = jax.random.randint(key_full, (), 0, ROLLOUT_COUNT)
    return jnp.where(jnp.arange(ROLLOUT_COUNT) == chosen, ROLLOUT_LENGTH, drawn).astype(jnp.int32)


def block_levels(rng, extent, cuts, smallest, high):
    level, own = 1.0, jax.random.fold_in(rng, 6)
    for dim, parts in cuts:
        draws = jnp.exp(jax.random.uniform(jax.random.fold_in(own, dim), (parts,), jnp.float32, smallest / len(cuts), high / len(cuts)))
        level = level * jnp.repeat(draws, extent[dim] // parts).reshape([-1 if axis == dim else 1 for axis in range(len(extent))])
    return level


def length_profile(count, total, most, lean):
    loads = [(1 << 20) // math.isqrt(rank ** lean) + 1 for rank in range(2, count + 1)]
    surplus, given = total - most - (count - 1), [1] * (count - 1)
    while surplus > 0:
        candidates = [i for i in range(count - 1) if given[i] < most]
        mass, budget = sum([loads[i] for i in candidates]), surplus
        for i in candidates:
            addition = min(most - given[i], max(1, budget * loads[i] // mass), surplus)
            given[i] = given[i] + addition
            surplus = surplus - addition
    return np.array([most] + given)


def uneven_parts(rng, count, total, limit, skew):
    if count == 2:
        one = jax.random.randint(rng, (), max(1, total - limit), min(limit, total - 1) + 1)
        return jnp.stack([one, total - one])
    sizes = jnp.asarray(length_profile(count, total, limit, skew), jnp.int32)
    couples = (count - 1) // 2
    donor, receiver = sizes[1:1 + 2 * couples:2], sizes[2:2 + 2 * couples:2]
    slack = jnp.minimum(donor - 1, limit - receiver)
    moved = jax.random.randint(jax.random.fold_in(rng, 1), (couples,), 0, 1 << 20) % (slack + 1)
    sizes = sizes.at[1:1 + 2 * couples:2].set(donor - moved).at[2:2 + 2 * couples:2].set(receiver + moved)
    return sizes[jax.random.permutation(jax.random.fold_in(rng, 2), count)]


def bell_draw(own_key, shape, scale, reach, cuts=(), kind=jnp.bfloat16):
    loudness = block_levels(own_key, shape, cuts, -0.22, 0.18) if cuts else 1.0
    values = jax.random.normal(own_key, shape, jnp.float32) * scale * loudness
    return jnp.minimum(jnp.maximum(values, -reach), reach).astype(kind)


def setup_inputs(seed: int = 0) -> dict:
    keys = jax.random.split(jax.random.key(seed), 10)
    qkv = draw_qkv(jax.random.fold_in(keys[9], 71), 0)
    ssd_b = bell_draw(keys[1], (ROLLOUT_COUNT, ROLLOUT_LENGTH, NS), 1.0, 5.0, ((0, 4), (1, 4)))
    ssd_c = bell_draw(keys[2], (ROLLOUT_COUNT, ROLLOUT_LENGTH, NS), NS ** -0.5, 0.5, ((0, 4), (1, 4)))
    step_size = draw_step_size(jax.random.fold_in(keys[9], 71), 0)
    decay_rate = jnp.clip(jnp.exp(math.log(2.0) - 1.3862944 * jax.random.uniform(keys[4], (MH,), jnp.float32) ** block_levels(keys[4], (MH,), ((0, 2),), -0.2, 0.2)), 0.5, 2.0)
    value_weight = bell_draw(keys[5], (MH * MP,), (MH * MP) ** -0.5, 0.09375, ((0, 2),))
    returns = bell_draw(keys[6], (ROLLOUT_COUNT, NSTEPS), 1.0, 4.0, ((0, 4),), jnp.float32)
    step_labels = jax.vmap(lambda own: jnp.searchsorted(jnp.cumsum(uneven_parts(own, NSTEPS, ROLLOUT_LENGTH, STEP_MOST, 2)), jnp.arange(ROLLOUT_LENGTH), side="right"))(jax.random.split(keys[7], ROLLOUT_COUNT)).reshape((ROLLOUT_COUNT, ROLLOUT_LENGTH)).astype(jnp.int32)
    lengths = draw_lengths(jax.random.fold_in(keys[9], 71), 0)
    return dict(qkv=qkv, ssd_b=ssd_b, ssd_c=ssd_c, step_size=step_size, decay_rate=decay_rate, value_weight=value_weight, returns=returns, step_labels=step_labels, lengths=lengths)


MASK_FILL = -1e+30
NORM_EPS = 1e-05
HIGHEST_PREC = lax.Precision.HIGHEST

def block_probs(query_block, key_rows, first_row):
    head_size = query_block.shape[1]
    scores = lax.dot_general(query_block, key_rows, (((1,), (1,)), ((), ())), preferred_element_type=jnp.float32)
    scores = scores * (1.0 / math.sqrt(head_size))
    row_ids = first_row + jnp.arange(query_block.shape[0], dtype=jnp.int32)[:, None]
    col_ids = jnp.arange(key_rows.shape[0], dtype=jnp.int32)[None, :]
    scores = jnp.where(col_ids <= row_ids, scores, MASK_FILL)
    row_max = lax.stop_gradient(lax.optimization_barrier(jnp.max(scores, axis=1, keepdims=True)))
    weights = jnp.exp(scores - row_max)
    return weights / lax.optimization_barrier(jnp.sum(weights, axis=1, keepdims=True))

def head_forward(queries, key_rows, values, offset):
    block_rows = min(512, queries.shape[0])
    block_count = queries.shape[0] // block_rows
    blocks = queries.reshape(block_count, block_rows, queries.shape[1])
    starts = offset + jnp.arange(block_count, dtype=jnp.int32) * block_rows

    def one_block(operands):
        probability = block_probs(operands[0], key_rows, operands[1]).astype(jnp.bfloat16)
        return jnp.dot(probability, values, preferred_element_type=jnp.float32).astype(jnp.bfloat16)
    return lax.map(one_block, (blocks, starts)).reshape(queries.shape)

def head_backward(queries, key_rows, values, grad_out, offset):
    head_size = queries.shape[1]
    block_rows = min(512, queries.shape[0])
    block_count = queries.shape[0] // block_rows
    blocks = queries.reshape(block_count, block_rows, head_size)
    grad_blocks = grad_out.reshape(block_count, block_rows, head_size)
    starts = offset + jnp.arange(block_count, dtype=jnp.int32) * block_rows

    def one_block(carried, operands):
        key_grad, value_grad = carried
        query_block, grad_block, first_row = operands
        probability = block_probs(query_block, key_rows, first_row)
        rounded = probability.astype(jnp.bfloat16)
        value_grad = value_grad + lax.dot_general(rounded, grad_block, (((0,), (0,)), ((), ())), preferred_element_type=jnp.float32)
        prob_grad = lax.dot_general(grad_block, values, (((1,), (1,)), ((), ())), preferred_element_type=jnp.float32)
        centre = lax.optimization_barrier(jnp.sum(probability * prob_grad, axis=1, keepdims=True))
        score_grad = (probability * (prob_grad - centre) * (1.0 / math.sqrt(head_size))).astype(jnp.bfloat16)
        query_grad = jnp.dot(score_grad, key_rows, preferred_element_type=jnp.float32).astype(jnp.bfloat16)
        key_grad = key_grad + lax.dot_general(score_grad, query_block, (((0,), (0,)), ((), ())), preferred_element_type=jnp.float32)
        return ((key_grad, value_grad), query_grad)
    zero_grad = jnp.zeros(key_rows.shape, jnp.float32)
    totals, query_grad = lax.scan(one_block, (zero_grad, zero_grad), (blocks, grad_blocks, starts))
    return (query_grad.reshape(queries.shape), totals[0], totals[1])

def attend(queries, key_rows, values, offset):

    def per_head(operands):
        return head_forward(operands[0], operands[1], operands[2], offset)
    result = lax.map(per_head, (jnp.swapaxes(queries, 0, 1), jnp.swapaxes(key_rows, 0, 1), jnp.swapaxes(values, 0, 1)))
    return jnp.swapaxes(result, 0, 1)

def attend_back(queries, key_rows, values, grad_out, offset):

    def per_head(operands):
        return head_backward(operands[0], operands[1], operands[2], operands[3], offset)
    query_grad, key_grad, value_grad = lax.map(per_head, (jnp.swapaxes(queries, 0, 1), jnp.swapaxes(key_rows, 0, 1), jnp.swapaxes(values, 0, 1), jnp.swapaxes(grad_out, 0, 1)))
    return (jnp.swapaxes(query_grad, 0, 1), jnp.swapaxes(key_grad, 0, 1), jnp.swapaxes(value_grad, 0, 1))

def ssd_parts(inputs, step_dt, rate, b_proj):
    cumulative = jnp.cumsum(-step_dt * rate[None, :], axis=0)
    tail_decay = jnp.exp(cumulative[-1:, :] - cumulative)
    state_term = jnp.einsum('th,thp,tn->hpn', tail_decay, inputs, b_proj, precision=HIGHEST_PREC)
    return (jnp.exp(cumulative[-1]), state_term)

def ssd_output(inputs, step_dt, rate, b_proj, c_proj, state_in):
    cumulative = jnp.cumsum(-step_dt * rate[None, :], axis=0)
    cum_heads = cumulative.T
    row_count = inputs.shape[0]
    causal = (jnp.arange(row_count)[:, None] >= jnp.arange(row_count)[None, :])[None]
    log_gap = jnp.where(causal, cum_heads[:, :, None] - cum_heads[:, None, :], 0.0)
    decay_mask = jnp.where(causal, jnp.exp(log_gap), 0.0)
    inner_prod = lax.optimization_barrier(jnp.sum(c_proj[:, None, :] * b_proj[None, :, :], axis=2))
    local_out = jnp.einsum('hts,shp->thp', decay_mask * inner_prod[None], inputs, precision=HIGHEST_PREC)
    carried = jnp.einsum('tn,hpn->thp', c_proj, state_in, precision=HIGHEST_PREC) * jnp.exp(cumulative)[:, :, None]
    return local_out + carried

def value_part(outputs, weight):
    norm_scale = lax.rsqrt(lax.optimization_barrier(jnp.mean(outputs * outputs, axis=2, keepdims=True)) + NORM_EPS)
    normed = (outputs * norm_scale).reshape(outputs.shape[0], -1)
    return jnp.dot(normed, weight, precision=HIGHEST_PREC)

def whole_ssd(inputs, step_dt, rate, b_proj, c_proj):
    pieces = inputs.shape[0] // TOK_DEV

    def split_rows(array):
        return array.reshape((pieces, TOK_DEV) + array.shape[1:])

    def advance(state_in, operands):
        part_in, part_step, part_b, part_c = operands
        outputs = ssd_output(part_in, part_step, rate, part_b, part_c, state_in)
        decays, state_term = ssd_parts(part_in, part_step, rate, part_b)
        return (decays[:, None, None] * state_in + state_term, outputs)
    zero_state = jnp.zeros((inputs.shape[1], inputs.shape[2], b_proj.shape[1]), jnp.float32)
    final_state, outputs = lax.scan(advance, zero_state, (split_rows(inputs), split_rows(step_dt), split_rows(b_proj), split_rows(c_proj)))
    return outputs.reshape(inputs.shape)

def post_attention(attended, step_dt, rate, b_proj, c_proj, weight):
    inputs = attended.reshape(attended.shape[0], MH, MP).astype(jnp.float32)
    return value_part(whole_ssd(inputs, step_dt, rate, b_proj, c_proj), weight)

def reference(qkv, ssd_b, ssd_c, step_size, decay_rate, value_weight, returns, step_labels, lengths):
    weight_full = value_weight.astype(jnp.float32)

    def per_rollout(operands):
        qkv_one, b_one, c_one, step_one, table_one, labels_one, length_one = operands
        zero_offset = jnp.int32(0)
        attended = attend(qkv_one[0], qkv_one[1], qkv_one[2], zero_offset)
        b_rows = b_one.astype(jnp.float32)
        c_rows = c_one.astype(jnp.float32)
        value, post_back = jax.vjp(post_attention, attended, step_one, decay_rate, b_rows, c_rows, weight_full)
        onehot = (labels_one[:, None] == jnp.arange(NSTEPS, dtype=jnp.int32)[None, :]).astype(jnp.float32)
        target = jnp.dot(onehot, table_one, precision=HIGHEST_PREC)
        valid_mask = (jnp.arange(value.shape[0], dtype=jnp.int32) < length_one).astype(jnp.float32)
        error_term = (value - target) * valid_mask
        loss_one = 0.5 * jnp.sum(error_term * error_term)
        attended_grad, step_grad, rate_grad, b_grad, c_grad, weight_grad = post_back(error_term)
        query_grad, key_grad, value_grad = attend_back(qkv_one[0], qkv_one[1], qkv_one[2], attended_grad, zero_offset)
        qkv_grad = jnp.stack([query_grad, key_grad.astype(jnp.bfloat16), value_grad.astype(jnp.bfloat16)])
        return (loss_one, qkv_grad, b_grad, c_grad, step_grad, rate_grad, weight_grad)
    losses, qkv_grads, b_grads, c_grads, step_grads, rate_grads, weight_grads = lax.map(per_rollout, (jnp.swapaxes(qkv, 0, 1), ssd_b, ssd_c, step_size, returns, step_labels, lengths))
    loss = jnp.sum(losses) / jnp.sum(lengths).astype(jnp.float32)
    return (loss, jnp.swapaxes(qkv_grads, 0, 1), b_grads, c_grads, step_grads, lax.optimization_barrier(jnp.sum(rate_grads, axis=0)), lax.optimization_barrier(jnp.sum(weight_grads, axis=0)))
```

```python
import functools
import math

import jax
import jax.numpy as jnp
from jax import lax
from jax.experimental import pallas as pl
from jax.experimental.pallas import tpu as pltpu
from jax.sharding import PartitionSpec as P

MASK_FILL = -1e30
NORM_EPS = 1e-05
HIGHEST = lax.Precision.HIGHEST
LOG2E = 1.4426950408889634
F32 = jnp.float32
BF16 = jnp.bfloat16
VMEM_LIMIT = 56 * 1024 * 1024
ANY = pl.BlockSpec(memory_space=pl.ANY)
VM = pl.BlockSpec(memory_space=pltpu.VMEM)
SM = pl.BlockSpec(memory_space=pltpu.SMEM)


def dot(a, b, precision=None):
    return jnp.dot(a, b, preferred_element_type=F32, precision=precision)


def dot_nt(a, b, precision=None):
    return lax.dot_general(a, b, (((1,), (1,)), ((), ())), preferred_element_type=F32, precision=precision)


def dot_tn(a, b, precision=None):
    return lax.dot_general(a, b, (((0,), (0,)), ((), ())), preferred_element_type=F32, precision=precision)


def iota(shape, dim):
    return lax.broadcasted_iota(jnp.int32, shape, dim)


def mat(cond):
    return jnp.where(cond, 1.0, 0.0).astype(F32)


class Sizes:
    def __init__(self, n, tokens, heads_local, head_dim, ssd_local, state):
        self.n, self.t, self.hl, self.hd, self.ns = n, tokens, heads_local, head_dim, state
        self.s = n * tokens
        self.a = heads_local // n
        self.groups = 2 if self.a % 2 == 0 else 1
        self.ag = self.a // self.groups
        self.h = ssd_local // n
        self.hg = self.h // self.groups
        self.mp = heads_local * head_dim // ssd_local
        self.fg = self.ag * head_dim
        self.f = self.a * head_dim
        self.r = -(-(self.h + 1) // 8) * 8
        self.rows = min(256, self.s)
        self.blocks = self.s // self.rows
        self.static = self.blocks <= 2

    def each_block(self, body):
        if self.static:
            for i in range(self.blocks):
                body(i)
        else:

            @pl.loop(0, self.blocks)
            def _(i):
                body(i)

    def upto(self, i):
        return (i + 1) * self.rows if self.static else self.s

    def onward(self, i):
        return i * self.rows if self.static else 0

    def block(self, i):
        return pl.ds(i * self.rows if self.static else pl.multiple_of(i * self.rows, self.rows), self.rows)


def call(kernel, name, out_shape, in_specs, out_specs, scratch, args, flops=0, nbytes=0):
    return pl.pallas_call(
        kernel,
        name=name,
        out_shape=out_shape,
        in_specs=in_specs,
        out_specs=out_specs,
        scratch_shapes=scratch,
        compiler_params=pltpu.CompilerParams(vmem_limit_bytes=VMEM_LIMIT),
        cost_estimate=pl.CostEstimate(flops=flops, bytes_accessed=nbytes, transcendentals=0),
    )(*args)


def prep_kernel(z, info, qkv, *refs):
    outs, (held, sems) = refs[: z.n * z.groups], refs[z.n * z.groups :]
    for c in range(3):
        held[c] = jnp.swapaxes(qkv[c, 0], 0, 1)
    me = info[0]
    copies = []
    for g in range(z.groups):
        for s in range(z.n):
            first = lax.rem(me + s, z.n) * z.a + g * z.ag
            copies.append(
                pltpu.make_async_copy(
                    held.at[:, pl.ds(first, z.ag)], outs[g * z.n + s], sems.at[g, s]
                )
            )
            copies[-1].start()
    for one in copies:
        one.wait()


def finish_kernel(z, info, *refs):
    count = z.n * z.groups
    ins, out, (held, sems) = refs[:count], refs[count], refs[count + 1 :]
    me = info[0]
    copies = []
    for g in range(z.groups):
        for s in range(z.n):
            first = lax.rem(me + z.n - s, z.n) * z.a + g * z.ag
            copies.append(
                pltpu.make_async_copy(
                    ins[g * z.n + s], held.at[:, pl.ds(first, z.ag)], sems.at[g, s]
                )
            )
            copies[-1].start()
    for one in copies:
        one.wait()
    for c in range(3):
        out[c, 0] = jnp.swapaxes(held[c], 0, 1)


def gather_blocks(z, info, ins, target, sems, slot, rows_dim):
    me = info[0]
    copies = []
    for s in range(z.n):
        source = lax.rem(me + z.n - s, z.n)
        if rows_dim is None:
            place = target.at[source]
        else:
            place = target.at[:, :, pl.ds(pl.multiple_of(source * z.t, z.t), z.t)]
        one = pltpu.make_async_copy(ins[s], place, sems.at[slot, s])
        one.start()
        copies.append(one)
    return copies


def decay_terms(z, dt_rows, rates, g):
    causal = mat(iota((z.t, z.t), 0) >= iota((z.t, z.t), 1))
    spread = mat(iota((z.r, z.fg), 0) == g * z.hg + iota((z.r, z.fg), 1) // z.mp)
    cum = dot(dot_nt(causal, dt_rows, HIGHEST), spread, HIGHEST) * (-rates)
    mid = 0.5 * cum[z.t - 1 : z.t]
    return jnp.exp(cum - mid), jnp.exp(mid - cum), jnp.exp(mid)


def forward_kernel(z, g, info, *refs):
    n = z.n
    qkvs, bcs, pays, wr = refs[:n], refs[n : 2 * n], refs[2 * n : 3 * n], refs[3 * n]
    prob, attended, normed, slope, states, value = refs[3 * n + 1 : 3 * n + 7]
    held, bc, pay, state, sems = refs[3 * n + 7 :]
    first = gather_blocks(z, info, qkvs, held, sems, 0, 2)
    later = gather_blocks(z, info, bcs, bc, sems, 1, None)
    later += gather_blocks(z, info, pays, pay, sems, 2, None)
    for one in first:
        one.wait()
    factor = LOG2E / math.sqrt(z.hd)

    def attend(i):
        width = z.upto(i)
        rows = z.block(i)
        keep = iota((z.rows, width), 1) <= i * z.rows + iota((z.rows, width), 0)
        for a in range(z.ag):
            scores = dot_nt(held[0, a, rows, :], held[1, a, :width, :])
            scores = jnp.where(keep, scores, MASK_FILL)
            weights = jnp.exp2((scores - jnp.max(scores, axis=1, keepdims=True)) * factor)
            weights = weights * (1.0 / jnp.sum(weights, axis=1, keepdims=True))
            weights = weights.astype(BF16)
            prob[a, rows, :width] = weights
            attended[rows, a * z.hd : (a + 1) * z.hd] = dot(weights, held[2, a, :width, :]).astype(BF16)

    z.each_block(attend)
    for one in later:
        one.wait()
    weight, rates = wr[0:1], wr[1:2]
    causal = iota((z.t, z.t), 0) >= iota((z.t, z.t), 1)
    same_head = mat(iota((z.hd, z.hd), 0) // z.mp == iota((z.hd, z.hd), 1) // z.mp).astype(BF16)
    state[...] = jnp.zeros_like(state)

    def chunk(c):
        rows = pl.ds(c * z.t if isinstance(c, int) else pl.multiple_of(c * z.t, z.t), z.t)
        up, down, mid = decay_terms(z, pay[c], rates, g)
        b, cp = bc[c, 0], bc[c, 1]
        inner = jnp.where(causal, dot_nt(cp, b), 0.0).astype(BF16)
        x = (down * attended[rows, :].astype(F32)).astype(BF16)
        carried = (mid * state[...]).astype(BF16)
        states[c] = carried
        y = up * (dot(inner, x) + dot(cp, carried))
        state[...] = mid * (mid * state[...] + dot_tn(b, x))
        total = jnp.zeros((z.t, z.hd), F32)
        for a in range(z.ag):
            lanes = slice(a * z.hd, (a + 1) * z.hd)
            ya = y[:, lanes]
            scale = lax.rsqrt(dot((ya * ya).astype(BF16), same_head) * (1.0 / z.mp) + NORM_EPS)
            unit = ya * scale
            term = unit * weight[:, lanes]
            total = total + term
            high = term.astype(BF16)
            mean = (dot(high, same_head) + dot((term - high.astype(F32)).astype(BF16), same_head)) * (1.0 / z.mp)
            normed[rows, lanes] = unit.astype(BF16)
            slope[rows, lanes] = scale * (weight[:, lanes] - unit * mean)
        row = dot_nt(jnp.ones((8, z.hd), F32), total, HIGHEST)
        value[:, rows] = row[0:1]

    if z.static:
        for c in range(n):
            chunk(c)
    else:
        pl.loop(0, n)(chunk)


def forward(z, g, info, qkvs, bcs, pays, wr):
    shape = jax.ShapeDtypeStruct
    outs = (
        shape((z.ag, z.s, z.s), BF16),
        shape((z.s, z.fg), BF16),
        shape((z.s, z.fg), BF16),
        shape((z.s, z.fg), F32),
        shape((z.n, z.ns, z.fg), BF16),
        shape((1, z.s), F32),
    )
    scratch = [
        pltpu.VMEM((3, z.ag, z.s, z.hd), BF16),
        pltpu.VMEM((z.n, 2, z.t, z.ns), BF16),
        pltpu.VMEM((z.n, z.r, z.t), F32),
        pltpu.VMEM((z.ns, z.fg), F32),
        pltpu.SemaphoreType.DMA((3, z.n)),
    ]
    return call(
        functools.partial(forward_kernel, z, g),
        "forward_%d" % g,
        outs,
        [SM] + [ANY] * (3 * z.n) + [VM],
        [VM] * 6,
        scratch,
        (info, *qkvs, *bcs, *pays, wr),
        flops=z.ag * z.s * z.s * z.hd * 4,
        nbytes=z.ag * z.s * z.s * 8,
    )


def ssd_back_kernel(z, info, *refs):
    n, groups = z.n, z.groups
    values, refs = refs[:n], refs[n:]
    bcs, pays, refs = refs[:n], refs[n : 2 * n], refs[2 * n :]
    wr, rate_rows, refs = refs[0], refs[1], refs[2:]
    saved, refs = [refs[4 * g : 4 * g + 4] for g in range(groups)], refs[4 * groups :]
    grads, refs = refs[:groups], refs[groups:]
    keep_out, give_out, step_out, small_out = refs[:4]
    bc, pay, dstates, sems = refs[4], refs[5], refs[6 : 6 + groups], refs[6 + groups]
    copies = gather_blocks(z, info, bcs, bc, sems, 0, None)
    copies += gather_blocks(z, info, pays, pay, sems, 1, None)
    for one in copies:
        one.wait()
    head, length = info[1], info[2]
    value = values[0][...]
    for s in range(1, n):
        value = value + values[s][...]
    t = z.t
    row_id, col_id = iota((t, t), 0), iota((t, t), 1)
    causal = row_id >= col_id
    after = mat(col_id >= row_id)
    before = mat(col_id < row_id)
    for d in dstates:
        d[...] = jnp.zeros_like(d)
    small_out[...] = jnp.zeros_like(small_out)
    features = z.f // z.hd

    def chunk(step):
        c = n - 1 - step
        if isinstance(c, int):
            rows = pl.ds(c * t, t)
            value_row = value[:, c * t : (c + 1) * t]
        else:
            rows = pl.ds(pl.multiple_of(c * t, t), t)
            value_row = jnp.zeros((1, t), F32)
            for j in range(n):
                value_row = jnp.where(c == j, value[:, j * t : (j + 1) * t], value_row)
        dt_rows = pay[c]
        valid = c * t + iota((1, t), 1) < length
        error = jnp.where(valid, value_row - dt_rows[z.h : z.h + 1], 0.0)
        small_out[features + 1 : features + 2, :] += 0.5 * error * error
        error8 = jnp.broadcast_to(error, (8, t))
        error_col = jnp.transpose(jnp.broadcast_to(error, (t, t)))
        b, cp = bc[c, 0], bc[c, 1]
        inner = jnp.where(causal, dot_nt(cp, b), 0.0)
        inner_low = inner.astype(BF16)
        w_sum = jnp.zeros((t, t), F32)
        grad_c = jnp.zeros((t, z.ns), F32)
        grad_b = jnp.zeros((t, z.ns), F32)
        gain = jnp.zeros((t, t), F32)
        for g in range(groups):
            attended, normed, slope, states = saved[g]
            up, down, mid = decay_terms(z, dt_rows, wr[1:2, g * z.fg : (g + 1) * z.fg], g)
            per_head = mat(iota((z.fg, t), 1) == g * z.hg + iota((z.fg, t), 0) // z.mp)
            unit = normed[rows, :].astype(F32)
            weight_grad = dot(error8, unit, HIGHEST)
            for a in range(z.ag):
                small_out[g * z.ag + a : g * z.ag + a + 1, :] += weight_grad[0:1, a * z.hd : (a + 1) * z.hd]
            x = (down * attended[rows, :].astype(F32)).astype(BF16)
            error_wide = jnp.concatenate([error_col] * z.ag, axis=1)
            d = (up * (error_wide * slope[rows, :])).astype(BF16)
            state_in = states[c]
            dstate = mid * dstates[g][...]
            dstate_low = dstate.astype(BF16)
            local = dot_tn(inner_low, d)
            outer = dot(b, dstate_low)
            carried = dot(cp, state_in)
            grads[g][rows, :] = (down * (local + outer)).astype(BF16)
            dstates[g][...] = mid * (dstate + dot_tn(cp, d))
            grad_c += dot_nt(d, state_in)
            grad_b += dot_nt(x, dstate_low)
            down_sum = dot(d.astype(F32) * carried, per_head, HIGHEST)
            up_sum = dot(x.astype(F32) * outer, per_head, HIGHEST)
            through = jnp.sum(dstate * state_in.astype(F32), axis=0, keepdims=True)
            through = dot(jnp.broadcast_to(through, (8, z.fg)), per_head, HIGHEST)
            gain += dot(after, down_sum, HIGHEST) + dot(before, up_sum, HIGHEST) + through[0:1]
            parts = []
            for k in range(z.hg):
                lanes = slice(k * z.mp // z.hd * z.hd, (k * z.mp // z.hd + 1) * z.hd)
                mine = iota((t, z.hd), 1) // z.mp == k % (z.hd // z.mp)
                d_head = jnp.where(mine, d[:, lanes], jnp.zeros((), BF16))
                w = jnp.where(causal, dot_nt(d_head, x[:, lanes]), 0.0)
                w_sum += w
                parts.append((w * inner).astype(BF16))
            straddle = dot(after.astype(BF16), jnp.concatenate(parts, axis=1))
            for k in range(z.hg):
                strict = jnp.where(col_id < row_id, straddle[:, k * t : (k + 1) * t], 0.0)
                gain += jnp.where(col_id == g * z.hg + k, jnp.sum(strict, axis=1, keepdims=True), 0.0)
        w_low = w_sum.astype(BF16)
        grad_c += dot(w_low, b)
        grad_b += dot_tn(w_low, cp)
        keep_out[c] = jnp.where(head == 0, grad_b, grad_c)
        give_out[c] = jnp.where(head == 0, grad_c, grad_b).astype(BF16)
        gain_rows = jnp.transpose(gain)[: z.r]
        step_out[c] = -rate_rows[...] * gain_rows
        rate_part = jnp.sum(dt_rows * gain_rows, axis=1, keepdims=True)
        lane = iota((z.r, t), 1) == iota((z.r, t), 0)
        small_out[features : features + 1, :] -= jnp.sum(jnp.where(lane, rate_part, 0.0), axis=0, keepdims=True)

    if z.static:
        for step in range(n):
            chunk(step)
    else:
        pl.loop(0, n)(chunk)


def ssd_back(z, info, values, bcs, pays, wr, rate_rows, saved):
    shape = jax.ShapeDtypeStruct
    small_rows = -(-(z.f // z.hd + 2) // 8) * 8
    outs = (
        *[shape((z.s, z.fg), BF16)] * z.groups,
        shape((z.n, z.t, z.ns), F32),
        shape((z.n, z.t, z.ns), BF16),
        shape((z.n, z.r, z.t), F32),
        shape((small_rows, z.t), F32),
    )
    scratch = [
        pltpu.VMEM((z.n, 2, z.t, z.ns), BF16),
        pltpu.VMEM((z.n, z.r, z.t), F32),
        *[pltpu.VMEM((z.ns, z.fg), F32)] * z.groups,
        pltpu.SemaphoreType.DMA((2, z.n)),
    ]
    flat = [x for group in saved for x in group]
    return call(
        functools.partial(ssd_back_kernel, z),
        "ssd_back",
        outs,
        [SM] + [VM] * z.n + [ANY] * (2 * z.n) + [VM] * (2 + len(flat)),
        [VM] * len(outs),
        scratch,
        (info, *values, *bcs, *pays, wr, rate_rows, *flat),
        flops=z.s * z.f * z.ns * 20,
        nbytes=z.s * z.f * 32,
    )


def attend_back_kernel(z, info, *refs):
    n = z.n
    qkvs, prob, grad = refs[:n], refs[n], refs[n + 1]
    outs, (held, result, dscore, sems, out_sems) = refs[n + 2 : 2 * n + 2], refs[2 * n + 2 :]
    for one in gather_blocks(z, info, qkvs, held, sems, 0, 2):
        one.wait()
    factor = 1.0 / math.sqrt(z.hd)
    for a in range(z.ag):
        lanes = slice(a * z.hd, (a + 1) * z.hd)

        def by_query(i):
            width, rows = z.upto(i), z.block(i)
            p = prob[a, rows, :width].astype(F32)
            dp = dot_nt(grad[rows, lanes], held[2, a, :width, :])
            product = p * dp
            ds = (product - p * jnp.sum(product, axis=1, keepdims=True)).astype(BF16)
            dscore[rows, :width] = ds
            result[0, a, rows, :] = (dot(ds, held[1, a, :width, :]) * factor).astype(BF16)

        z.each_block(by_query)

        def by_key(j):
            first, cols = z.onward(j), z.block(j)
            result[1, a, cols, :] = (dot_tn(dscore[first:, cols], held[0, a, first:, :]) * factor).astype(BF16)
            result[2, a, cols, :] = dot_tn(prob[a, first:, cols], grad[first:, lanes]).astype(BF16)

        z.each_block(by_key)
    me = info[0]
    copies = []
    for s in range(n):
        place = pl.ds(pl.multiple_of(lax.rem(me + s, n) * z.t, z.t), z.t)
        copies.append(pltpu.make_async_copy(result.at[:, :, place], outs[s], out_sems.at[s]))
        copies[-1].start()
    for one in copies:
        one.wait()


def attend_back(z, g, info, qkvs, prob, grad):
    shape = jax.ShapeDtypeStruct
    scratch = [
        pltpu.VMEM((3, z.ag, z.s, z.hd), BF16),
        pltpu.VMEM((3, z.ag, z.s, z.hd), BF16),
        pltpu.VMEM((z.s, z.s), BF16),
        pltpu.SemaphoreType.DMA((1, z.n)),
        pltpu.SemaphoreType.DMA((z.n,)),
    ]
    return call(
        functools.partial(attend_back_kernel, z),
        "attend_back_%d" % g,
        [shape((3, z.ag, z.t, z.hd), BF16)] * z.n,
        [SM] + [ANY] * z.n + [VM] * 2,
        [ANY] * z.n,
        scratch,
        (info, *qkvs, prob, grad),
        flops=z.ag * z.s * z.s * z.hd * 8,
        nbytes=z.ag * z.s * z.s * 8,
    )


def shift(x, axis, size, step):
    return lax.ppermute(x, axis, [(i, (i + step) % size) for i in range(size)])


def spread(parts, axis):
    return [parts[0]] + [shift(x, axis, len(parts), s) for s, x in enumerate(parts) if s]


def total_over(x, axis):
    return sum(spread([x] * lax.axis_size(axis), axis))


def local(qkv, ssd_b, ssd_c, step_size, decay_rate, value_weight, returns, step_labels, lengths):
    n = lax.axis_size("context")
    me = lax.axis_index("context")
    head = lax.axis_index("head")
    z = Sizes(n, qkv.shape[2], qkv.shape[3], qkv.shape[4], step_size.shape[2], ssd_b.shape[2])
    my_length = lax.dynamic_index_in_dim(lengths, lax.axis_index("rollout"), 0, keepdims=False)
    info = jnp.stack([me, head, my_length, me]).astype(jnp.int32)
    shape = jax.ShapeDtypeStruct

    sends = call(
        functools.partial(prep_kernel, z),
        "prep",
        [shape((3, z.ag, z.t, z.hd), BF16)] * (n * z.groups),
        [SM, VM],
        [ANY] * (n * z.groups),
        [pltpu.VMEM((3, z.hl, z.t, z.hd), BF16), pltpu.SemaphoreType.DMA((z.groups, n))],
        (info, qkv),
        nbytes=qkv.size * 4,
    )
    both = jnp.stack([ssd_b[0], ssd_c[0]])
    bcs = spread([both] * n, "context")
    table = returns[0]
    onehot = (step_labels[0][:, None] == jnp.arange(table.shape[0], dtype=jnp.int32)[None, :]).astype(F32)
    target = jnp.sum(onehot * table[None, :], axis=1)
    steps = step_size[0].T.reshape(n, z.h, z.t)
    pay = jnp.concatenate(
        [
            steps,
            jnp.broadcast_to(target[None, None, :], (n, 1, z.t)),
            jnp.zeros((n, z.r - z.h - 1, z.t), F32),
        ],
        axis=1,
    )
    pays = spread(
        [lax.dynamic_index_in_dim(pay, (me + s) % n, 0, keepdims=False) for s in range(n)], "context"
    )
    rates = lax.dynamic_slice_in_dim(decay_rate, me * z.h, z.h)
    weights = lax.dynamic_slice_in_dim(value_weight, me * z.f, z.f).astype(F32)
    wr = jnp.stack([weights, jnp.repeat(rates, z.mp)])
    rate_rows = jnp.broadcast_to(jnp.pad(rates, (0, z.r - z.h))[:, None], (z.r, z.t))

    arrived = [spread(sends[g * n : (g + 1) * n], "context") for g in range(z.groups)]
    probs, saved, value = [], [], None
    for g in range(z.groups):
        prob, attended, normed, slope, states, part = forward(
            z, g, info, arrived[g], bcs, pays, wr[:, g * z.fg : (g + 1) * z.fg]
        )
        probs.append(prob)
        saved.append((attended, normed, slope, states))
        value = part if value is None else value + part
    value = total_over(value, "head")
    values = spread([value] * n, "context")
    *grads, keep, give, steps_out, small = ssd_back(z, info, values, bcs, pays, wr, rate_rows, saved)

    mine = (keep + total_over_other(give)).astype(BF16)
    proj = spread(
        [lax.dynamic_index_in_dim(mine, (me + s) % n, 0, keepdims=False) for s in range(n)], "context"
    )
    step_parts = spread(
        [lax.dynamic_index_in_dim(steps_out, (me + s) % n, 0, keepdims=False) for s in range(n)], "context"
    )
    small_parts = spread([small] * n, "context")

    finals = []
    for g in range(z.groups):
        finals += spread(attend_back(z, g, info, arrived[g], probs[g], grads[g]), "context")
    qkv_grad = call(
        functools.partial(finish_kernel, z),
        "finish",
        shape((3, 1, z.t, z.hl, z.hd), BF16),
        [SM] + [ANY] * (n * z.groups),
        VM,
        [pltpu.VMEM((3, z.hl, z.t, z.hd), BF16), pltpu.SemaphoreType.DMA((z.groups, n))],
        (info, *finals),
        nbytes=qkv.size * 4,
    )
    proj_sum = sum(x.astype(F32) for x in proj)
    other = shift(proj_sum, "head", 2, 1)
    b_grad = jnp.where(head == 0, proj_sum, other)
    c_grad = jnp.where(head == 0, other, proj_sum)

    order = (me - jnp.arange(n)) % n
    step_grad = jnp.stack([x[: z.h] for x in step_parts])[order].reshape(n * z.h, z.t).T
    gathered = total_over(jnp.stack(small_parts), "rollout")
    features = z.f // z.hd
    loss = jnp.sum(gathered[0, features + 1]) / jnp.sum(lengths).astype(F32)
    gathered = gathered[order]
    weight_grad = gathered[:, :features].reshape(-1)
    rate_grad = gathered[:, features, : z.h].reshape(-1)
    return loss, qkv_grad, b_grad[None], c_grad[None], step_grad[None], rate_grad, weight_grad


def total_over_other(x):
    return shift(x, "head", 2, 1).astype(F32)


def solution(mesh):
    in_specs = (
        P(None, "rollout", "context", "head", None),
        P("rollout", "context", None),
        P("rollout", "context", None),
        P("rollout", "context", "head"),
        P("head"),
        P("head"),
        P("rollout", None),
        P("rollout", "context"),
        P(),
    )
    out_specs = (
        P(),
        P(None, "rollout", "context", "head", None),
        P("rollout", "context", None),
        P("rollout", "context", None),
        P("rollout", "context", "head"),
        P("head"),
        P("head"),
    )
    return jax.shard_map(local, mesh=mesh, in_specs=in_specs, out_specs=out_specs, check_vma=False)
```

```python
import functools
import math

import jax
import jax.numpy as jnp
from jax import lax
from jax.experimental import pallas as pl
from jax.experimental.pallas import tpu as pltpu
from jax.sharding import PartitionSpec as P

MASK_FILL = -1e30
NORM_EPS = 1e-05
HIGHEST = lax.Precision.HIGHEST
LOG2E = 1.4426950408889634
GROUPS = (2, 2)
F32 = jnp.float32
BF16 = jnp.bfloat16

ANY = pl.BlockSpec(memory_space=pl.ANY)
SHAPE = jax.ShapeDtypeStruct
VM = pl.BlockSpec(memory_space=pltpu.VMEM)
SM = pl.BlockSpec(memory_space=pltpu.SMEM)


def dot(a, b, precision=None):
    return jnp.dot(a, b, preferred_element_type=F32, precision=precision)


def dot_nt(a, b, precision=None):
    return lax.dot_general(a, b, (((1,), (1,)), ((), ())), preferred_element_type=F32, precision=precision)


def dot_tn(a, b, precision=None):
    return lax.dot_general(a, b, (((0,), (0,)), ((), ())), preferred_element_type=F32, precision=precision)


def iota(shape, dim):
    return lax.broadcasted_iota(jnp.int32, shape, dim)


def mat(cond):
    return jnp.where(cond, 1.0, 0.0).astype(F32)


class Sizes:
    def __init__(self, n, tokens, heads_local, head_dim, ssd_local, state):
        self.n, self.t, self.hl, self.hd, self.ns = n, tokens, heads_local, head_dim, state
        self.s = n * tokens
        self.a = heads_local // n
        self.sizes = GROUPS if sum(GROUPS) == self.a else (self.a,)
        self.first = [sum(self.sizes[:g]) for g in range(len(self.sizes))]
        self.groups = len(self.sizes)
        self.h = ssd_local // n
        self.hl_ssd = ssd_local
        self.mp = heads_local * head_dim // ssd_local
        self.f = self.a * head_dim
        self.r = -(-(self.h + 1) // 8) * 8
        self.rp = -(-self.r // 16) * 16
        self.features = self.f // head_dim
        self.v = -(-(self.features + 2) // 8) * 8
        self.rows = min(256, self.s)
        self.blocks = self.s // self.rows
        self.static = self.blocks <= 2
        self.up, self.down, self.mid = 0, self.s, 2 * self.s
        self.pay = self.mid + 8 * n
        self.rate = self.pay + self.r * n
        self.weight = self.rate + self.r
        self.term_rows = self.weight + 8
        self.pay_rows = tokens + 2 * self.rp

    def sent_rows(self, g):
        return 3 * self.sizes[g] * self.t + (0 if g else self.pay_rows)

    def back_rows(self, g):
        rows = 3 * self.sizes[g] * self.t
        if g == 0:
            rows += self.t + self.rp + 2 * self.v
        return rows

    def rows_of(self, g, k, a):
        first = (k * self.sizes[g] + a) * self.t
        return slice(first, first + self.t)

    def lanes(self, g):
        return pl.ds(self.first[g] * self.hd, self.sizes[g] * self.hd)

    def each_block(self, body):
        if self.static:
            for i in range(self.blocks):
                body(i)
        else:

            @pl.loop(0, self.blocks)
            def _(i):
                body(i)

    def upto(self, i):
        return (i + 1) * self.rows if self.static else self.s

    def onward(self, i):
        return i * self.rows if self.static else 0

    def each_chunk(self, body):
        if self.static:
            for c in range(self.n):
                body(c)
        else:

            @pl.loop(0, self.n)
            def _(c):
                body(c)

    def chunk(self, c, base=0):
        return pl.ds(base + c * self.t if isinstance(c, int) else pl.multiple_of(base + c * self.t, self.t), self.t)

    def small(self, c, base, rows):
        return pl.ds(base + c * rows if isinstance(c, int) else pl.multiple_of(base + c * rows, 8), rows)

    def block(self, i):
        return pl.ds(i * self.rows if self.static else pl.multiple_of(i * self.rows, self.rows), self.rows)


def call(z, kernel, name, out_shape, in_specs, out_specs, scratch, args, flops=0, nbytes=0):
    return pl.pallas_call(
        functools.partial(kernel, z),
        name=name,
        out_shape=out_shape,
        in_specs=in_specs,
        out_specs=out_specs,
        scratch_shapes=scratch,
        compiler_params=pltpu.CompilerParams(vmem_limit_bytes=(14 if z.static else 56) * 1024 * 1024),
        cost_estimate=pl.CostEstimate(flops=flops, bytes_accessed=nbytes, transcendentals=0),
    )(*args)


def in_hbm(x):
    return pltpu.with_memory_space_constraint(x, pltpu.HBM)


class Copies:
    def __init__(self, sems):
        self.sems, self.count = sems, 0

    def start(self, source, target):
        one = pltpu.make_async_copy(source, target, self.sems.at[self.count])
        self.count += 1
        one.start()
        return one


def wait_all(copies):
    for one in copies:
        one.wait()


def split3(x):
    high = x.astype(BF16)
    rest = x - high.astype(F32)
    middle = rest.astype(BF16)
    return high, middle, (rest - middle.astype(F32)).astype(BF16)


def split2_dot(x, exact):
    high, low = split3(x)[:2]
    return dot(high, exact) + dot(low, exact)


def prep_kernel(z, qkv, b_in, c_in, step_in, labels_in, table_in, *refs):
    outs, refs = refs[: z.n * z.groups], refs[z.n * z.groups :]
    held, (parts, b, c, step, labels, table, sems) = refs[: z.groups], refs[z.groups :]
    me, core = lax.axis_index("context"), lax.axis_index("head")
    mover = Copies(sems)
    loads = [mover.start(qkv.at[k, 0], parts.at[k]) for k in range(3)]
    tiny = [
        mover.start(b_in.at[0], b),
        mover.start(c_in.at[0], c),
        mover.start(step_in.at[0], step),
        mover.start(labels_in, labels),
        mover.start(table_in, table),
    ]
    wait_all(tiny)
    onehot = mat(iota((table.shape[1], z.t), 0) == labels[...])
    target = dot(table[...], onehot, HIGHEST)
    mine = jnp.where(core == 0, b[...], c[...])
    end = 3 * z.sizes[0] * z.t
    for j in range(z.n):
        row = iota((z.r, z.hl_ssd), 0)
        pick = mat((iota((z.r, z.hl_ssd), 1) == j * z.h + row) & (row < z.h))
        pay = dot(pick, step[...], HIGHEST)
        pay = jnp.where(iota((z.r, z.t), 0) == z.h, target, pay)
        held[0][j, end : end + z.t] = mine
        held[0][j, end + z.t :] = jnp.zeros((2 * z.rp, z.t), BF16)
        for i, term in enumerate(split3(pay)[:2]):
            start = end + z.t + i * z.rp
            held[0][j, start : start + z.r] = term
    for k in range(3):
        loads[k].wait()
        turned = jnp.swapaxes(parts[k], 0, 1)
        for g in range(z.groups):
            for j in range(z.n):
                for a in range(z.sizes[g]):
                    held[g][j, z.rows_of(g, k, a), :] = turned[j * z.a + z.first[g] + a]
    copies = []
    for g in range(z.groups):
        for s in range(z.n):
            copies.append(mover.start(held[g].at[lax.rem(me + s, z.n)], outs[g * z.n + s]))
    wait_all(copies)


def prep(z, qkv, b, c, step, labels, table):
    args = [in_hbm(x) for x in (qkv, b, c, step, labels, table)]
    return call(
        z,
        prep_kernel,
        "prep",
        [SHAPE((z.sent_rows(g), z.hd), BF16) for g in range(z.groups) for _ in range(z.n)],
        [ANY] * 6,
        [ANY] * (z.n * z.groups),
        [
            *[pltpu.VMEM((z.n, z.sent_rows(g), z.hd), BF16) for g in range(z.groups)],
            pltpu.VMEM((3, z.t, z.hl, z.hd), BF16),
            pltpu.VMEM((z.t, z.ns), BF16),
            pltpu.VMEM((z.t, z.ns), BF16),
            pltpu.VMEM(step.shape[1:], F32),
            pltpu.VMEM(labels.shape, jnp.int32),
            pltpu.VMEM(table.shape, F32),
            pltpu.SemaphoreType.DMA((8 + z.n * z.groups,)),
        ],
        args,
        nbytes=qkv.size * 4,
    )


def pick_kernel(z, *refs):
    ins, (mine, pay, parts, sems) = refs[: z.n], refs[z.n :]
    me = lax.axis_index("context")
    mover = Copies(sems)
    rows = pl.ds(3 * z.sizes[0] * z.t, z.pay_rows)
    wait_all([mover.start(ins[s].at[rows], parts.at[s]) for s in range(z.n)])
    for s in range(z.n):
        source = lax.rem(me + z.n - s, z.n)
        mine[source] = parts[s, : z.t]
        terms = [parts[s, z.t + k * z.rp : z.t + k * z.rp + z.r].astype(F32) for k in range(2)]
        pay[source] = terms[0] + terms[1]


def pick(z, ins):
    return call(
        z,
        pick_kernel,
        "pick",
        (SHAPE((z.n, z.t, z.ns), BF16), SHAPE((z.n, z.r, z.t), F32)),
        [ANY] * z.n,
        [VM] * 2,
        [pltpu.VMEM((z.n, z.pay_rows, z.t), BF16), pltpu.SemaphoreType.DMA((z.n,))],
        ins,
    )


def decay_kernel(z, mine, theirs, pay, rate, weight, terms, bc):
    n, t = z.n, z.t
    me, core = lax.axis_index("context"), lax.axis_index("head")
    heads = z.hl_ssd
    row, col = iota((z.r, heads), 0), iota((z.r, heads), 1)
    pick = mat((col == me * z.h + row) & (row < z.h))
    terms[z.rate : z.rate + z.r, :t] = dot_nt(pick, jnp.broadcast_to(rate[...], (t, heads)), HIGHEST)
    pick = mat(iota((8, z.hl), 1) == me * z.a + iota((8, z.hl), 0))
    terms[z.weight : z.weight + 8, : z.hd] = dot(pick, weight[...].astype(F32))
    rates = jnp.broadcast_to(rate[...], (8, heads))
    rates = dot(rates, mat(iota((heads, z.f), 0) == me * z.h + iota((heads, z.f), 1) // z.mp), HIGHEST)
    rates = rates[0:1]
    for c in range(n):
        bc[c, 0] = jnp.where(core == 0, mine[c], theirs[c])
        bc[c, 1] = jnp.where(core == 0, theirs[c], mine[c])
        terms[z.pay + c * z.r : z.pay + (c + 1) * z.r, :t] = pay[c]
    causal = iota((t, t), 0) >= iota((t, t), 1)
    lower = mat(causal)
    spread_heads = mat(iota((z.r, z.f), 0) == iota((z.r, z.f), 1) // z.mp)

    def chunk(c):
        steps = terms[z.small(c, z.pay, z.r), :t]
        cum = dot(dot_nt(lower, steps, HIGHEST), spread_heads, HIGHEST) * (-rates)
        half = 0.5 * cum[t - 1 : t]
        terms[z.chunk(c, z.up), :] = jnp.exp(cum - half)
        terms[z.chunk(c, z.down), :] = jnp.exp(half - cum)
        terms[z.small(c, z.mid, 8), :] = jnp.broadcast_to(jnp.exp(half), (8, z.f))
        inner = split3(jnp.where(causal, dot_nt(bc[c, 1], bc[c, 0]), 0.0))
        bc[c, 2] = inner[0]
        bc[c, 3] = inner[1]

    z.each_chunk(chunk)


def decay(z, mine, theirs, pay, rate, weight):
    return call(
        z,
        decay_kernel,
        "decay",
        (SHAPE((z.term_rows, z.f), F32), SHAPE((z.n, 4, z.t, z.ns), BF16)),
        [VM] * 5,
        [VM] * 2,
        [],
        (mine, theirs, pay, rate, weight),
        nbytes=8 * z.s * z.f,
    )


def attend_kernel(z, g, *refs):
    n, t, count = z.n, z.t, z.sizes[g]
    ins, refs = refs[:n], refs[n + (1 if g else 0) :]
    prob_out, attended_out, qkv_out, held, prob, attended, sems = refs
    mover = Copies(sems)
    me = lax.axis_index("context")
    rows = pl.ds(0, 3 * count * t)
    wait_all([mover.start(ins[s].at[rows], held.at[lax.rem(me + n - s, n)]) for s in range(n)])
    stores = [mover.start(held, qkv_out)]

    def rows_upto(k, a, width):
        return held[: width // t, z.rows_of(g, k, a), :].reshape(width, z.hd)

    def rows_block(k, a, i):
        per = z.rows // t
        return held[pl.ds(i * per, per), z.rows_of(g, k, a), :].reshape(z.rows, z.hd)

    factor = LOG2E / math.sqrt(z.hd)
    for a in range(count):

        def attend(i):
            width = z.upto(i)
            rows = z.block(i)
            scores = dot_nt(rows_block(0, a, i), rows_upto(1, a, width))
            keep = iota((z.rows, width), 1) <= i * z.rows + iota((z.rows, width), 0)
            scores = jnp.where(keep, scores, MASK_FILL)
            weight = jnp.exp2((scores - jnp.max(scores, axis=1, keepdims=True)) * factor)
            weight = (weight * (1.0 / jnp.sum(weight, axis=1, keepdims=True))).astype(BF16)
            prob[a, rows, :width] = weight
            attended[rows, a * z.hd : (a + 1) * z.hd] = dot(weight, rows_upto(2, a, width)).astype(BF16)

        z.each_block(attend)
        stores.append(mover.start(prob.at[a], prob_out.at[a]))
    stores.append(mover.start(attended, attended_out))
    wait_all(stores)


def attend(z, g, ins, after):
    count = z.sizes[g]
    outs = (
        SHAPE((count, z.s, z.s), BF16),
        SHAPE((z.s, count * z.hd), BF16),
        SHAPE((z.n, 3 * count * z.t, z.hd), BF16),
    )
    scratch = [
        pltpu.VMEM((z.n, 3 * count * z.t, z.hd), BF16),
        pltpu.VMEM((count, z.s, z.s), BF16),
        pltpu.VMEM((z.s, count * z.hd), BF16),
        pltpu.SemaphoreType.DMA((z.n + 2 + count,)),
    ]
    return call(
        z,
        lambda z, *refs: attend_kernel(z, g, *refs),
        "attend_%d" % g,
        outs,
        [ANY] * (z.n + len(after)),
        [ANY] * 3,
        scratch,
        (*ins, *after),
        flops=count * z.s * z.s * z.hd * 4,
        nbytes=count * z.s * z.s * 8,
    )


def ssd_kernel(z, *refs):
    n, t = z.n, z.t
    ins, refs = refs[: z.groups], refs[z.groups :]
    terms, bc, saved_out, value, attended, saved, state_low, adds, sems = refs
    mover = Copies(sems)
    wait_all([mover.start(ins[g], attended.at[:, z.lanes(g)]) for g in range(z.groups)])
    same_head = mat(iota((z.hd, z.hd), 0) // z.mp == iota((z.hd, z.hd), 1) // z.mp).astype(BF16)

    def enter(c):
        rows = z.chunk(c)
        high, low = split3(terms[z.chunk(c, z.down), :] * attended[rows, :].astype(F32))[:2]
        saved[0, rows, :] = high
        saved[5, rows, :] = low
        adds[rows, :] = dot_tn(bc[c, 0], high) + dot_tn(bc[c, 0], low)

    z.each_chunk(enter)

    def step(c, state):
        m = terms[z.small(c, z.mid, 8), :][0:1]
        state = m * state
        high, low = split3(state)[:2]
        saved[3, z.chunk(c), :] = high
        state_low[z.chunk(c), :] = low
        return m * (state + adds[z.chunk(c), :])

    state = jnp.zeros((z.ns, z.f), F32)
    if z.static:
        for c in range(n):
            state = step(c, state)
    else:
        lax.fori_loop(0, n, step, state)

    def leave(c):
        rows = z.chunk(c)
        up = terms[z.chunk(c, z.up), :]
        left = [bc[c, k] for k in (2, 2, 3, 1, 1)]
        right = [saved[0, rows, :], saved[5, rows, :], saved[0, rows, :], saved[3, rows, :], state_low[rows, :]]
        y = up * dot(jnp.concatenate(left, axis=1), jnp.concatenate(right, axis=0))
        total = jnp.zeros((t, z.hd), F32)
        for a in range(z.a):
            part = slice(a * z.hd, (a + 1) * z.hd)
            ya = y[:, part]
            weight = terms[z.weight + a : z.weight + a + 1, : z.hd]
            scale = lax.rsqrt(split2_dot(ya * ya, same_head) * (1.0 / z.mp) + NORM_EPS)
            unit = ya * scale
            term = unit * weight
            total = total + term
            mean = split2_dot(term, same_head) * (1.0 / z.mp)
            saved[1, rows, part] = unit.astype(BF16)
            slope = split3(up[:, part] * scale * (weight - unit * mean))
            saved[2, rows, part] = slope[0]
            saved[4, rows, part] = slope[1]
        high, low = split3(total)[:2]
        ones = jnp.ones((8, z.hd), BF16)
        value[:, rows] = (dot_nt(ones, high) + dot_nt(ones, low))[0:1]

    z.each_chunk(leave)
    mover.start(saved, saved_out).wait()


def ssd(z, ins, terms, bc):
    return call(
        z,
        ssd_kernel,
        "ssd",
        (SHAPE((6, z.s, z.f), BF16), SHAPE((1, z.s), F32)),
        [ANY] * z.groups + [VM] * 2,
        [ANY, VM],
        [
            pltpu.VMEM((z.s, z.f), BF16),
            pltpu.VMEM((6, z.s, z.f), BF16),
            pltpu.VMEM((z.s, z.f), BF16),
            pltpu.VMEM((z.n * z.ns, z.f), F32),
            pltpu.SemaphoreType.DMA((1 + z.groups,)),
        ],
        (*ins, terms, bc),
        flops=z.s * z.f * z.ns * 20,
        nbytes=z.s * z.f * 32,
    )


def ssd_back_kernel(z, *refs):
    n, t = z.n, z.t
    lengths, values, refs = refs[0], refs[1 : n + 1], refs[n + 1 :]
    terms, bc_in, refs = refs[0], refs[1], refs[2:]
    saved_in, refs = refs[0], refs[1:]
    grad_out, keep_out, give_out, step_out, vec, refs = *refs[:5], refs[5:]
    down, small, bc, saved, d, adds, dstates, through, grads, sems = refs
    mover = Copies(sems)

    def load(k):
        return [mover.start(saved_in.at[k], saved.at[k])]

    loads = load(2) + load(4) + [
        mover.start(bc_in, bc),
        mover.start(terms.at[pl.ds(z.mid, z.term_rows - z.mid)], small),
    ]
    later = load(3) + load(1)
    last = load(0) + load(5) + [mover.start(terms.at[pl.ds(z.down, z.s)], down)]
    me, core = lax.axis_index("context"), lax.axis_index("head")
    length = lengths[lax.axis_index("rollout")]
    value = values[0][...]
    for s in range(1, n):
        value = value + values[s][...]
    row_id, col_id = iota((t, t), 0), iota((t, t), 1)
    causal = row_id >= col_id
    strict = row_id > col_id
    after = mat(col_id >= row_id).astype(BF16)
    before = mat(strict).astype(BF16)
    per_head = mat(iota((z.f, t), 1) == iota((z.f, t), 0) // z.mp).astype(BF16)
    per_row = mat(iota((z.h * t, t), 1) == iota((z.h * t, t), 0) // t).astype(BF16)
    vec[...] = jnp.zeros_like(vec)
    wait_all(loads)

    def pays(c):
        return small[z.small(c, z.pay - z.mid, z.r), :t]

    def enter(c):
        rows = z.chunk(c)
        if z.static:
            value_row = value[:, c * t : (c + 1) * t]
        else:
            value_row = jnp.zeros((1, t), F32)
            for j in range(n):
                value_row = jnp.where(c == j, value[:, j * t : (j + 1) * t], value_row)
        valid = c * t + iota((1, t), 1) < length
        error = jnp.where(valid, value_row - pays(c)[z.h : z.h + 1], 0.0)
        vec[z.features + 1 : z.features + 2, :] += 0.5 * error * error
        column = jnp.transpose(jnp.broadcast_to(error, (t, t)))
        wide = jnp.concatenate([column] * (z.f // t), axis=1)
        dc = split3(wide * (saved[2, rows, :].astype(F32) + saved[4, rows, :].astype(F32)))[:2]
        d[0, rows, :] = dc[0]
        d[1, rows, :] = dc[1]
        adds[rows, :] = dot_tn(bc[c, 1], dc[0]) + dot_tn(bc[c, 1], dc[1])
        high, low = split3(error)[:2]
        pair = jnp.concatenate([high, low, jnp.zeros((6, t), BF16)], axis=0)
        weight_grad = dot(pair, saved[1, rows, :])
        weight_grad = weight_grad[0:1] + weight_grad[1:2]
        for a in range(z.features):
            vec[a : a + 1, :] += weight_grad[:, a * z.hd : (a + 1) * z.hd]

    wait_all(later)
    z.each_chunk(enter)

    def carry(c, dstate):
        m = small[z.small(c, 0, 8), :][0:1]
        rows = z.chunk(c)
        dstate = m * dstate
        dstates[rows, :] = dstate.astype(BF16)
        sums = jnp.sum(dstate * saved[3, rows, :].astype(F32), axis=0, keepdims=True)
        through[z.small(c, 0, 8), :] = jnp.broadcast_to(sums, (8, z.f))
        return m * (dstate + adds[rows, :])

    dstate = jnp.zeros((z.ns, z.f), F32)
    if z.static:
        for c in range(n - 1, -1, -1):
            dstate = carry(c, dstate)
    else:
        lax.fori_loop(0, n, lambda k, v: carry(n - 1 - k, v), dstate)
    wait_all(last)

    def leave(c):
        rows = z.chunk(c)
        b, cp, inner = bc[c, 0], bc[c, 1], bc[c, 2]
        dc, dl = d[0, rows, :], d[1, rows, :]
        xc, xl, state_in, dstate_in = saved[0, rows, :], saved[5, rows, :], saved[3, rows, :], dstates[rows, :]
        local = dot_tn(inner, dc) + dot_tn(inner, dl)
        outer = dot(b, dstate_in)
        carried = dot(cp, state_in)
        grads[rows, :] = (down[rows, :] * (local + outer)).astype(BF16)
        grad_c = dot_nt(dc, state_in) + dot_nt(dl, state_in)
        grad_b = dot_nt(xc, dstate_in)
        down_sum = dot(((dc.astype(F32) + dl.astype(F32)) * carried).astype(BF16), per_head)
        up_sum = dot((xc.astype(F32) * outer).astype(BF16), per_head)
        inner_wide = inner.astype(F32)
        w_sum = jnp.zeros((t, t), F32)
        parts = []
        for k in range(z.h):
            first = k * z.mp // z.hd * z.hd
            mine = iota((t, z.hd), 1) // z.mp == k % (z.hd // z.mp)
            pair = slice(first, first + z.hd)
            x_head = jnp.where(mine, xc[:, pair], jnp.zeros((), BF16))
            x_low = jnp.where(mine, xl[:, pair], jnp.zeros((), BF16))
            left = jnp.concatenate([dc[:, pair], dl[:, pair], dc[:, pair]], axis=1)
            w = jnp.where(causal, dot_nt(left, jnp.concatenate([x_head, x_head, x_low], axis=1)), 0.0)
            w_sum += w
            parts.append((w * inner_wide).astype(BF16))
        straddle = dot(after, jnp.concatenate(parts, axis=1))
        straddle = jnp.concatenate(
            [jnp.where(strict, straddle[:, k * t : (k + 1) * t], 0.0).astype(BF16) for k in range(z.h)], axis=1
        )
        sums = [*split3(down_sum)[:2], *split3(up_sum)[:2]]
        gain = dot(
            jnp.concatenate([after, after, before, before], axis=1), jnp.concatenate(sums, axis=0)
        ) + dot(straddle, per_row)
        gain = gain + split2_dot(through[z.small(c, 0, 8), :], per_head)[0:1]
        w_low = w_sum.astype(BF16)
        grad_c += dot(w_low, b)
        grad_b += dot_tn(w_low, cp)
        keep_out[c] = jnp.where(core == 0, grad_b, grad_c)
        give_out[c] = jnp.where(core == 0, grad_c, grad_b).astype(BF16)
        gain_rows = jnp.transpose(gain)[: z.r]
        step_out[c] = -small[z.rate - z.mid : z.rate - z.mid + z.r, :t] * gain_rows
        rate_part = jnp.sum(pays(c) * gain_rows, axis=1, keepdims=True)
        lane = (iota((z.r, t), 1) == me * z.h + iota((z.r, t), 0)) & (iota((z.r, t), 0) < z.h)
        vec[z.features : z.features + 1, :] -= jnp.sum(jnp.where(lane, rate_part, 0.0), axis=0, keepdims=True)

    z.each_chunk(leave)
    mover.start(grads, grad_out).wait()


def ssd_back(z, lengths, values, terms, bc, saved):
    outs = (
        SHAPE((z.s, z.f), BF16),
        SHAPE((z.n, z.t, z.ns), F32),
        SHAPE((z.n, z.t, z.ns), BF16),
        SHAPE((z.n, z.r, z.t), F32),
        SHAPE((z.v, z.t), F32),
    )
    scratch = [
        pltpu.VMEM((z.s, z.f), F32),
        pltpu.VMEM((z.term_rows - z.mid, z.f), F32),
        pltpu.VMEM((z.n, 4, z.t, z.ns), BF16),
        pltpu.VMEM((6, z.s, z.f), BF16),
        pltpu.VMEM((2, z.s, z.f), BF16),
        pltpu.VMEM((z.n * z.ns, z.f), F32),
        pltpu.VMEM((z.n * z.ns, z.f), BF16),
        pltpu.VMEM((z.n * 8, z.f), F32),
        pltpu.VMEM((z.s, z.f), BF16),
        pltpu.SemaphoreType.DMA((10,)),
    ]
    return call(
        z,
        ssd_back_kernel,
        "ssd_back",
        outs,
        [SM] + [VM] * z.n + [ANY] * 3,
        [ANY] + [VM] * 4,
        scratch,
        (lengths, *values, terms, bc, saved),
        flops=z.s * z.f * z.ns * 20,
        nbytes=z.s * z.f * 32,
    )


def attend_back_kernel(z, g, *refs):
    n, t, count = z.n, z.t, z.sizes[g]
    qkv, prob_in, grad_in, refs = *refs[:3], refs[3:]
    if g == 0:
        keep, other, step, vec, refs = *refs[:4], refs[4:]
    else:
        refs = refs[1:]
    outs, refs = refs[:n], refs[n:]
    held, prob, grad, result, dscore, sems = refs
    mover = Copies(sems)
    me = lax.axis_index("context")
    first = [mover.start(grad_in.at[:, z.lanes(g)], grad), mover.start(qkv, held)]
    probs = [mover.start(prob_in.at[a], prob.at[a]) for a in range(count)]
    if g == 0:
        end = 3 * count * t
        for j in range(n):
            result[j, end : end + t] = (keep[j] + other[j].astype(F32)).astype(BF16)
            result[j, end + t :] = jnp.zeros((z.rp + 2 * z.v, t), BF16)
            result[j, end + t : end + t + z.r] = step[j].astype(BF16)
            result[j, end + t + z.rp :] = jnp.concatenate(split3(vec[...])[:2], axis=0)
    wait_all(first)
    factor = 1.0 / math.sqrt(z.hd)
    per = z.rows // t

    def rows_span(k, a, first, last):
        return held[first // t : last // t, z.rows_of(g, k, a), :].reshape(last - first, z.hd)

    def store(k, a, i, x):
        result[pl.ds(i * per, per), z.rows_of(g, k, a), :] = x.astype(BF16).reshape(per, t, z.hd)

    for a in range(count):
        lanes = slice(a * z.hd, (a + 1) * z.hd)
        probs[a].wait()

        def by_query(i):
            width, rows = z.upto(i), z.block(i)
            p = prob[a, rows, :width].astype(F32)
            dp = dot_nt(grad[rows, lanes], rows_span(2, a, 0, width))
            product = p * dp
            ds = (product - p * jnp.sum(product, axis=1, keepdims=True)).astype(BF16)
            dscore[a, rows, :width] = ds
            store(0, a, i, dot(ds, rows_span(1, a, 0, width)) * factor)

        z.each_block(by_query)

        def by_key(j):
            start, cols = z.onward(j), z.block(j)
            store(1, a, j, dot_tn(dscore[a, start:, cols], rows_span(0, a, start, z.s)) * factor)
            store(2, a, j, dot_tn(prob[a, start:, cols], grad[start:, lanes]))

        z.each_block(by_key)
    wait_all([mover.start(result.at[lax.rem(me + s, n)], outs[s]) for s in range(n)])


def attend_back(z, g, qkv, prob, grad, small):
    count = z.sizes[g]
    rows = z.back_rows(g)
    scratch = [
        pltpu.VMEM((z.n, 3 * count * z.t, z.hd), BF16),
        pltpu.VMEM((count, z.s, z.s), BF16),
        pltpu.VMEM((z.s, count * z.hd), BF16),
        pltpu.VMEM((z.n, rows, z.hd), BF16),
        pltpu.VMEM((count, z.s, z.s), BF16),
        pltpu.SemaphoreType.DMA((2 + z.n + count,)),
    ]
    return call(
        z,
        lambda z, *refs: attend_back_kernel(z, g, *refs),
        "attend_back_%d" % g,
        [SHAPE((rows, z.hd), BF16)] * z.n,
        [ANY] * 3 + ([ANY] if g else [VM] * len(small)),
        [ANY] * z.n,
        scratch,
        (qkv, prob, grad, *small),
        flops=count * z.s * z.s * z.hd * 8,
        nbytes=count * z.s * z.s * 8,
    )


def unpack_kernel(z, *refs):
    n, t = z.n, z.t
    ins, (proj, step, vecs, parts, sems) = refs[:n], refs[n:]
    me = lax.axis_index("context")
    mover = Copies(sems)
    rows = pl.ds(3 * z.sizes[0] * t, t + z.rp + 2 * z.v)
    wait_all([mover.start(ins[s].at[rows], parts.at[s]) for s in range(n)])
    total = jnp.zeros((t, z.ns), F32)
    steps = jnp.zeros((n * z.h, t), F32)
    for s in range(n):
        total = total + parts[s, :t].astype(F32)
        source = lax.rem(me + n - s, n)
        row, col = iota((n * z.h, z.r), 0), iota((n * z.h, z.r), 1)
        place = mat((row == source * z.h + col) & (col < z.h)).astype(BF16)
        steps = steps + dot(place, parts[s, t : t + z.r])
        vec = parts[s, t + z.rp :].astype(F32)
        vecs[source] = vec[: z.v] + vec[z.v :]
    proj[...] = total
    step[0] = steps


def unpack(z, parts):
    return call(
        z,
        unpack_kernel,
        "unpack",
        (SHAPE((z.t, z.ns), F32), SHAPE((1, z.n * z.h, z.t), F32), SHAPE((z.n, z.v, z.t), F32)),
        [ANY] * z.n,
        [VM] * 3,
        [pltpu.VMEM((z.n, z.t + z.rp + 2 * z.v, z.t), BF16), pltpu.SemaphoreType.DMA((z.n,))],
        parts,
    )


def choose_kernel(z, lengths, mine, theirs, vecs, b, c, weight, rate, loss):
    core = lax.axis_index("head")
    b[0] = jnp.where(core == 0, mine[...], theirs[...])
    c[0] = jnp.where(core == 0, theirs[...], mine[...])
    valid = lengths[0]
    for k in range(1, lengths.shape[0]):
        valid = valid + lengths[k]
    rates = jnp.zeros((1, z.t), F32)
    for j in range(z.n):
        weight[j] = vecs[j, : z.features]
        rates = rates + vecs[j, z.features : z.features + 1]
    losses = vecs[0, z.features + 1 : z.features + 2]
    loss[...] = jnp.sum(losses, axis=1, keepdims=True) / valid.astype(F32)
    rate[...] = rates[:, : z.n * z.h]


def choose(z, lengths, mine, theirs, vecs):
    return call(
        z,
        choose_kernel,
        "choose",
        (
            SHAPE((1, z.t, z.ns), F32),
            SHAPE((1, z.t, z.ns), F32),
            SHAPE((z.n, z.features, z.hd), F32),
            SHAPE((1, z.n * z.h), F32),
            SHAPE((1, 1), F32),
        ),
        [SM] + [VM] * 3,
        [VM] * 5,
        [],
        (lengths, mine, theirs, vecs),
    )


def finish_kernel(z, *refs):
    count = z.n * z.groups
    ins, out, refs = refs[:count], refs[count + 1], refs[count + 2 :]
    held, (turned, sems) = refs[: z.groups], refs[z.groups :]
    me = lax.axis_index("context")
    mover = Copies(sems)
    loads = []
    for g in range(z.groups):
        for s in range(z.n):
            rows = pl.ds(0, 3 * z.sizes[g] * z.t)
            loads.append(mover.start(ins[g * z.n + s].at[rows], held[g].at[lax.rem(me + z.n - s, z.n)]))
    wait_all(loads)
    stores = []
    for k in range(3):
        heads = [
            held[g][j, z.rows_of(g, k, a), :]
            for j in range(z.n)
            for g in range(z.groups)
            for a in range(z.sizes[g])
        ]
        turned[k] = jnp.swapaxes(jnp.stack(heads), 0, 1)
        stores.append(mover.start(turned.at[k], out.at[k, 0]))
    wait_all(stores)


def finish(z, parts, after):
    return call(
        z,
        finish_kernel,
        "finish",
        SHAPE((3, 1, z.t, z.hl, z.hd), BF16),
        [ANY] * (z.n * z.groups + 1),
        ANY,
        [
            *[pltpu.VMEM((z.n, 3 * k * z.t, z.hd), BF16) for k in z.sizes],
            pltpu.VMEM((3, z.t, z.hl, z.hd), BF16),
            pltpu.SemaphoreType.DMA((z.n * z.groups + 3,)),
        ],
        (*parts, after),
        nbytes=12 * z.t * z.hl * z.hd,
    )


def shift(x, axis, size, step):
    return lax.ppermute(x, axis, [(i, (i + step) % size) for i in range(size)])


def spread(parts, axis):
    return [parts[0]] + [shift(x, axis, len(parts), s) for s, x in enumerate(parts) if s]


def local(qkv, ssd_b, ssd_c, step_size, decay_rate, value_weight, returns, step_labels, lengths):
    n = lax.axis_size("context")
    z = Sizes(n, qkv.shape[2], qkv.shape[3], qkv.shape[4], step_size.shape[2], ssd_b.shape[2])

    sends = prep(z, qkv, ssd_b, ssd_c, jnp.swapaxes(step_size, 1, 2), step_labels, returns)
    arrived = [spread(sends[g * n : (g + 1) * n], "context") for g in range(z.groups)]
    mine, pay = pick(z, arrived[0])
    theirs = shift(mine, "head", 2, 1)
    attended = [attend(z, 0, arrived[0], [])]
    terms, bc = decay(z, mine, theirs, pay, decay_rate.reshape(1, -1), value_weight.reshape(z.hl, z.hd))
    for g in range(1, z.groups):
        attended.append(attend(z, g, arrived[g], [bc]))
    saved, value = ssd(z, [x[1] for x in attended], terms, bc)
    value = value + shift(value, "head", 2, 1)
    values = spread([value] * n, "context")
    grad, keep, give, steps, vec = ssd_back(z, lengths, values, terms, bc, saved)
    finals, small = [], [keep, shift(give, "head", 2, 1), steps, vec]
    for g in range(z.groups):
        back = attend_back(z, g, attended[g][2], attended[g][0], grad, small)
        finals.append(spread(back, "context"))
        small = back[:1]
    proj, step_grad, vecs = unpack(z, finals[0])
    other = shift(proj, "head", 2, 1)
    step = 1
    while step < lax.axis_size("rollout"):
        pairs = [(i, i ^ step) for i in range(lax.axis_size("rollout"))]
        vecs = vecs + lax.ppermute(vecs, "rollout", pairs)
        step *= 2
    b_grad, c_grad, weight_grad, rate_grad, loss = choose(z, lengths, proj, other, vecs)
    qkv_grad = finish(z, [x for part in finals for x in part], rate_grad)
    return (
        loss.reshape(()),
        qkv_grad,
        b_grad,
        c_grad,
        jnp.swapaxes(step_grad, 1, 2),
        rate_grad.reshape(-1),
        weight_grad.reshape(-1),
    )


def solution(mesh):
    in_specs = (
        P(None, "rollout", "context", "head", None),
        P("rollout", "context", None),
        P("rollout", "context", None),
        P("rollout", "context", "head"),
        P("head"),
        P("head"),
        P("rollout", None),
        P("rollout", "context"),
        P(),
    )
    out_specs = (
        P(),
        P(None, "rollout", "context", "head", None),
        P("rollout", "context", None),
        P("rollout", "context", None),
        P("rollout", "context", "head"),
        P("head"),
        P("head"),
    )
    return jax.shard_map(local, mesh=mesh, in_specs=in_specs, out_specs=out_specs, check_vma=False)
```

```python
import functools
import math

import jax
import jax.numpy as jnp
from jax import lax
from jax.experimental import pallas as pl
from jax.experimental.pallas import tpu as pltpu
from jax.sharding import PartitionSpec as P

MASK_FILL = -1e30
NORM_EPS = 1e-05
HIGHEST = lax.Precision.HIGHEST
LOG2E = 1.4426950408889634
GROUPS = (2, 2)
VMEM_MIB = 24
F32 = jnp.float32
BF16 = jnp.bfloat16

ANY = pl.BlockSpec(memory_space=pl.ANY)
SHAPE = jax.ShapeDtypeStruct
VM = pl.BlockSpec(memory_space=pltpu.VMEM)
SM = pl.BlockSpec(memory_space=pltpu.SMEM)


def dot(a, b, precision=None):
    return jnp.dot(a, b, preferred_element_type=F32, precision=precision)


def dot_nt(a, b, precision=None):
    return lax.dot_general(a, b, (((1,), (1,)), ((), ())), preferred_element_type=F32, precision=precision)


def dot_tn(a, b, precision=None):
    return lax.dot_general(a, b, (((0,), (0,)), ((), ())), preferred_element_type=F32, precision=precision)


def iota(shape, dim):
    return lax.broadcasted_iota(jnp.int32, shape, dim)


def mat(cond):
    return jnp.where(cond, 1.0, 0.0).astype(F32)


class Sizes:
    def __init__(self, n, tokens, heads_local, head_dim, ssd_local, state):
        self.n, self.t, self.hl, self.hd, self.ns = n, tokens, heads_local, head_dim, state
        self.s = n * tokens
        self.shifts = list(range(n))
        self.back_shifts = sorted(range(n), key=lambda s: (min(s, n - s), s))
        self.a = heads_local // n
        self.sizes = GROUPS if sum(GROUPS) == self.a else (self.a,)
        self.first = [sum(self.sizes[:g]) for g in range(len(self.sizes))]
        self.groups = len(self.sizes)
        self.h = ssd_local // n
        self.hl_ssd = ssd_local
        self.mp = heads_local * head_dim // ssd_local
        self.f = self.a * head_dim
        self.r = -(-(self.h + 1) // 8) * 8
        self.rp = -(-self.r // 16) * 16
        self.features = self.f // head_dim
        self.v = -(-(self.features + 2) // 8) * 8
        self.rows = min(256, self.s)
        self.blocks = self.s // self.rows
        self.static = self.blocks <= 2
        self.up, self.down, self.mid = 0, self.s, 2 * self.s
        self.pay = self.mid + 8 * n
        self.rate = self.pay + self.r * n
        self.weight = self.rate + self.r
        self.term_rows = self.weight + 8
        self.pay_rows = tokens + 2 * self.rp

    def sent_rows(self, g):
        return 3 * self.sizes[g] * self.t + (0 if g else self.pay_rows)

    def back_rows(self, g):
        rows = 3 * self.sizes[g] * self.t
        if g == 0:
            rows += self.t + self.rp + 2 * self.v
        return rows

    def rows_of(self, g, k, a):
        first = (k * self.sizes[g] + a) * self.t
        return slice(first, first + self.t)

    def lanes(self, g):
        return pl.ds(self.first[g] * self.hd, self.sizes[g] * self.hd)

    def each_block(self, body):
        if self.static:
            for i in range(self.blocks):
                body(i)
        else:

            @pl.loop(0, self.blocks)
            def _(i):
                body(i)

    def upto(self, i):
        return (i + 1) * self.rows if self.static else self.s

    def onward(self, i):
        return i * self.rows if self.static else 0

    def each_chunk(self, body):
        if self.static:
            for c in range(self.n):
                body(c)
        else:

            @pl.loop(0, self.n)
            def _(c):
                body(c)

    def chunk(self, c, base=0):
        return pl.ds(base + c * self.t if isinstance(c, int) else pl.multiple_of(base + c * self.t, self.t), self.t)

    def small(self, c, base, rows):
        return pl.ds(base + c * rows if isinstance(c, int) else pl.multiple_of(base + c * rows, 8), rows)

    def block(self, i):
        return pl.ds(i * self.rows if self.static else pl.multiple_of(i * self.rows, self.rows), self.rows)


def call(z, kernel, name, out_shape, in_specs, out_specs, scratch, args, flops=0, nbytes=0):
    return pl.pallas_call(
        functools.partial(kernel, z),
        name=name,
        out_shape=out_shape,
        in_specs=in_specs,
        out_specs=out_specs,
        scratch_shapes=scratch,
        compiler_params=pltpu.CompilerParams(vmem_limit_bytes=(VMEM_MIB if z.static else 56) * 1024 * 1024),
        cost_estimate=pl.CostEstimate(flops=flops, bytes_accessed=nbytes, transcendentals=0),
    )(*args)


def in_hbm(x):
    return pltpu.with_memory_space_constraint(x, pltpu.HBM)


class Copies:
    def __init__(self, sems):
        self.sems, self.count = sems, 0

    def start(self, source, target):
        one = pltpu.make_async_copy(source, target, self.sems.at[self.count])
        self.count += 1
        one.start()
        return one


def wait_all(copies):
    for one in copies:
        one.wait()


def split3(x):
    high = x.astype(BF16)
    rest = x - high.astype(F32)
    middle = rest.astype(BF16)
    return high, middle, (rest - middle.astype(F32)).astype(BF16)


def split2_dot(x, exact):
    high, low = split3(x)[:2]
    return dot(high, exact) + dot(low, exact)


def prep_kernel(z, qkv, b_in, c_in, step_in, labels_in, table_in, *refs):
    outs, refs = refs[: z.n * z.groups], refs[z.n * z.groups :]
    held, (parts, b, c, step, labels, table, sems) = refs[: z.groups], refs[z.groups :]
    me, core = lax.axis_index("context"), lax.axis_index("head")
    mover = Copies(sems)
    tiny = [
        mover.start(b_in.at[0], b),
        mover.start(c_in.at[0], c),
        mover.start(step_in.at[0], step),
        mover.start(labels_in, labels),
        mover.start(table_in, table),
    ]
    loads = [mover.start(qkv.at[k, 0], parts.at[k]) for k in range(3)]
    wait_all(tiny)
    onehot = mat(iota((table.shape[1], z.t), 0) == labels[...])
    target = dot(table[...], onehot, HIGHEST)
    mine = jnp.where(core == 0, b[...], c[...])
    end = 3 * z.sizes[0] * z.t
    for j in range(z.n):
        row = iota((z.r, z.hl_ssd), 0)
        pick = mat((iota((z.r, z.hl_ssd), 1) == j * z.h + row) & (row < z.h))
        pay = dot(pick, step[...], HIGHEST)
        pay = jnp.where(iota((z.r, z.t), 0) == z.h, target, pay)
        held[0][j, end : end + z.t] = mine
        held[0][j, end + z.t :] = jnp.zeros((2 * z.rp, z.t), BF16)
        for i, term in enumerate(split3(pay)[:2]):
            start = end + z.t + i * z.rp
            held[0][j, start : start + z.r] = term
    for k in range(3):
        loads[k].wait()
        turned = jnp.swapaxes(parts[k], 0, 1)
        for g in range(z.groups):
            for j in range(z.n):
                for a in range(z.sizes[g]):
                    held[g][j, z.rows_of(g, k, a), :] = turned[j * z.a + z.first[g] + a]
    for g in range(z.groups):
        for s in range(z.n):
            outs[g * z.n + s][...] = held[g][lax.rem(me + z.shifts[s], z.n)]


def prep(z, qkv, b, c, step, labels, table):
    args = [in_hbm(x) for x in (qkv, b, c, step, labels, table)]
    return call(
        z,
        prep_kernel,
        "prep",
        [SHAPE((z.sent_rows(g), z.hd), BF16) for g in range(z.groups) for _ in range(z.n)],
        [ANY] * 6,
        [VM] * (z.n * z.groups),
        [
            *[pltpu.VMEM((z.n, z.sent_rows(g), z.hd), BF16) for g in range(z.groups)],
            pltpu.VMEM((3, z.t, z.hl, z.hd), BF16),
            pltpu.VMEM((z.t, z.ns), BF16),
            pltpu.VMEM((z.t, z.ns), BF16),
            pltpu.VMEM(step.shape[1:], F32),
            pltpu.VMEM(labels.shape, jnp.int32),
            pltpu.VMEM(table.shape, F32),
            pltpu.SemaphoreType.DMA((8,)),
        ],
        args,
        nbytes=qkv.size * 4,
    )


def pick_kernel(z, *refs):
    ins, (mine, pay) = refs[: z.n], refs[z.n :]
    me = lax.axis_index("context")
    first = 3 * z.sizes[0] * z.t
    for s in range(z.n):
        source = lax.rem(me + z.n - z.shifts[s], z.n)
        mine[source] = ins[s][first : first + z.t]
        start = first + z.t
        terms = [ins[s][start + k * z.rp : start + k * z.rp + z.r].astype(F32) for k in range(2)]
        pay[source] = terms[0] + terms[1]


def pick(z, ins):
    return call(
        z,
        pick_kernel,
        "pick",
        (SHAPE((z.n, z.t, z.ns), BF16), SHAPE((z.n, z.r, z.t), F32)),
        [VM] * z.n,
        [VM] * 2,
        [],
        ins,
    )


def decay_kernel(z, mine, theirs, pay, rate, weight, terms, bc):
    n, t = z.n, z.t
    me, core = lax.axis_index("context"), lax.axis_index("head")
    heads = z.hl_ssd
    row, col = iota((z.r, heads), 0), iota((z.r, heads), 1)
    pick = mat((col == me * z.h + row) & (row < z.h))
    terms[z.rate : z.rate + z.r, :t] = dot_nt(pick, jnp.broadcast_to(rate[...], (t, heads)), HIGHEST)
    pick = mat(iota((8, z.hl), 1) == me * z.a + iota((8, z.hl), 0))
    terms[z.weight : z.weight + 8, : z.hd] = dot(pick, weight[...].astype(F32))
    rates = jnp.broadcast_to(rate[...], (8, heads))
    rates = dot(rates, mat(iota((heads, z.f), 0) == me * z.h + iota((heads, z.f), 1) // z.mp), HIGHEST)
    rates = rates[0:1]
    for c in range(n):
        bc[c, 0] = jnp.where(core == 0, mine[c], theirs[c])
        bc[c, 1] = jnp.where(core == 0, theirs[c], mine[c])
        terms[z.pay + c * z.r : z.pay + (c + 1) * z.r, :t] = pay[c]
    causal = iota((t, t), 0) >= iota((t, t), 1)
    lower = mat(causal)
    spread_heads = mat(iota((z.r, z.f), 0) == iota((z.r, z.f), 1) // z.mp)

    def chunk(c):
        steps = terms[z.small(c, z.pay, z.r), :t]
        cum = dot(dot_nt(lower, steps, HIGHEST), spread_heads, HIGHEST) * (-rates)
        half = 0.5 * cum[t - 1 : t]
        terms[z.chunk(c, z.up), :] = jnp.exp(cum - half)
        terms[z.chunk(c, z.down), :] = jnp.exp(half - cum)
        terms[z.small(c, z.mid, 8), :] = jnp.broadcast_to(jnp.exp(half), (8, z.f))
        inner = split3(jnp.where(causal, dot_nt(bc[c, 1], bc[c, 0]), 0.0))
        bc[c, 2] = inner[0]
        bc[c, 3] = inner[1]

    z.each_chunk(chunk)


def decay(z, mine, theirs, pay, rate, weight):
    return call(
        z,
        decay_kernel,
        "decay",
        (SHAPE((z.term_rows, z.f), F32), SHAPE((z.n, 4, z.t, z.ns), BF16)),
        [VM] * 5,
        [VM] * 2,
        [],
        (mine, theirs, pay, rate, weight),
        nbytes=8 * z.s * z.f,
    )


def attend_kernel(z, g, *refs):
    n, t, count = z.n, z.t, z.sizes[g]
    ins, refs = refs[:n], refs[n + (1 if g else 0) :]
    prob, attended, held = refs
    me = lax.axis_index("context")
    for s in range(n):
        held[lax.rem(me + n - z.shifts[s], n)] = ins[s][: 3 * count * t]

    def rows_upto(k, a, width):
        return held[: width // t, z.rows_of(g, k, a), :].reshape(width, z.hd)

    def rows_block(k, a, i):
        per = z.rows // t
        return held[pl.ds(i * per, per), z.rows_of(g, k, a), :].reshape(z.rows, z.hd)

    factor = LOG2E / math.sqrt(z.hd)
    for a in range(count):

        def attend(i):
            width = z.upto(i)
            rows = z.block(i)
            scores = dot_nt(rows_block(0, a, i), rows_upto(1, a, width))
            keep = iota((z.rows, width), 1) <= i * z.rows + iota((z.rows, width), 0)
            scores = jnp.where(keep, scores, MASK_FILL)
            weight = jnp.exp2((scores - jnp.max(scores, axis=1, keepdims=True)) * factor)
            weight = (weight * (1.0 / jnp.sum(weight, axis=1, keepdims=True))).astype(BF16)
            prob[a, rows, :width] = weight
            attended[rows, a * z.hd : (a + 1) * z.hd] = dot(weight, rows_upto(2, a, width)).astype(BF16)

        z.each_block(attend)


def attend(z, g, ins, after):
    count = z.sizes[g]
    outs = (
        SHAPE((count, z.s, z.s), BF16),
        SHAPE((z.s, count * z.hd), BF16),
        SHAPE((z.n, 3 * count * z.t, z.hd), BF16),
    )
    return call(
        z,
        lambda z, *refs: attend_kernel(z, g, *refs),
        "attend_%d" % g,
        outs,
        [VM] * z.n + [ANY] * len(after),
        [VM] * 3,
        [],
        (*ins, *after),
        flops=count * z.s * z.s * z.hd * 4,
        nbytes=count * z.s * z.s * 8,
    )


def ssd_kernel(z, *refs):
    n, t = z.n, z.t
    ins, refs = refs[: z.groups], refs[z.groups :]
    terms, bc, saved, value, state_low, adds = refs
    same_head = mat(iota((z.hd, z.hd), 0) // z.mp == iota((z.hd, z.hd), 1) // z.mp).astype(BF16)

    def enter(c):
        rows = z.chunk(c)
        attended = jnp.concatenate([one[rows, :] for one in ins], axis=1)
        high, low = split3(terms[z.chunk(c, z.down), :] * attended.astype(F32))[:2]
        saved[0, rows, :] = high
        saved[5, rows, :] = low
        adds[rows, :] = dot_tn(bc[c, 0], high) + dot_tn(bc[c, 0], low)

    z.each_chunk(enter)

    def step(c, state):
        m = terms[z.small(c, z.mid, 8), :][0:1]
        state = m * state
        high, low = split3(state)[:2]
        saved[3, z.chunk(c), :] = high
        state_low[z.chunk(c), :] = low
        return m * (state + adds[z.chunk(c), :])

    state = jnp.zeros((z.ns, z.f), F32)
    if z.static:
        for c in range(n):
            state = step(c, state)
    else:
        lax.fori_loop(0, n, step, state)

    def leave(c):
        rows = z.chunk(c)
        up = terms[z.chunk(c, z.up), :]
        left = [bc[c, k] for k in (2, 2, 3, 1, 1)]
        right = [saved[0, rows, :], saved[5, rows, :], saved[0, rows, :], saved[3, rows, :], state_low[rows, :]]
        y = up * dot(jnp.concatenate(left, axis=1), jnp.concatenate(right, axis=0))
        total = jnp.zeros((t, z.hd), F32)
        for a in range(z.a):
            part = slice(a * z.hd, (a + 1) * z.hd)
            ya = y[:, part]
            weight = terms[z.weight + a : z.weight + a + 1, : z.hd]
            scale = lax.rsqrt(split2_dot(ya * ya, same_head) * (1.0 / z.mp) + NORM_EPS)
            unit = ya * scale
            term = unit * weight
            total = total + term
            mean = split2_dot(term, same_head) * (1.0 / z.mp)
            saved[1, rows, part] = unit.astype(BF16)
            slope = split3(up[:, part] * scale * (weight - unit * mean))
            saved[2, rows, part] = slope[0]
            saved[4, rows, part] = slope[1]
        high, low = split3(total)[:2]
        ones = jnp.ones((8, z.hd), BF16)
        value[:, rows] = (dot_nt(ones, high) + dot_nt(ones, low))[0:1]

    z.each_chunk(leave)


def ssd(z, ins, terms, bc):
    return call(
        z,
        ssd_kernel,
        "ssd",
        (SHAPE((6, z.s, z.f), BF16), SHAPE((1, z.s), F32)),
        [VM] * (z.groups + 2),
        [VM] * 2,
        [
            pltpu.VMEM((z.s, z.f), BF16),
            pltpu.VMEM((z.n * z.ns, z.f), F32),
        ],
        (*ins, terms, bc),
        flops=z.s * z.f * z.ns * 20,
        nbytes=z.s * z.f * 32,
    )


def ssd_back_kernel(z, *refs):
    n, t = z.n, z.t
    lengths, values, refs = refs[0], refs[1 : n + 1], refs[n + 1 :]
    terms, bc, saved, refs = *refs[:3], refs[3:]
    grads, keep_out, give_out, step_out, vec, refs = *refs[:5], refs[5:]
    d, adds, dstates, through = refs
    me, core = lax.axis_index("context"), lax.axis_index("head")
    length = lengths[lax.axis_index("rollout")]
    value = values[0][...]
    for s in range(1, n):
        value = value + values[s][...]
    row_id, col_id = iota((t, t), 0), iota((t, t), 1)
    causal = row_id >= col_id
    strict = row_id > col_id
    after = mat(col_id >= row_id).astype(BF16)
    before = mat(strict).astype(BF16)
    per_head = mat(iota((z.f, t), 1) == iota((z.f, t), 0) // z.mp).astype(BF16)
    per_row = mat(iota((z.h * t, t), 1) == iota((z.h * t, t), 0) // t).astype(BF16)
    vec[...] = jnp.zeros_like(vec)

    def pays(c):
        return terms[z.small(c, z.pay, z.r), :t]

    def enter(c):
        rows = z.chunk(c)
        if z.static:
            value_row = value[:, c * t : (c + 1) * t]
        else:
            value_row = jnp.zeros((1, t), F32)
            for j in range(n):
                value_row = jnp.where(c == j, value[:, j * t : (j + 1) * t], value_row)
        valid = c * t + iota((1, t), 1) < length
        error = jnp.where(valid, value_row - pays(c)[z.h : z.h + 1], 0.0)
        vec[z.features + 1 : z.features + 2, :] += 0.5 * error * error
        column = jnp.transpose(jnp.broadcast_to(error, (t, t)))
        wide = jnp.concatenate([column] * (z.f // t), axis=1)
        dc = split3(wide * (saved[2, rows, :].astype(F32) + saved[4, rows, :].astype(F32)))[:2]
        d[0, rows, :] = dc[0]
        d[1, rows, :] = dc[1]
        adds[rows, :] = dot_tn(bc[c, 1], dc[0]) + dot_tn(bc[c, 1], dc[1])
        high, low = split3(error)[:2]
        pair = jnp.concatenate([high, low, jnp.zeros((6, t), BF16)], axis=0)
        weight_grad = dot(pair, saved[1, rows, :])
        weight_grad = weight_grad[0:1] + weight_grad[1:2]
        for a in range(z.features):
            vec[a : a + 1, :] += weight_grad[:, a * z.hd : (a + 1) * z.hd]

    z.each_chunk(enter)

    def carry(c, dstate):
        m = terms[z.small(c, z.mid, 8), :][0:1]
        rows = z.chunk(c)
        dstate = m * dstate
        dstates[rows, :] = dstate.astype(BF16)
        sums = jnp.sum(dstate * saved[3, rows, :].astype(F32), axis=0, keepdims=True)
        through[z.small(c, 0, 8), :] = jnp.broadcast_to(sums, (8, z.f))
        return m * (dstate + adds[rows, :])

    dstate = jnp.zeros((z.ns, z.f), F32)
    if z.static:
        for c in range(n - 1, -1, -1):
            dstate = carry(c, dstate)
    else:
        lax.fori_loop(0, n, lambda k, v: carry(n - 1 - k, v), dstate)

    def leave(c):
        rows = z.chunk(c)
        b, cp, inner = bc[c, 0], bc[c, 1], bc[c, 2]
        dc, dl = d[0, rows, :], d[1, rows, :]
        xc, xl, state_in, dstate_in = saved[0, rows, :], saved[5, rows, :], saved[3, rows, :], dstates[rows, :]
        local = dot_tn(inner, dc) + dot_tn(inner, dl)
        outer = dot(b, dstate_in)
        carried = dot(cp, state_in)
        grads[rows, :] = (terms[z.chunk(c, z.down), :] * (local + outer)).astype(BF16)
        grad_c = dot_nt(dc, state_in) + dot_nt(dl, state_in)
        grad_b = dot_nt(xc, dstate_in)
        down_sum = dot(((dc.astype(F32) + dl.astype(F32)) * carried).astype(BF16), per_head)
        up_sum = dot((xc.astype(F32) * outer).astype(BF16), per_head)
        inner_wide = inner.astype(F32)
        w_sum = jnp.zeros((t, t), F32)
        parts = []
        for k in range(z.h):
            first = k * z.mp // z.hd * z.hd
            mine = iota((t, z.hd), 1) // z.mp == k % (z.hd // z.mp)
            pair = slice(first, first + z.hd)
            x_head = jnp.where(mine, xc[:, pair], jnp.zeros((), BF16))
            x_low = jnp.where(mine, xl[:, pair], jnp.zeros((), BF16))
            left = jnp.concatenate([dc[:, pair], dl[:, pair], dc[:, pair]], axis=1)
            w = jnp.where(causal, dot_nt(left, jnp.concatenate([x_head, x_head, x_low], axis=1)), 0.0)
            w_sum += w
            parts.append((w * inner_wide).astype(BF16))
        straddle = dot(after, jnp.concatenate(parts, axis=1))
        straddle = jnp.concatenate(
            [jnp.where(strict, straddle[:, k * t : (k + 1) * t], 0.0).astype(BF16) for k in range(z.h)], axis=1
        )
        sums = [*split3(down_sum)[:2], *split3(up_sum)[:2]]
        gain = dot(
            jnp.concatenate([after, after, before, before], axis=1), jnp.concatenate(sums, axis=0)
        ) + dot(straddle, per_row)
        gain = gain + split2_dot(through[z.small(c, 0, 8), :], per_head)[0:1]
        w_low = w_sum.astype(BF16)
        grad_c += dot(w_low, b)
        grad_b += dot_tn(w_low, cp)
        keep_out[c] = jnp.where(core == 0, grad_b, grad_c)
        give_out[c] = jnp.where(core == 0, grad_c, grad_b).astype(BF16)
        gain_rows = jnp.transpose(gain)[: z.r]
        step_out[c] = -terms[z.rate : z.rate + z.r, :t] * gain_rows
        rate_part = jnp.sum(pays(c) * gain_rows, axis=1, keepdims=True)
        lane = (iota((z.r, t), 1) == me * z.h + iota((z.r, t), 0)) & (iota((z.r, t), 0) < z.h)
        vec[z.features : z.features + 1, :] -= jnp.sum(jnp.where(lane, rate_part, 0.0), axis=0, keepdims=True)

    z.each_chunk(leave)


def ssd_back(z, lengths, values, terms, bc, saved):
    outs = (
        SHAPE((z.s, z.f), BF16),
        SHAPE((z.n, z.t, z.ns), F32),
        SHAPE((z.n, z.t, z.ns), BF16),
        SHAPE((z.n, z.r, z.t), F32),
        SHAPE((z.v, z.t), F32),
    )
    scratch = [
        pltpu.VMEM((2, z.s, z.f), BF16),
        pltpu.VMEM((z.n * z.ns, z.f), F32),
        pltpu.VMEM((z.n * z.ns, z.f), BF16),
        pltpu.VMEM((z.n * 8, z.f), F32),
    ]
    return call(
        z,
        ssd_back_kernel,
        "ssd_back",
        outs,
        [SM] + [VM] * (z.n + 3),
        [VM] * 5,
        scratch,
        (lengths, *values, terms, bc, saved),
        flops=z.s * z.f * z.ns * 20,
        nbytes=z.s * z.f * 32,
    )


def attend_back_kernel(z, g, *refs):
    n, t, count = z.n, z.t, z.sizes[g]
    held, prob, grad_in, refs = *refs[:3], refs[3:]
    grad = grad_in.at[:, z.lanes(g)]
    if g == 0:
        keep, other, step, vec, refs = *refs[:4], refs[4:]
    else:
        refs = refs[1:]
    outs, refs = refs[:n], refs[n:]
    result, dscore = refs
    me = lax.axis_index("context")
    if g == 0:
        end = 3 * count * t
        for j in range(n):
            result[j, end : end + t] = (keep[j] + other[j].astype(F32)).astype(BF16)
            result[j, end + t :] = jnp.zeros((z.rp + 2 * z.v, t), BF16)
            result[j, end + t : end + t + z.r] = step[j].astype(BF16)
            result[j, end + t + z.rp :] = jnp.concatenate(split3(vec[...])[:2], axis=0)
    factor = 1.0 / math.sqrt(z.hd)
    per = z.rows // t

    def rows_span(k, a, first, last):
        return held[first // t : last // t, z.rows_of(g, k, a), :].reshape(last - first, z.hd)

    def store(k, a, i, x):
        result[pl.ds(i * per, per), z.rows_of(g, k, a), :] = x.astype(BF16).reshape(per, t, z.hd)

    for a in range(count):
        lanes = slice(a * z.hd, (a + 1) * z.hd)

        def by_query(i):
            width, rows = z.upto(i), z.block(i)
            p = prob[a, rows, :width].astype(F32)
            dp = dot_nt(grad[rows, lanes], rows_span(2, a, 0, width))
            product = p * dp
            ds = (product - p * jnp.sum(product, axis=1, keepdims=True)).astype(BF16)
            dscore[a, rows, :width] = ds
            store(0, a, i, dot(ds, rows_span(1, a, 0, width)) * factor)

        z.each_block(by_query)

        def by_key(j):
            start, cols = z.onward(j), z.block(j)
            store(1, a, j, dot_tn(dscore[a, start:, cols], rows_span(0, a, start, z.s)) * factor)
            store(2, a, j, dot_tn(prob[a, start:, cols], grad[start:, lanes]))

        z.each_block(by_key)
    for s in range(n):
        outs[s][...] = result[lax.rem(me + z.back_shifts[s], n)]


def attend_back(z, g, qkv, prob, grad, small):
    count = z.sizes[g]
    rows = z.back_rows(g)
    scratch = [
        pltpu.VMEM((z.n, rows, z.hd), BF16),
        pltpu.VMEM((count, z.s, z.s), BF16),
    ]
    return call(
        z,
        lambda z, *refs: attend_back_kernel(z, g, *refs),
        "attend_back_%d" % g,
        [SHAPE((rows, z.hd), BF16)] * z.n,
        [VM] * 3 + ([ANY] if g else [VM] * len(small)),
        [VM] * z.n,
        scratch,
        (qkv, prob, grad, *small),
        flops=count * z.s * z.s * z.hd * 8,
        nbytes=count * z.s * z.s * 8,
    )


def unpack_kernel(z, *refs):
    n, t = z.n, z.t
    ins, (proj, step, vecs) = refs[:n], refs[n:]
    me = lax.axis_index("context")
    parts = [ins[s][3 * z.sizes[0] * t :] for s in range(n)]
    total = jnp.zeros((t, z.ns), F32)
    steps = jnp.zeros((n * z.h, t), F32)
    for s in range(n):
        total = total + parts[s][:t].astype(F32)
        source = lax.rem(me + n - z.back_shifts[s], n)
        row, col = iota((n * z.h, z.r), 0), iota((n * z.h, z.r), 1)
        place = mat((row == source * z.h + col) & (col < z.h)).astype(BF16)
        steps = steps + dot(place, parts[s][t : t + z.r])
        vec = parts[s][t + z.rp :].astype(F32)
        vecs[source] = vec[: z.v] + vec[z.v :]
    proj[...] = total
    step[0] = steps


def unpack(z, parts):
    return call(
        z,
        unpack_kernel,
        "unpack",
        (SHAPE((z.t, z.ns), F32), SHAPE((1, z.n * z.h, z.t), F32), SHAPE((z.n, z.v, z.t), F32)),
        [VM] * z.n,
        [VM] * 3,
        [],
        parts,
    )


def choose_kernel(z, lengths, mine, theirs, vecs, b, c, weight, rate, loss):
    core = lax.axis_index("head")
    b[0] = jnp.where(core == 0, mine[...], theirs[...])
    c[0] = jnp.where(core == 0, theirs[...], mine[...])
    valid = lengths[0]
    for k in range(1, lengths.shape[0]):
        valid = valid + lengths[k]
    rates = jnp.zeros((1, z.t), F32)
    for j in range(z.n):
        weight[j] = vecs[j, : z.features]
        rates = rates + vecs[j, z.features : z.features + 1]
    losses = vecs[0, z.features + 1 : z.features + 2]
    loss[...] = jnp.sum(losses, axis=1, keepdims=True) / valid.astype(F32)
    rate[...] = rates[:, : z.n * z.h]


def choose(z, lengths, mine, theirs, vecs):
    return call(
        z,
        choose_kernel,
        "choose",
        (
            SHAPE((1, z.t, z.ns), F32),
            SHAPE((1, z.t, z.ns), F32),
            SHAPE((z.n, z.features, z.hd), F32),
            SHAPE((1, z.n * z.h), F32),
            SHAPE((1, 1), F32),
        ),
        [SM] + [VM] * 3,
        [VM] * 5,
        [],
        (lengths, mine, theirs, vecs),
    )


def finish_kernel(z, *refs):
    count = z.n * z.groups
    ins, out, refs = refs[:count], refs[count], refs[count + 1 :]
    held, (turned, sems) = refs[: z.groups], refs[z.groups :]
    me = lax.axis_index("context")
    mover = Copies(sems)
    for g in range(z.groups):
        for s in range(z.n):
            held[g][lax.rem(me + z.n - z.back_shifts[s], z.n)] = ins[g * z.n + s][: 3 * z.sizes[g] * z.t]
    stores = []
    for k in range(3):
        heads = [
            held[g][j, z.rows_of(g, k, a), :]
            for j in range(z.n)
            for g in range(z.groups)
            for a in range(z.sizes[g])
        ]
        turned[k] = jnp.swapaxes(jnp.stack(heads), 0, 1)
        stores.append(mover.start(turned.at[k], out.at[k, 0]))
    wait_all(stores)


def finish(z, parts):
    return call(
        z,
        finish_kernel,
        "finish",
        SHAPE((3, 1, z.t, z.hl, z.hd), BF16),
        [VM] * (z.n * z.groups),
        ANY,
        [
            *[pltpu.VMEM((z.n, 3 * k * z.t, z.hd), BF16) for k in z.sizes],
            pltpu.VMEM((3, z.t, z.hl, z.hd), BF16),
            pltpu.SemaphoreType.DMA((3,)),
        ],
        parts,
        nbytes=12 * z.t * z.hl * z.hd,
    )


def shift(x, axis, size, step):
    return lax.ppermute(x, axis, [(i, (i + step) % size) for i in range(size)])


def spread(parts, axis, shifts):
    return [parts[0]] + [shift(x, axis, len(parts), s) for x, s in zip(parts[1:], shifts[1:])]


def partners(x, axis, step):
    return lax.ppermute(x, axis, [(i, i ^ step) for i in range(lax.axis_size(axis))])


def local(qkv, ssd_b, ssd_c, step_size, decay_rate, value_weight, returns, step_labels, lengths):
    n = lax.axis_size("context")
    z = Sizes(n, qkv.shape[2], qkv.shape[3], qkv.shape[4], step_size.shape[2], ssd_b.shape[2])

    sends = prep(z, qkv, ssd_b, ssd_c, jnp.swapaxes(step_size, 1, 2), step_labels, returns)
    arrived = [spread(sends[g * n : (g + 1) * n], "context", z.shifts) for g in range(z.groups)]
    mine, pay = pick(z, arrived[0])
    theirs = shift(mine, "head", 2, 1)
    attended = [attend(z, 0, arrived[0], [])]
    terms, bc = decay(z, mine, theirs, pay, decay_rate.reshape(1, -1), value_weight.reshape(z.hl, z.hd))
    for g in range(1, z.groups):
        attended.append(attend(z, g, arrived[g], [bc]))
    saved, value = ssd(z, [x[1] for x in attended], terms, bc)
    value = value + shift(value, "head", 2, 1)
    values = [value] + [partners(value, "context", s) for s in range(1, n)]
    grad, keep, give, steps, vec = ssd_back(z, lengths, values, terms, bc, saved)
    finals, small = [], [keep, shift(give, "head", 2, 1), steps, vec]
    for g in range(z.groups):
        back = attend_back(z, g, attended[g][2], attended[g][0], grad, small)
        finals.append(spread(back, "context", z.back_shifts))
        small = back[:1]
    proj, step_grad, vecs = unpack(z, finals[0])
    other = shift(proj, "head", 2, 1)
    step = 1
    while step < lax.axis_size("rollout"):
        vecs = vecs + partners(vecs, "rollout", step)
        step *= 2
    b_grad, c_grad, weight_grad, rate_grad, loss = choose(z, lengths, proj, other, vecs)
    qkv_grad = finish(z, [x for part in finals for x in part])
    return (
        loss.reshape(()),
        qkv_grad,
        b_grad,
        c_grad,
        jnp.swapaxes(step_grad, 1, 2),
        rate_grad.reshape(-1),
        weight_grad.reshape(-1),
    )


def solution(mesh):
    in_specs = (
        P(None, "rollout", "context", "head", None),
        P("rollout", "context", None),
        P("rollout", "context", None),
        P("rollout", "context", "head"),
        P("head"),
        P("head"),
        P("rollout", None),
        P("rollout", "context"),
        P(),
    )
    out_specs = (
        P(),
        P(None, "rollout", "context", "head", None),
        P("rollout", "context", None),
        P("rollout", "context", None),
        P("rollout", "context", "head"),
        P("head"),
        P("head"),
    )
    return jax.shard_map(local, mesh=mesh, in_specs=in_specs, out_specs=out_specs, check_vma=False)
```

```python
import functools
import math

import jax
import jax.numpy as jnp
from jax import lax
from jax.experimental import pallas as pl
from jax.experimental.pallas import tpu as pltpu
from jax.sharding import PartitionSpec as P

MASK_FILL = -1e30
NORM_EPS = 1e-05
HIGHEST = lax.Precision.HIGHEST
LOG2E = 1.4426950408889634
GROUPS = (2, 2)
VMEM_MIB = 24
F32 = jnp.float32
BF16 = jnp.bfloat16

ANY = pl.BlockSpec(memory_space=pl.ANY)
SHAPE = jax.ShapeDtypeStruct
VM = pl.BlockSpec(memory_space=pltpu.VMEM)
SM = pl.BlockSpec(memory_space=pltpu.SMEM)


def dot(a, b, precision=None):
    return jnp.dot(a, b, preferred_element_type=F32, precision=precision)


def dot_nt(a, b, precision=None):
    return lax.dot_general(a, b, (((1,), (1,)), ((), ())), preferred_element_type=F32, precision=precision)


def dot_tn(a, b, precision=None):
    return lax.dot_general(a, b, (((0,), (0,)), ((), ())), preferred_element_type=F32, precision=precision)


def iota(shape, dim):
    return lax.broadcasted_iota(jnp.int32, shape, dim)


def mat(cond):
    return jnp.where(cond, 1.0, 0.0).astype(F32)


class Sizes:
    def __init__(self, n, tokens, heads_local, head_dim, ssd_local, state):
        self.n, self.t, self.hl, self.hd, self.ns = n, tokens, heads_local, head_dim, state
        self.s = n * tokens
        self.a = heads_local // n
        self.sizes = GROUPS if sum(GROUPS) == self.a else (self.a,)
        self.first = [sum(self.sizes[:g]) for g in range(len(self.sizes))]
        self.groups = len(self.sizes)
        self.shifts = [list(range(n)) for _ in range(self.groups)]
        self.back_shifts = self.shifts
        self.h = ssd_local // n
        self.hl_ssd = ssd_local
        self.mp = heads_local * head_dim // ssd_local
        self.f = self.a * head_dim
        self.r = -(-(self.h + 1) // 8) * 8
        self.rp = -(-self.r // 16) * 16
        self.features = self.f // head_dim
        self.v = -(-(self.features + 2) // 8) * 8
        self.rows = min(256, self.s)
        self.blocks = self.s // self.rows
        self.static = self.blocks <= 2
        self.up, self.down, self.mid = 0, self.s, 2 * self.s
        self.pay = self.mid + 8 * n
        self.rate = self.pay + self.r * n
        self.weight = self.rate + self.r
        self.term_rows = self.weight + 8
        self.pay_rows = tokens + 2 * self.rp

    def sent_rows(self, g):
        return 3 * self.sizes[g] * self.t + (0 if g else self.pay_rows)

    def back_rows(self, g):
        rows = 3 * self.sizes[g] * self.t
        if g == 0:
            rows += self.t + self.rp + 2 * self.v
        return rows

    def rows_of(self, g, k, a):
        first = (k * self.sizes[g] + a) * self.t
        return slice(first, first + self.t)

    def lanes(self, g):
        return pl.ds(self.first[g] * self.hd, self.sizes[g] * self.hd)

    def each_block(self, body):
        if self.static:
            for i in range(self.blocks):
                body(i)
        else:

            @pl.loop(0, self.blocks)
            def _(i):
                body(i)

    def upto(self, i):
        return (i + 1) * self.rows if self.static else self.s

    def onward(self, i):
        return i * self.rows if self.static else 0

    def each_chunk(self, body):
        if self.static:
            for c in range(self.n):
                body(c)
        else:

            @pl.loop(0, self.n)
            def _(c):
                body(c)

    def chunk(self, c, base=0):
        return pl.ds(base + c * self.t if isinstance(c, int) else pl.multiple_of(base + c * self.t, self.t), self.t)

    def small(self, c, base, rows):
        return pl.ds(base + c * rows if isinstance(c, int) else pl.multiple_of(base + c * rows, 8), rows)

    def block(self, i):
        return pl.ds(i * self.rows if self.static else pl.multiple_of(i * self.rows, self.rows), self.rows)


def call(z, kernel, name, out_shape, in_specs, out_specs, scratch, args, flops=0, nbytes=0):
    return pl.pallas_call(
        functools.partial(kernel, z),
        name=name,
        out_shape=out_shape,
        in_specs=in_specs,
        out_specs=out_specs,
        scratch_shapes=scratch,
        compiler_params=pltpu.CompilerParams(vmem_limit_bytes=(VMEM_MIB if z.static else 56) * 1024 * 1024),
        cost_estimate=pl.CostEstimate(flops=flops, bytes_accessed=nbytes, transcendentals=0),
    )(*args)


def in_hbm(x):
    return pltpu.with_memory_space_constraint(x, pltpu.HBM)


class Copies:
    def __init__(self, sems):
        self.sems, self.count = sems, 0

    def start(self, source, target):
        one = pltpu.make_async_copy(source, target, self.sems.at[self.count])
        self.count += 1
        one.start()
        return one


def wait_all(copies):
    for one in copies:
        one.wait()


def split3(x):
    high = x.astype(BF16)
    rest = x - high.astype(F32)
    middle = rest.astype(BF16)
    return high, middle, (rest - middle.astype(F32)).astype(BF16)


def split2_dot(x, exact):
    high, low = split3(x)[:2]
    return dot(high, exact) + dot(low, exact)


def prep_kernel(z, qkv, b_in, c_in, step_in, labels_in, table_in, *refs):
    outs, refs = refs[: z.n * z.groups], refs[z.n * z.groups :]
    held, (parts, b, c, step, labels, table, sems) = refs[: z.groups], refs[z.groups :]
    me, core = lax.axis_index("context"), lax.axis_index("head")
    mover = Copies(sems)
    tiny = [
        mover.start(b_in.at[0], b),
        mover.start(c_in.at[0], c),
        mover.start(step_in.at[0], step),
        mover.start(labels_in, labels),
        mover.start(table_in, table),
    ]
    loads = [mover.start(qkv.at[k, 0], parts.at[k]) for k in range(3)]
    wait_all(tiny)
    onehot = mat(iota((table.shape[1], z.t), 0) == labels[...])
    target = dot(table[...], onehot, HIGHEST)
    mine = jnp.where(core == 0, b[...], c[...])
    end = 3 * z.sizes[0] * z.t
    for j in range(z.n):
        row = iota((z.r, z.hl_ssd), 0)
        pick = mat((iota((z.r, z.hl_ssd), 1) == j * z.h + row) & (row < z.h))
        pay = dot(pick, step[...], HIGHEST)
        pay = jnp.where(iota((z.r, z.t), 0) == z.h, target, pay)
        held[0][j, end : end + z.t] = mine
        held[0][j, end + z.t :] = jnp.zeros((2 * z.rp, z.t), BF16)
        for i, term in enumerate(split3(pay)[:2]):
            start = end + z.t + i * z.rp
            held[0][j, start : start + z.r] = term
    for k in range(3):
        loads[k].wait()
        turned = jnp.swapaxes(parts[k], 0, 1)
        for g in range(z.groups):
            for j in range(z.n):
                for a in range(z.sizes[g]):
                    held[g][j, z.rows_of(g, k, a), :] = turned[j * z.a + z.first[g] + a]
    for g in range(z.groups):
        for s in range(z.n):
            outs[g * z.n + s][...] = held[g][lax.rem(me + z.shifts[g][s], z.n)]


def prep(z, qkv, b, c, step, labels, table):
    args = [in_hbm(x) for x in (qkv, b, c, step, labels, table)]
    return call(
        z,
        prep_kernel,
        "prep",
        [SHAPE((z.sent_rows(g), z.hd), BF16) for g in range(z.groups) for _ in range(z.n)],
        [ANY] * 6,
        [VM] * (z.n * z.groups),
        [
            *[pltpu.VMEM((z.n, z.sent_rows(g), z.hd), BF16) for g in range(z.groups)],
            pltpu.VMEM((3, z.t, z.hl, z.hd), BF16),
            pltpu.VMEM((z.t, z.ns), BF16),
            pltpu.VMEM((z.t, z.ns), BF16),
            pltpu.VMEM(step.shape[1:], F32),
            pltpu.VMEM(labels.shape, jnp.int32),
            pltpu.VMEM(table.shape, F32),
            pltpu.SemaphoreType.DMA((8,)),
        ],
        args,
        nbytes=qkv.size * 4,
    )


def pick_kernel(z, *refs):
    ins, (mine, pay) = refs[: z.n], refs[z.n :]
    me = lax.axis_index("context")
    first = 3 * z.sizes[0] * z.t
    for s in range(z.n):
        source = lax.rem(me + z.n - z.shifts[0][s], z.n)
        mine[source] = ins[s][first : first + z.t]
        start = first + z.t
        terms = [ins[s][start + k * z.rp : start + k * z.rp + z.r].astype(F32) for k in range(2)]
        pay[source] = terms[0] + terms[1]


def pick(z, ins):
    return call(
        z,
        pick_kernel,
        "pick",
        (SHAPE((z.n, z.t, z.ns), BF16), SHAPE((z.n, z.r, z.t), F32)),
        [VM] * z.n,
        [VM] * 2,
        [],
        ins,
    )


def decay_kernel(z, mine, theirs, pay, rate, weight, terms, bc):
    n, t = z.n, z.t
    me, core = lax.axis_index("context"), lax.axis_index("head")
    heads = z.hl_ssd
    row, col = iota((z.r, heads), 0), iota((z.r, heads), 1)
    pick = mat((col == me * z.h + row) & (row < z.h))
    terms[z.rate : z.rate + z.r, :t] = dot_nt(pick, jnp.broadcast_to(rate[...], (t, heads)), HIGHEST)
    pick = mat(iota((8, z.hl), 1) == me * z.a + iota((8, z.hl), 0))
    terms[z.weight : z.weight + 8, : z.hd] = dot(pick, weight[...].astype(F32))
    rates = jnp.broadcast_to(rate[...], (8, heads))
    rates = dot(rates, mat(iota((heads, z.f), 0) == me * z.h + iota((heads, z.f), 1) // z.mp), HIGHEST)
    rates = rates[0:1]
    for c in range(n):
        bc[c, 0] = jnp.where(core == 0, mine[c], theirs[c])
        bc[c, 1] = jnp.where(core == 0, theirs[c], mine[c])
        terms[z.pay + c * z.r : z.pay + (c + 1) * z.r, :t] = pay[c]
    causal = iota((t, t), 0) >= iota((t, t), 1)
    lower = mat(causal)
    spread_heads = mat(iota((z.r, z.f), 0) == iota((z.r, z.f), 1) // z.mp)

    def chunk(c):
        steps = terms[z.small(c, z.pay, z.r), :t]
        cum = dot(dot_nt(lower, steps, HIGHEST), spread_heads, HIGHEST) * (-rates)
        half = 0.5 * cum[t - 1 : t]
        terms[z.chunk(c, z.up), :] = jnp.exp(cum - half)
        terms[z.chunk(c, z.down), :] = jnp.exp(half - cum)
        terms[z.small(c, z.mid, 8), :] = jnp.broadcast_to(jnp.exp(half), (8, z.f))
        inner = split3(jnp.where(causal, dot_nt(bc[c, 1], bc[c, 0]), 0.0))
        bc[c, 2] = inner[0]
        bc[c, 3] = inner[1]

    z.each_chunk(chunk)


def decay(z, mine, theirs, pay, rate, weight):
    return call(
        z,
        decay_kernel,
        "decay",
        (SHAPE((z.term_rows, z.f), F32), SHAPE((z.n, 4, z.t, z.ns), BF16)),
        [VM] * 5,
        [VM] * 2,
        [],
        (mine, theirs, pay, rate, weight),
        nbytes=8 * z.s * z.f,
    )


def attend_kernel(z, g, *refs):
    n, t, count = z.n, z.t, z.sizes[g]
    ins, refs = refs[:n], refs[n + (1 if g else 0) :]
    prob, attended, held = refs
    me = lax.axis_index("context")
    for s in range(n):
        held[lax.rem(me + n - z.shifts[g][s], n)] = ins[s][: 3 * count * t]

    def rows_upto(k, a, width):
        return held[: width // t, z.rows_of(g, k, a), :].reshape(width, z.hd)

    def rows_block(k, a, i):
        per = z.rows // t
        return held[pl.ds(i * per, per), z.rows_of(g, k, a), :].reshape(z.rows, z.hd)

    factor = LOG2E / math.sqrt(z.hd)
    for a in range(count):

        def attend(i):
            width = z.upto(i)
            rows = z.block(i)
            scores = dot_nt(rows_block(0, a, i), rows_upto(1, a, width))
            keep = iota((z.rows, width), 1) <= i * z.rows + iota((z.rows, width), 0)
            scores = jnp.where(keep, scores, MASK_FILL)
            weight = jnp.exp2((scores - jnp.max(scores, axis=1, keepdims=True)) * factor)
            weight = (weight * (1.0 / jnp.sum(weight, axis=1, keepdims=True))).astype(BF16)
            prob[a, rows, :width] = weight
            attended[rows, a * z.hd : (a + 1) * z.hd] = dot(weight, rows_upto(2, a, width)).astype(BF16)

        z.each_block(attend)


def attend(z, g, ins, after):
    count = z.sizes[g]
    outs = (
        SHAPE((count, z.s, z.s), BF16),
        SHAPE((z.s, count * z.hd), BF16),
        SHAPE((z.n, 3 * count * z.t, z.hd), BF16),
    )
    return call(
        z,
        lambda z, *refs: attend_kernel(z, g, *refs),
        "attend_%d" % g,
        outs,
        [VM] * z.n + [ANY] * len(after),
        [VM] * 3,
        [],
        (*ins, *after),
        flops=count * z.s * z.s * z.hd * 4,
        nbytes=count * z.s * z.s * 8,
    )


def ssd_kernel(z, *refs):
    n, t = z.n, z.t
    ins, refs = refs[: z.groups], refs[z.groups :]
    terms, bc, saved, value, state_low, adds = refs
    same_head = mat(iota((z.hd, z.hd), 0) // z.mp == iota((z.hd, z.hd), 1) // z.mp).astype(BF16)

    def enter(c):
        rows = z.chunk(c)
        attended = jnp.concatenate([one[rows, :] for one in ins], axis=1)
        high, low = split3(terms[z.chunk(c, z.down), :] * attended.astype(F32))[:2]
        saved[0, rows, :] = high
        saved[5, rows, :] = low
        adds[rows, :] = dot_tn(bc[c, 0], high) + dot_tn(bc[c, 0], low)

    z.each_chunk(enter)

    def step(c, state):
        m = terms[z.small(c, z.mid, 8), :][0:1]
        state = m * state
        high, low = split3(state)[:2]
        saved[3, z.chunk(c), :] = high
        state_low[z.chunk(c), :] = low
        return m * (state + adds[z.chunk(c), :])

    state = jnp.zeros((z.ns, z.f), F32)
    if z.static:
        for c in range(n):
            state = step(c, state)
    else:
        lax.fori_loop(0, n, step, state)

    def leave(c):
        rows = z.chunk(c)
        up = terms[z.chunk(c, z.up), :]
        left = [bc[c, k] for k in (2, 2, 3, 1, 1)]
        right = [saved[0, rows, :], saved[5, rows, :], saved[0, rows, :], saved[3, rows, :], state_low[rows, :]]
        y = up * dot(jnp.concatenate(left, axis=1), jnp.concatenate(right, axis=0))
        total = jnp.zeros((t, z.hd), F32)
        for a in range(z.a):
            part = slice(a * z.hd, (a + 1) * z.hd)
            ya = y[:, part]
            weight = terms[z.weight + a : z.weight + a + 1, : z.hd]
            scale = lax.rsqrt(split2_dot(ya * ya, same_head) * (1.0 / z.mp) + NORM_EPS)
            unit = ya * scale
            term = unit * weight
            total = total + term
            mean = split2_dot(term, same_head) * (1.0 / z.mp)
            saved[1, rows, part] = unit.astype(BF16)
            slope = split3(up[:, part] * scale * (weight - unit * mean))
            saved[2, rows, part] = slope[0]
            saved[4, rows, part] = slope[1]
        high, low = split3(total)[:2]
        ones = jnp.ones((8, z.hd), BF16)
        value[:, rows] = (dot_nt(ones, high) + dot_nt(ones, low))[0:1]

    z.each_chunk(leave)


def ssd(z, ins, terms, bc):
    return call(
        z,
        ssd_kernel,
        "ssd",
        (SHAPE((6, z.s, z.f), BF16), SHAPE((1, z.s), F32)),
        [VM] * (z.groups + 2),
        [VM] * 2,
        [
            pltpu.VMEM((z.s, z.f), BF16),
            pltpu.VMEM((z.n * z.ns, z.f), F32),
        ],
        (*ins, terms, bc),
        flops=z.s * z.f * z.ns * 20,
        nbytes=z.s * z.f * 32,
    )


def ssd_pre_kernel(z, bc, saved, w_sums, straddled, down_sums):
    t = z.t
    causal = iota((t, t), 0) >= iota((t, t), 1)
    per_head = mat(iota((z.f, t), 1) == iota((z.f, t), 0) // z.mp).astype(BF16)

    def chunk(c):
        rows = z.chunk(c)
        sc, sl, xc, xl = saved[2, rows, :], saved[4, rows, :], saved[0, rows, :], saved[5, rows, :]
        carried = dot(bc[c, 1], saved[3, rows, :])
        down_sums[rows, :] = dot(((sc.astype(F32) + sl.astype(F32)) * carried).astype(BF16), per_head)
        inner = bc[c, 2].astype(F32)
        w_sum = jnp.zeros((t, t), F32)
        for k in range(z.h):
            first = k * z.mp // z.hd * z.hd
            mine = iota((t, z.hd), 1) // z.mp == k % (z.hd // z.mp)
            pair = slice(first, first + z.hd)
            x_head = jnp.where(mine, xc[:, pair], jnp.zeros((), BF16))
            x_low = jnp.where(mine, xl[:, pair], jnp.zeros((), BF16))
            left = jnp.concatenate([sc[:, pair], sl[:, pair], sc[:, pair]], axis=1)
            w = jnp.where(causal, dot_nt(left, jnp.concatenate([x_head, x_head, x_low], axis=1)), 0.0)
            w_sum += w
            straddled[rows, k * t : (k + 1) * t] = (w * inner).astype(BF16)
        w_sums[rows, :] = w_sum

    z.each_chunk(chunk)


def ssd_pre(z, bc, saved):
    return call(
        z,
        ssd_pre_kernel,
        "ssd_pre",
        (SHAPE((z.s, z.t), F32), SHAPE((z.s, z.h * z.t), BF16), SHAPE((z.s, z.t), F32)),
        [VM] * 2,
        [VM] * 3,
        [],
        (bc, saved),
        flops=z.s * z.f * z.ns * 20,
        nbytes=z.s * z.f * 8,
    )


def ssd_back_kernel(z, *refs):
    n, t = z.n, z.t
    lengths, values, refs = refs[0], refs[1 : n + 1], refs[n + 1 :]
    terms, bc, saved, w_sums, straddled, down_sums, refs = *refs[:6], refs[6:]
    grads, keep_out, give_out, step_out, vec, refs = *refs[:5], refs[5:]
    d, adds, dstates, through, errors = refs
    me, core = lax.axis_index("context"), lax.axis_index("head")
    length = lengths[lax.axis_index("rollout")]
    value = values[0][...]
    for s in range(1, n):
        value = value + values[s][...]
    row_id, col_id = iota((t, t), 0), iota((t, t), 1)
    strict = row_id > col_id
    after = mat(col_id >= row_id).astype(BF16)
    before = mat(strict).astype(BF16)
    per_head = mat(iota((z.f, t), 1) == iota((z.f, t), 0) // z.mp).astype(BF16)
    per_row = mat(iota((z.h * t, t), 1) == iota((z.h * t, t), 0) // t).astype(BF16)
    vec[...] = jnp.zeros_like(vec)

    def pays(c):
        return terms[z.small(c, z.pay, z.r), :t]

    def enter(c):
        rows = z.chunk(c)
        if z.static:
            value_row = value[:, c * t : (c + 1) * t]
        else:
            value_row = jnp.zeros((1, t), F32)
            for j in range(n):
                value_row = jnp.where(c == j, value[:, j * t : (j + 1) * t], value_row)
        valid = c * t + iota((1, t), 1) < length
        error = jnp.where(valid, value_row - pays(c)[z.h : z.h + 1], 0.0)
        vec[z.features + 1 : z.features + 2, :] += 0.5 * error * error
        column = jnp.transpose(jnp.broadcast_to(error, (t, t)))
        errors[0, rows, :] = jnp.broadcast_to(error, (t, t))
        errors[1, rows, :] = column
        wide = jnp.concatenate([column] * (z.f // t), axis=1)
        dc = split3(wide * (saved[2, rows, :].astype(F32) + saved[4, rows, :].astype(F32)))[:2]
        d[0, rows, :] = dc[0]
        d[1, rows, :] = dc[1]
        adds[rows, :] = dot_tn(bc[c, 1], dc[0]) + dot_tn(bc[c, 1], dc[1])
        high, low = split3(error)[:2]
        pair = jnp.concatenate([high, low, jnp.zeros((6, t), BF16)], axis=0)
        weight_grad = dot(pair, saved[1, rows, :])
        weight_grad = weight_grad[0:1] + weight_grad[1:2]
        for a in range(z.features):
            vec[a : a + 1, :] += weight_grad[:, a * z.hd : (a + 1) * z.hd]

    z.each_chunk(enter)

    def carry(c, dstate):
        m = terms[z.small(c, z.mid, 8), :][0:1]
        rows = z.chunk(c)
        dstate = m * dstate
        dstates[rows, :] = dstate.astype(BF16)
        sums = jnp.sum(dstate * saved[3, rows, :].astype(F32), axis=0, keepdims=True)
        through[z.small(c, 0, 8), :] = jnp.broadcast_to(sums, (8, z.f))
        return m * (dstate + adds[rows, :])

    dstate = jnp.zeros((z.ns, z.f), F32)
    if z.static:
        for c in range(n - 1, -1, -1):
            dstate = carry(c, dstate)
    else:
        lax.fori_loop(0, n, lambda k, v: carry(n - 1 - k, v), dstate)

    def leave(c):
        rows = z.chunk(c)
        b, cp, inner = bc[c, 0], bc[c, 1], bc[c, 2]
        dc, dl = d[0, rows, :], d[1, rows, :]
        xc, state_in, dstate_in = saved[0, rows, :], saved[3, rows, :], dstates[rows, :]
        local = dot_tn(inner, dc) + dot_tn(inner, dl)
        outer = dot(b, dstate_in)
        grads[rows, :] = (terms[z.chunk(c, z.down), :] * (local + outer)).astype(BF16)
        grad_c = dot_nt(dc, state_in) + dot_nt(dl, state_in)
        grad_b = dot_nt(xc, dstate_in)
        down_sum = errors[1, rows, :] * down_sums[rows, :]
        up_sum = dot((xc.astype(F32) * outer).astype(BF16), per_head)
        straddle = dot(jnp.where(col_id >= row_id, errors[0, rows, :], 0.0).astype(BF16), straddled[rows, :])
        straddle = jnp.concatenate(
            [jnp.where(strict, straddle[:, k * t : (k + 1) * t], 0.0).astype(BF16) for k in range(z.h)], axis=1
        )
        sums = [*split3(down_sum)[:2], *split3(up_sum)[:2]]
        gain = dot(
            jnp.concatenate([after, after, before, before], axis=1), jnp.concatenate(sums, axis=0)
        ) + dot(straddle, per_row)
        gain = gain + split2_dot(through[z.small(c, 0, 8), :], per_head)[0:1]
        w_low = (errors[1, rows, :] * w_sums[rows, :]).astype(BF16)
        grad_c += dot(w_low, b)
        grad_b += dot_tn(w_low, cp)
        keep_out[c] = jnp.where(core == 0, grad_b, grad_c)
        give_out[c] = jnp.where(core == 0, grad_c, grad_b).astype(BF16)
        gain_rows = jnp.transpose(gain)[: z.r]
        step_out[c] = -terms[z.rate : z.rate + z.r, :t] * gain_rows
        rate_part = jnp.sum(pays(c) * gain_rows, axis=1, keepdims=True)
        lane = (iota((z.r, t), 1) == me * z.h + iota((z.r, t), 0)) & (iota((z.r, t), 0) < z.h)
        vec[z.features : z.features + 1, :] -= jnp.sum(jnp.where(lane, rate_part, 0.0), axis=0, keepdims=True)

    z.each_chunk(leave)


def ssd_back(z, lengths, values, terms, bc, saved, early):
    outs = (
        SHAPE((z.s, z.f), BF16),
        SHAPE((z.n, z.t, z.ns), F32),
        SHAPE((z.n, z.t, z.ns), BF16),
        SHAPE((z.n, z.r, z.t), F32),
        SHAPE((z.v, z.t), F32),
    )
    scratch = [
        pltpu.VMEM((2, z.s, z.f), BF16),
        pltpu.VMEM((z.n * z.ns, z.f), F32),
        pltpu.VMEM((z.n * z.ns, z.f), BF16),
        pltpu.VMEM((z.n * 8, z.f), F32),
        pltpu.VMEM((2, z.s, z.t), F32),
    ]
    return call(
        z,
        ssd_back_kernel,
        "ssd_back",
        outs,
        [SM] + [VM] * (z.n + 6),
        [VM] * 5,
        scratch,
        (lengths, *values, terms, bc, saved, *early),
        flops=z.s * z.f * z.ns * 20,
        nbytes=z.s * z.f * 32,
    )


def attend_back_kernel(z, g, *refs):
    n, t, count = z.n, z.t, z.sizes[g]
    held, prob, grad_in, refs = *refs[:3], refs[3:]
    grad = grad_in.at[:, z.lanes(g)]
    if g == 0:
        keep, other, step, vec, refs = *refs[:4], refs[4:]
    else:
        refs = refs[1:]
    outs, refs = refs[:n], refs[n:]
    result, dscore = refs
    me = lax.axis_index("context")
    if g == 0:
        end = 3 * count * t
        for j in range(n):
            result[j, end : end + t] = (keep[j] + other[j].astype(F32)).astype(BF16)
            result[j, end + t :] = jnp.zeros((z.rp + 2 * z.v, t), BF16)
            result[j, end + t : end + t + z.r] = step[j].astype(BF16)
            result[j, end + t + z.rp :] = jnp.concatenate(split3(vec[...])[:2], axis=0)
    factor = 1.0 / math.sqrt(z.hd)
    per = z.rows // t

    def rows_span(k, a, first, last):
        return held[first // t : last // t, z.rows_of(g, k, a), :].reshape(last - first, z.hd)

    def store(k, a, i, x):
        result[pl.ds(i * per, per), z.rows_of(g, k, a), :] = x.astype(BF16).reshape(per, t, z.hd)

    for a in range(count):
        lanes = slice(a * z.hd, (a + 1) * z.hd)

        def by_query(i):
            width, rows = z.upto(i), z.block(i)
            p = prob[a, rows, :width].astype(F32)
            dp = dot_nt(grad[rows, lanes], rows_span(2, a, 0, width))
            product = p * dp
            ds = (product - p * jnp.sum(product, axis=1, keepdims=True)).astype(BF16)
            dscore[a, rows, :width] = ds
            store(0, a, i, dot(ds, rows_span(1, a, 0, width)) * factor)

        z.each_block(by_query)

        def by_key(j):
            start, cols = z.onward(j), z.block(j)
            store(1, a, j, dot_tn(dscore[a, start:, cols], rows_span(0, a, start, z.s)) * factor)
            store(2, a, j, dot_tn(prob[a, start:, cols], grad[start:, lanes]))

        z.each_block(by_key)
    for s in range(n):
        outs[s][...] = result[lax.rem(me + z.back_shifts[g][s], n)]


def attend_back(z, g, qkv, prob, grad, small):
    count = z.sizes[g]
    rows = z.back_rows(g)
    scratch = [
        pltpu.VMEM((z.n, rows, z.hd), BF16),
        pltpu.VMEM((count, z.s, z.s), BF16),
    ]
    return call(
        z,
        lambda z, *refs: attend_back_kernel(z, g, *refs),
        "attend_back_%d" % g,
        [SHAPE((rows, z.hd), BF16)] * z.n,
        [VM] * 3 + ([ANY] if g else [VM] * len(small)),
        [VM] * z.n,
        scratch,
        (qkv, prob, grad, *small),
        flops=count * z.s * z.s * z.hd * 8,
        nbytes=count * z.s * z.s * 8,
    )


def unpack_kernel(z, *refs):
    n, t = z.n, z.t
    ins, (proj, step, vecs) = refs[:n], refs[n:]
    me = lax.axis_index("context")
    parts = [ins[s][3 * z.sizes[0] * t :] for s in range(n)]
    total = jnp.zeros((t, z.ns), F32)
    steps = jnp.zeros((n * z.h, t), F32)
    for s in range(n):
        total = total + parts[s][:t].astype(F32)
        source = lax.rem(me + n - z.back_shifts[0][s], n)
        row, col = iota((n * z.h, z.r), 0), iota((n * z.h, z.r), 1)
        place = mat((row == source * z.h + col) & (col < z.h)).astype(BF16)
        steps = steps + dot(place, parts[s][t : t + z.r])
        vec = parts[s][t + z.rp :].astype(F32)
        vecs[source] = vec[: z.v] + vec[z.v :]
    proj[...] = total
    step[0] = steps


def unpack(z, parts):
    return call(
        z,
        unpack_kernel,
        "unpack",
        (SHAPE((z.t, z.ns), F32), SHAPE((1, z.n * z.h, z.t), F32), SHAPE((z.n, z.v, z.t), F32)),
        [VM] * z.n,
        [VM] * 3,
        [],
        parts,
    )


def choose_kernel(z, lengths, mine, theirs, vecs, b, c, weight, rate, loss):
    core = lax.axis_index("head")
    b[0] = jnp.where(core == 0, mine[...], theirs[...])
    c[0] = jnp.where(core == 0, theirs[...], mine[...])
    valid = lengths[0]
    for k in range(1, lengths.shape[0]):
        valid = valid + lengths[k]
    rates = jnp.zeros((1, z.t), F32)
    for j in range(z.n):
        weight[j] = vecs[j, : z.features]
        rates = rates + vecs[j, z.features : z.features + 1]
    losses = vecs[0, z.features + 1 : z.features + 2]
    loss[...] = jnp.sum(losses, axis=1, keepdims=True) / valid.astype(F32)
    rate[...] = rates[:, : z.n * z.h]


def choose(z, lengths, mine, theirs, vecs):
    return call(
        z,
        choose_kernel,
        "choose",
        (
            SHAPE((1, z.t, z.ns), F32),
            SHAPE((1, z.t, z.ns), F32),
            SHAPE((z.n, z.features, z.hd), F32),
            SHAPE((1, z.n * z.h), F32),
            SHAPE((1, 1), F32),
        ),
        [SM] + [VM] * 3,
        [VM] * 5,
        [],
        (lengths, mine, theirs, vecs),
    )


def finish_kernel(z, *refs):
    count = z.n * z.groups
    ins, out, refs = refs[:count], refs[count], refs[count + 1 :]
    held, (turned, sems) = refs[: z.groups], refs[z.groups :]
    me = lax.axis_index("context")
    mover = Copies(sems)
    for g in range(z.groups):
        for s in range(z.n):
            held[g][lax.rem(me + z.n - z.back_shifts[g][s], z.n)] = ins[g * z.n + s][: 3 * z.sizes[g] * z.t]
    stores = []
    for k in range(3):
        heads = [
            held[g][j, z.rows_of(g, k, a), :]
            for j in range(z.n)
            for g in range(z.groups)
            for a in range(z.sizes[g])
        ]
        turned[k] = jnp.swapaxes(jnp.stack(heads), 0, 1)
        stores.append(mover.start(turned.at[k], out.at[k, 0]))
    wait_all(stores)


def finish(z, parts):
    return call(
        z,
        finish_kernel,
        "finish",
        SHAPE((3, 1, z.t, z.hl, z.hd), BF16),
        [VM] * (z.n * z.groups),
        ANY,
        [
            *[pltpu.VMEM((z.n, 3 * k * z.t, z.hd), BF16) for k in z.sizes],
            pltpu.VMEM((3, z.t, z.hl, z.hd), BF16),
            pltpu.SemaphoreType.DMA((3,)),
        ],
        parts,
        nbytes=12 * z.t * z.hl * z.hd,
    )


def shift(x, axis, size, step):
    return lax.ppermute(x, axis, [(i, (i + step) % size) for i in range(size)])


def spread(parts, axis, shifts):
    return [parts[0]] + [shift(x, axis, len(parts), s) for x, s in zip(parts[1:], shifts[1:])]


def partners(x, axis, step):
    return lax.ppermute(x, axis, [(i, i ^ step) for i in range(lax.axis_size(axis))])


def local(qkv, ssd_b, ssd_c, step_size, decay_rate, value_weight, returns, step_labels, lengths):
    n = lax.axis_size("context")
    z = Sizes(n, qkv.shape[2], qkv.shape[3], qkv.shape[4], step_size.shape[2], ssd_b.shape[2])

    sends = prep(z, qkv, ssd_b, ssd_c, jnp.swapaxes(step_size, 1, 2), step_labels, returns)
    arrived = [spread(sends[g * n : (g + 1) * n], "context", z.shifts[g]) for g in range(z.groups)]
    mine, pay = pick(z, arrived[0])
    theirs = shift(mine, "head", 2, 1)
    attended = [attend(z, 0, arrived[0], [])]
    terms, bc = decay(z, mine, theirs, pay, decay_rate.reshape(1, -1), value_weight.reshape(z.hl, z.hd))
    for g in range(1, z.groups):
        attended.append(attend(z, g, arrived[g], [bc]))
    saved, value = ssd(z, [x[1] for x in attended], terms, bc)
    early = ssd_pre(z, bc, saved)
    value = value + shift(value, "head", 2, 1)
    values = [value] + [partners(value, "context", s) for s in range(1, n)]
    grad, keep, give, steps, vec = ssd_back(z, lengths, values, terms, bc, saved, early)
    finals, small = [], [keep, shift(give, "head", 2, 1), steps, vec]
    for g in range(z.groups):
        back = attend_back(z, g, attended[g][2], attended[g][0], grad, small)
        finals.append(spread(back, "context", z.back_shifts[g]))
        small = back[:1]
    proj, step_grad, vecs = unpack(z, finals[0])
    other = shift(proj, "head", 2, 1)
    step = 1
    while step < lax.axis_size("rollout"):
        vecs = vecs + partners(vecs, "rollout", step)
        step *= 2
    b_grad, c_grad, weight_grad, rate_grad, loss = choose(z, lengths, proj, other, vecs)
    qkv_grad = finish(z, [x for part in finals for x in part])
    return (
        loss.reshape(()),
        qkv_grad,
        b_grad,
        c_grad,
        jnp.swapaxes(step_grad, 1, 2),
        rate_grad.reshape(-1),
        weight_grad.reshape(-1),
    )


def solution(mesh):
    in_specs = (
        P(None, "rollout", "context", "head", None),
        P("rollout", "context", None),
        P("rollout", "context", None),
        P("rollout", "context", "head"),
        P("head"),
        P("head"),
        P("rollout", None),
        P("rollout", "context"),
        P(),
    )
    out_specs = (
        P(),
        P(None, "rollout", "context", "head", None),
        P("rollout", "context", None),
        P("rollout", "context", None),
        P("rollout", "context", "head"),
        P("head"),
        P("head"),
    )
    return jax.shard_map(local, mesh=mesh, in_specs=in_specs, out_specs=out_specs, check_vma=False)
```

```python
import functools
import math

import jax
import jax.numpy as jnp
from jax import lax
from jax.experimental import pallas as pl
from jax.experimental.pallas import tpu as pltpu
from jax.sharding import PartitionSpec as P

MASK_FILL = -1e30
NORM_EPS = 1e-05
HIGHEST = lax.Precision.HIGHEST
LOG2E = 1.4426950408889634
GROUPS = (2, 2)
VMEM_MIB = 24
F32 = jnp.float32
BF16 = jnp.bfloat16

ANY = pl.BlockSpec(memory_space=pl.ANY)
SHAPE = jax.ShapeDtypeStruct
VM = pl.BlockSpec(memory_space=pltpu.VMEM)
SM = pl.BlockSpec(memory_space=pltpu.SMEM)


def dot(a, b, precision=None):
    return jnp.dot(a, b, preferred_element_type=F32, precision=precision)


def dot_nt(a, b, precision=None):
    return lax.dot_general(a, b, (((1,), (1,)), ((), ())), preferred_element_type=F32, precision=precision)


def dot_tn(a, b, precision=None):
    return lax.dot_general(a, b, (((0,), (0,)), ((), ())), preferred_element_type=F32, precision=precision)


def iota(shape, dim):
    return lax.broadcasted_iota(jnp.int32, shape, dim)


def mat(cond):
    return jnp.where(cond, 1.0, 0.0).astype(F32)


class Sizes:
    def __init__(self, n, tokens, heads_local, head_dim, ssd_local, state):
        self.n, self.t, self.hl, self.hd, self.ns = n, tokens, heads_local, head_dim, state
        self.s = n * tokens
        self.a = heads_local // n
        self.sizes = GROUPS if sum(GROUPS) == self.a else (self.a,)
        self.first = [sum(self.sizes[:g]) for g in range(len(self.sizes))]
        self.groups = len(self.sizes)
        natural = list(range(n))
        half_first = sorted(natural, key=lambda s: (s != 0, s != n // 2, s))
        self.shifts = [natural for _ in self.sizes]
        self.back_shifts = [half_first for _ in self.sizes]
        self.h = ssd_local // n
        self.hl_ssd = ssd_local
        self.mp = heads_local * head_dim // ssd_local
        self.f = self.a * head_dim
        self.r = -(-(self.h + 1) // 8) * 8
        self.rp = -(-self.r // 16) * 16
        self.features = self.f // head_dim
        self.v = -(-(self.features + 2) // 8) * 8
        self.rows = min(256, self.s)
        self.blocks = self.s // self.rows
        self.static = self.blocks <= 2
        self.parts = 2 if self.static and n % 2 == 0 else 1
        self.per = n // self.parts
        self.up, self.down, self.mid = 0, self.s, 2 * self.s
        self.pay = self.mid + 8 * n
        self.rate = self.pay + self.r * n
        self.weight = self.rate + self.r
        self.term_rows = self.weight + 8
        self.pay_rows = tokens + 2 * self.rp

    def sent_rows(self, g):
        return 3 * self.sizes[g] * self.t + (0 if g else self.pay_rows)

    def back_rows(self, g):
        rows = 3 * self.sizes[g] * self.t
        if g == 0:
            rows += self.t + self.rp + 2 * self.v
        return rows

    def rows_of(self, g, k, a):
        first = (k * self.sizes[g] + a) * self.t
        return slice(first, first + self.t)

    def lanes(self, g):
        return pl.ds(self.first[g] * self.hd, self.sizes[g] * self.hd)

    def each_block(self, body):
        if self.static:
            for i in range(self.blocks):
                body(i)
        else:

            @pl.loop(0, self.blocks)
            def _(i):
                body(i)

    def upto(self, i):
        return (i + 1) * self.rows if self.static else self.s

    def onward(self, i):
        return i * self.rows if self.static else 0

    def each_chunk(self, body):
        if self.static:
            for c in range(self.n):
                body(c)
        else:

            @pl.loop(0, self.n)
            def _(c):
                body(c)

    def chunk(self, c, base=0):
        return pl.ds(base + c * self.t if isinstance(c, int) else pl.multiple_of(base + c * self.t, self.t), self.t)

    def small(self, c, base, rows):
        return pl.ds(base + c * rows if isinstance(c, int) else pl.multiple_of(base + c * rows, 8), rows)

    def block(self, i):
        return pl.ds(i * self.rows if self.static else pl.multiple_of(i * self.rows, self.rows), self.rows)


def call(z, kernel, name, out_shape, in_specs, out_specs, scratch, args, flops=0, nbytes=0):
    return pl.pallas_call(
        functools.partial(kernel, z),
        name=name,
        out_shape=out_shape,
        in_specs=in_specs,
        out_specs=out_specs,
        scratch_shapes=scratch,
        compiler_params=pltpu.CompilerParams(vmem_limit_bytes=(VMEM_MIB if z.static else 56) * 1024 * 1024),
        cost_estimate=pl.CostEstimate(flops=flops, bytes_accessed=nbytes, transcendentals=0),
    )(*args)


def in_hbm(x):
    return pltpu.with_memory_space_constraint(x, pltpu.HBM)


class Copies:
    def __init__(self, sems):
        self.sems, self.count = sems, 0

    def start(self, source, target):
        one = pltpu.make_async_copy(source, target, self.sems.at[self.count])
        self.count += 1
        one.start()
        return one


def wait_all(copies):
    for one in copies:
        one.wait()


def split3(x):
    high = x.astype(BF16)
    rest = x - high.astype(F32)
    middle = rest.astype(BF16)
    return high, middle, (rest - middle.astype(F32)).astype(BF16)


def split2_dot(x, exact):
    high, low = split3(x)[:2]
    return dot(high, exact) + dot(low, exact)


def prep_kernel(z, qkv, b_in, c_in, step_in, labels_in, table_in, *refs):
    outs, refs = refs[: z.n * z.groups], refs[z.n * z.groups :]
    held, (parts, b, c, step, labels, table, sems) = refs[: z.groups], refs[z.groups :]
    me, core = lax.axis_index("context"), lax.axis_index("head")
    mover = Copies(sems)
    tiny = [
        mover.start(b_in.at[0], b),
        mover.start(c_in.at[0], c),
        mover.start(step_in.at[0], step),
        mover.start(labels_in, labels),
        mover.start(table_in, table),
    ]
    loads = [mover.start(qkv.at[k, 0], parts.at[k]) for k in range(3)]
    wait_all(tiny)
    onehot = mat(iota((table.shape[1], z.t), 0) == labels[...])
    target = dot(table[...], onehot, HIGHEST)
    mine = jnp.where(core == 0, b[...], c[...])
    end = 3 * z.sizes[0] * z.t
    for j in range(z.n):
        row = iota((z.r, z.hl_ssd), 0)
        pick = mat((iota((z.r, z.hl_ssd), 1) == j * z.h + row) & (row < z.h))
        pay = dot(pick, step[...], HIGHEST)
        pay = jnp.where(iota((z.r, z.t), 0) == z.h, target, pay)
        held[0][j, end : end + z.t] = mine
        held[0][j, end + z.t :] = jnp.zeros((2 * z.rp, z.t), BF16)
        for i, term in enumerate(split3(pay)[:2]):
            start = end + z.t + i * z.rp
            held[0][j, start : start + z.r] = term
    for k in range(3):
        loads[k].wait()
        turned = jnp.swapaxes(parts[k], 0, 1)
        for g in range(z.groups):
            for j in range(z.n):
                for a in range(z.sizes[g]):
                    held[g][j, z.rows_of(g, k, a), :] = turned[j * z.a + z.first[g] + a]
    for g in range(z.groups):
        for s in range(z.n):
            outs[g * z.n + s][...] = held[g][lax.rem(me + z.shifts[g][s], z.n)]


def prep(z, qkv, b, c, step, labels, table):
    args = [in_hbm(x) for x in (qkv, b, c, step, labels, table)]
    return call(
        z,
        prep_kernel,
        "prep",
        [SHAPE((z.sent_rows(g), z.hd), BF16) for g in range(z.groups) for _ in range(z.n)],
        [ANY] * 6,
        [VM] * (z.n * z.groups),
        [
            *[pltpu.VMEM((z.n, z.sent_rows(g), z.hd), BF16) for g in range(z.groups)],
            pltpu.VMEM((3, z.t, z.hl, z.hd), BF16),
            pltpu.VMEM((z.t, z.ns), BF16),
            pltpu.VMEM((z.t, z.ns), BF16),
            pltpu.VMEM(step.shape[1:], F32),
            pltpu.VMEM(labels.shape, jnp.int32),
            pltpu.VMEM(table.shape, F32),
            pltpu.SemaphoreType.DMA((8,)),
        ],
        args,
        nbytes=qkv.size * 4,
    )


def pick_kernel(z, *refs):
    ins, (mine, pay) = refs[: z.n], refs[z.n :]
    me = lax.axis_index("context")
    first = 3 * z.sizes[0] * z.t
    for s in range(z.n):
        source = lax.rem(me + z.n - z.shifts[0][s], z.n)
        mine[source] = ins[s][first : first + z.t]
        start = first + z.t
        terms = [ins[s][start + k * z.rp : start + k * z.rp + z.r].astype(F32) for k in range(2)]
        pay[source] = terms[0] + terms[1]


def pick(z, ins):
    return call(
        z,
        pick_kernel,
        "pick",
        (SHAPE((z.n, z.t, z.ns), BF16), SHAPE((z.n, z.r, z.t), F32)),
        [VM] * z.n,
        [VM] * 2,
        [],
        ins,
    )


def decay_kernel(z, mine, theirs, pay, rate, weight, terms, bc):
    n, t = z.n, z.t
    me, core = lax.axis_index("context"), lax.axis_index("head")
    heads = z.hl_ssd
    row, col = iota((z.r, heads), 0), iota((z.r, heads), 1)
    pick = mat((col == me * z.h + row) & (row < z.h))
    terms[z.rate : z.rate + z.r, :t] = dot_nt(pick, jnp.broadcast_to(rate[...], (t, heads)), HIGHEST)
    pick = mat(iota((8, z.hl), 1) == me * z.a + iota((8, z.hl), 0))
    terms[z.weight : z.weight + 8, : z.hd] = dot(pick, weight[...].astype(F32))
    rates = jnp.broadcast_to(rate[...], (8, heads))
    rates = dot(rates, mat(iota((heads, z.f), 0) == me * z.h + iota((heads, z.f), 1) // z.mp), HIGHEST)
    rates = rates[0:1]
    for c in range(n):
        bc[c, 0] = jnp.where(core == 0, mine[c], theirs[c])
        bc[c, 1] = jnp.where(core == 0, theirs[c], mine[c])
        terms[z.pay + c * z.r : z.pay + (c + 1) * z.r, :t] = pay[c]
    causal = iota((t, t), 0) >= iota((t, t), 1)
    lower = mat(causal)
    spread_heads = mat(iota((z.r, z.f), 0) == iota((z.r, z.f), 1) // z.mp)

    def chunk(c):
        steps = terms[z.small(c, z.pay, z.r), :t]
        cum = dot(dot_nt(lower, steps, HIGHEST), spread_heads, HIGHEST) * (-rates)
        half = 0.5 * cum[t - 1 : t]
        terms[z.chunk(c, z.up), :] = jnp.exp(cum - half)
        terms[z.chunk(c, z.down), :] = jnp.exp(half - cum)
        terms[z.small(c, z.mid, 8), :] = jnp.broadcast_to(jnp.exp(half), (8, z.f))
        inner = split3(jnp.where(causal, dot_nt(bc[c, 1], bc[c, 0]), 0.0))
        bc[c, 2] = inner[0]
        bc[c, 3] = inner[1]

    z.each_chunk(chunk)


def decay(z, mine, theirs, pay, rate, weight):
    return call(
        z,
        decay_kernel,
        "decay",
        (SHAPE((z.term_rows, z.f), F32), SHAPE((z.n, 4, z.t, z.ns), BF16)),
        [VM] * 5,
        [VM] * 2,
        [],
        (mine, theirs, pay, rate, weight),
        nbytes=8 * z.s * z.f,
    )


def attend_kernel(z, g, *refs):
    n, t, count = z.n, z.t, z.sizes[g]
    ins, refs = refs[:n], refs[n:]
    prob, attended, held = refs
    me = lax.axis_index("context")
    for s in range(n):
        held[lax.rem(me + n - z.shifts[g][s], n)] = ins[s][: 3 * count * t]

    def rows_upto(k, a, width):
        return held[: width // t, z.rows_of(g, k, a), :].reshape(width, z.hd)

    def rows_block(k, a, i):
        per = z.rows // t
        return held[pl.ds(i * per, per), z.rows_of(g, k, a), :].reshape(z.rows, z.hd)

    factor = LOG2E / math.sqrt(z.hd)
    for a in range(count):

        def attend(i):
            width = z.upto(i)
            rows = z.block(i)
            scores = dot_nt(rows_block(0, a, i), rows_upto(1, a, width))
            keep = iota((z.rows, width), 1) <= i * z.rows + iota((z.rows, width), 0)
            scores = jnp.where(keep, scores, MASK_FILL)
            weight = jnp.exp2((scores - jnp.max(scores, axis=1, keepdims=True)) * factor)
            weight = (weight * (1.0 / jnp.sum(weight, axis=1, keepdims=True))).astype(BF16)
            prob[a, rows, :width] = weight
            attended[rows, a * z.hd : (a + 1) * z.hd] = dot(weight, rows_upto(2, a, width)).astype(BF16)

        z.each_block(attend)


def attend(z, g, ins):
    count = z.sizes[g]
    outs = (
        SHAPE((count, z.s, z.s), BF16),
        SHAPE((z.s, count * z.hd), BF16),
        SHAPE((z.n, 3 * count * z.t, z.hd), BF16),
    )
    return call(
        z,
        lambda z, *refs: attend_kernel(z, g, *refs),
        "attend_%d" % g,
        outs,
        [VM] * z.n,
        [VM] * 3,
        [],
        ins,
        flops=count * z.s * z.s * z.hd * 4,
        nbytes=count * z.s * z.s * 8,
    )


def ssd_kernel(z, *refs):
    n, t = z.n, z.t
    ins, refs = refs[: z.groups], refs[z.groups :]
    terms, bc, saved, value, state_low, adds = refs
    same_head = mat(iota((z.hd, z.hd), 0) // z.mp == iota((z.hd, z.hd), 1) // z.mp).astype(BF16)

    def enter(c):
        rows = z.chunk(c)
        attended = jnp.concatenate([one[rows, :] for one in ins], axis=1)
        high, low = split3(terms[z.chunk(c, z.down), :] * attended.astype(F32))[:2]
        saved[0, rows, :] = high
        saved[5, rows, :] = low
        adds[rows, :] = dot_tn(bc[c, 0], high) + dot_tn(bc[c, 0], low)

    z.each_chunk(enter)

    def step(c, state):
        m = terms[z.small(c, z.mid, 8), :][0:1]
        state = m * state
        high, low = split3(state)[:2]
        saved[3, z.chunk(c), :] = high
        state_low[z.chunk(c), :] = low
        return m * (state + adds[z.chunk(c), :])

    state = jnp.zeros((z.ns, z.f), F32)
    if z.static:
        for c in range(n):
            state = step(c, state)
    else:
        lax.fori_loop(0, n, step, state)

    def leave(c):
        rows = z.chunk(c)
        up = terms[z.chunk(c, z.up), :]
        left = [bc[c, k] for k in (2, 2, 3, 1, 1)]
        right = [saved[0, rows, :], saved[5, rows, :], saved[0, rows, :], saved[3, rows, :], state_low[rows, :]]
        y = up * dot(jnp.concatenate(left, axis=1), jnp.concatenate(right, axis=0))
        total = jnp.zeros((t, z.hd), F32)
        for a in range(z.a):
            part = slice(a * z.hd, (a + 1) * z.hd)
            ya = y[:, part]
            weight = terms[z.weight + a : z.weight + a + 1, : z.hd]
            scale = lax.rsqrt(split2_dot(ya * ya, same_head) * (1.0 / z.mp) + NORM_EPS)
            unit = ya * scale
            term = unit * weight
            total = total + term
            mean = split2_dot(term, same_head) * (1.0 / z.mp)
            saved[1, rows, part] = unit.astype(BF16)
            slope = split3(up[:, part] * scale * (weight - unit * mean))
            saved[2, rows, part] = slope[0]
            saved[4, rows, part] = slope[1]
        high, low = split3(total)[:2]
        ones = jnp.ones((8, z.hd), BF16)
        value[:, rows] = (dot_nt(ones, high) + dot_nt(ones, low))[0:1]

    z.each_chunk(leave)


def last_kernel(z, *refs):
    n, g = z.n, z.groups - 1
    ins, before, refs = refs[:n], refs[n : n + g], refs[n + g :]
    terms, bc, prob, attended, held, *rest = refs
    attend_kernel(z, g, *ins, prob, attended, held)
    ssd_kernel(z, *before, attended, terms, bc, *rest)


def attend_and_ssd(z, ins, before, terms, bc):
    count = z.sizes[-1]
    return call(
        z,
        last_kernel,
        "attend_and_ssd",
        (
            SHAPE((count, z.s, z.s), BF16),
            SHAPE((z.s, count * z.hd), BF16),
            SHAPE((z.n, 3 * count * z.t, z.hd), BF16),
            SHAPE((6, z.s, z.f), BF16),
            SHAPE((1, z.s), F32),
        ),
        [VM] * (z.n + z.groups + 1),
        [VM] * 5,
        [
            pltpu.VMEM((z.s, z.f), BF16),
            pltpu.VMEM((z.n * z.ns, z.f), F32),
        ],
        (*ins, *before, terms, bc),
        flops=z.s * z.f * z.ns * 20,
        nbytes=z.s * z.f * 32,
    )


def ssd_pre_kernel(z, part, bc, saved, w_sums, straddled, down_sums):
    t = z.t
    causal = iota((t, t), 0) >= iota((t, t), 1)
    per_head = mat(iota((z.f, t), 1) == iota((z.f, t), 0) // z.mp).astype(BF16)

    def chunk(c):
        rows, here = z.chunk(c), z.chunk(c - part * z.per)
        sc, sl, xc, xl = saved[2, rows, :], saved[4, rows, :], saved[0, rows, :], saved[5, rows, :]
        carried = dot(bc[c, 1], saved[3, rows, :])
        down_sums[here, :] = dot(((sc.astype(F32) + sl.astype(F32)) * carried).astype(BF16), per_head)
        inner = bc[c, 2].astype(F32)
        w_sum = jnp.zeros((t, t), F32)
        for k in range(z.h):
            first = k * z.mp // z.hd * z.hd
            mine = iota((t, z.hd), 1) // z.mp == k % (z.hd // z.mp)
            pair = slice(first, first + z.hd)
            x_head = jnp.where(mine, xc[:, pair], jnp.zeros((), BF16))
            x_low = jnp.where(mine, xl[:, pair], jnp.zeros((), BF16))
            left = jnp.concatenate([sc[:, pair], sl[:, pair], sc[:, pair]], axis=1)
            w = jnp.where(causal, dot_nt(left, jnp.concatenate([x_head, x_head, x_low], axis=1)), 0.0)
            w_sum += w
            straddled[here, k * t : (k + 1) * t] = (w * inner).astype(BF16)
        w_sums[here, :] = w_sum

    if z.parts > 1:
        for c in range(part * z.per, (part + 1) * z.per):
            chunk(c)
    else:
        z.each_chunk(chunk)


def ssd_pre(z, part, bc, saved):
    rows = z.per * z.t
    return call(
        z,
        lambda z, *refs: ssd_pre_kernel(z, part, *refs),
        "ssd_pre_%d" % part,
        (SHAPE((rows, z.t), F32), SHAPE((rows, z.h * z.t), BF16), SHAPE((rows, z.t), F32)),
        [VM] * 2,
        [VM] * 3,
        [],
        (bc, saved),
        flops=rows * z.f * z.ns * 20,
        nbytes=rows * z.f * 8,
    )


def ssd_back_kernel(z, *refs):
    n, t = z.n, z.t
    lengths, values, refs = refs[0], refs[1 : n + 1], refs[n + 1 :]
    terms, bc, saved, refs = *refs[:3], refs[3:]
    early, refs = refs[: 3 * z.parts], refs[3 * z.parts :]

    def made(kind, c):
        part = c // z.per if z.parts > 1 else 0
        return early[3 * part + kind][z.chunk(c - part * z.per), :]

    grads, keep_out, give_out, step_out, vec, refs = *refs[:5], refs[5:]
    d, adds, dstates, through, errors = refs
    me, core = lax.axis_index("context"), lax.axis_index("head")
    length = lengths[lax.axis_index("rollout")]
    value = values[0][...]
    for s in range(1, n):
        value = value + values[s][...]
    row_id, col_id = iota((t, t), 0), iota((t, t), 1)
    strict = row_id > col_id
    after = mat(col_id >= row_id).astype(BF16)
    before = mat(strict).astype(BF16)
    per_head = mat(iota((z.f, t), 1) == iota((z.f, t), 0) // z.mp).astype(BF16)
    per_row = mat(iota((z.h * t, t), 1) == iota((z.h * t, t), 0) // t).astype(BF16)
    vec[...] = jnp.zeros_like(vec)

    def pays(c):
        return terms[z.small(c, z.pay, z.r), :t]

    def enter(c):
        rows = z.chunk(c)
        if z.static:
            value_row = value[:, c * t : (c + 1) * t]
        else:
            value_row = jnp.zeros((1, t), F32)
            for j in range(n):
                value_row = jnp.where(c == j, value[:, j * t : (j + 1) * t], value_row)
        valid = c * t + iota((1, t), 1) < length
        error = jnp.where(valid, value_row - pays(c)[z.h : z.h + 1], 0.0)
        vec[z.features + 1 : z.features + 2, :] += 0.5 * error * error
        column = jnp.transpose(jnp.broadcast_to(error, (t, t)))
        errors[0, rows, :] = jnp.broadcast_to(error, (t, t))
        errors[1, rows, :] = column
        wide = jnp.concatenate([column] * (z.f // t), axis=1)
        dc = split3(wide * (saved[2, rows, :].astype(F32) + saved[4, rows, :].astype(F32)))[:2]
        d[0, rows, :] = dc[0]
        d[1, rows, :] = dc[1]
        adds[rows, :] = dot_tn(bc[c, 1], dc[0]) + dot_tn(bc[c, 1], dc[1])
        high, low = split3(error)[:2]
        pair = jnp.concatenate([high, low, jnp.zeros((6, t), BF16)], axis=0)
        weight_grad = dot(pair, saved[1, rows, :])
        weight_grad = weight_grad[0:1] + weight_grad[1:2]
        for a in range(z.features):
            vec[a : a + 1, :] += weight_grad[:, a * z.hd : (a + 1) * z.hd]

    z.each_chunk(enter)

    def carry(c, dstate):
        m = terms[z.small(c, z.mid, 8), :][0:1]
        rows = z.chunk(c)
        dstate = m * dstate
        dstates[rows, :] = dstate.astype(BF16)
        sums = jnp.sum(dstate * saved[3, rows, :].astype(F32), axis=0, keepdims=True)
        through[z.small(c, 0, 8), :] = jnp.broadcast_to(sums, (8, z.f))
        return m * (dstate + adds[rows, :])

    dstate = jnp.zeros((z.ns, z.f), F32)
    if z.static:
        for c in range(n - 1, -1, -1):
            dstate = carry(c, dstate)
    else:
        lax.fori_loop(0, n, lambda k, v: carry(n - 1 - k, v), dstate)

    def leave(c):
        rows = z.chunk(c)
        b, cp, inner = bc[c, 0], bc[c, 1], bc[c, 2]
        dc, dl = d[0, rows, :], d[1, rows, :]
        xc, state_in, dstate_in = saved[0, rows, :], saved[3, rows, :], dstates[rows, :]
        local = dot_tn(inner, dc) + dot_tn(inner, dl)
        outer = dot(b, dstate_in)
        grads[rows, :] = (terms[z.chunk(c, z.down), :] * (local + outer)).astype(BF16)
        grad_c = dot_nt(dc, state_in) + dot_nt(dl, state_in)
        grad_b = dot_nt(xc, dstate_in)
        down_sum = errors[1, rows, :] * made(2, c)
        up_sum = dot((xc.astype(F32) * outer).astype(BF16), per_head)
        straddle = dot(jnp.where(col_id >= row_id, errors[0, rows, :], 0.0).astype(BF16), made(1, c))
        straddle = jnp.concatenate(
            [jnp.where(strict, straddle[:, k * t : (k + 1) * t], 0.0).astype(BF16) for k in range(z.h)], axis=1
        )
        sums = [*split3(down_sum)[:2], *split3(up_sum)[:2]]
        gain = dot(
            jnp.concatenate([after, after, before, before], axis=1), jnp.concatenate(sums, axis=0)
        ) + dot(straddle, per_row)
        gain = gain + split2_dot(through[z.small(c, 0, 8), :], per_head)[0:1]
        w_low = (errors[1, rows, :] * made(0, c)).astype(BF16)
        grad_c += dot(w_low, b)
        grad_b += dot_tn(w_low, cp)
        keep_out[c] = jnp.where(core == 0, grad_b, grad_c)
        give_out[c] = jnp.where(core == 0, grad_c, grad_b).astype(BF16)
        gain_rows = jnp.transpose(gain)[: z.r]
        step_out[c] = -terms[z.rate : z.rate + z.r, :t] * gain_rows
        rate_part = jnp.sum(pays(c) * gain_rows, axis=1, keepdims=True)
        lane = (iota((z.r, t), 1) == me * z.h + iota((z.r, t), 0)) & (iota((z.r, t), 0) < z.h)
        vec[z.features : z.features + 1, :] -= jnp.sum(jnp.where(lane, rate_part, 0.0), axis=0, keepdims=True)

    z.each_chunk(leave)


def ssd_back(z, lengths, values, terms, bc, saved, early):
    outs = (
        SHAPE((z.s, z.f), BF16),
        SHAPE((z.n, z.t, z.ns), F32),
        SHAPE((z.n, z.t, z.ns), BF16),
        SHAPE((z.n, z.r, z.t), F32),
        SHAPE((z.v, z.t), F32),
    )
    scratch = [
        pltpu.VMEM((2, z.s, z.f), BF16),
        pltpu.VMEM((z.n * z.ns, z.f), F32),
        pltpu.VMEM((z.n * z.ns, z.f), BF16),
        pltpu.VMEM((z.n * 8, z.f), F32),
        pltpu.VMEM((2, z.s, z.t), F32),
    ]
    return call(
        z,
        ssd_back_kernel,
        "ssd_back",
        outs,
        [SM] + [VM] * (z.n + 3 + 3 * z.parts),
        [VM] * 5,
        scratch,
        (lengths, *values, terms, bc, saved, *early),
        flops=z.s * z.f * z.ns * 20,
        nbytes=z.s * z.f * 32,
    )


def attend_back_kernel(z, g, *refs):
    n, t, count = z.n, z.t, z.sizes[g]
    held, prob, grad_in, refs = *refs[:3], refs[3:]
    grad = grad_in.at[:, z.lanes(g)]
    if g == 0:
        keep, other, step, vec, refs = *refs[:4], refs[4:]
    else:
        refs = refs[1:]
    outs, refs = refs[:n], refs[n:]
    result, dscore = refs
    me = lax.axis_index("context")
    if g == 0:
        end = 3 * count * t
        for j in range(n):
            result[j, end : end + t] = (keep[j] + other[j].astype(F32)).astype(BF16)
            result[j, end + t :] = jnp.zeros((z.rp + 2 * z.v, t), BF16)
            result[j, end + t : end + t + z.r] = step[j].astype(BF16)
            result[j, end + t + z.rp :] = jnp.concatenate(split3(vec[...])[:2], axis=0)
    factor = 1.0 / math.sqrt(z.hd)
    per = z.rows // t

    def rows_span(k, a, first, last):
        return held[first // t : last // t, z.rows_of(g, k, a), :].reshape(last - first, z.hd)

    def store(k, a, i, x):
        result[pl.ds(i * per, per), z.rows_of(g, k, a), :] = x.astype(BF16).reshape(per, t, z.hd)

    for a in range(count):
        lanes = slice(a * z.hd, (a + 1) * z.hd)

        def by_query(i):
            width, rows = z.upto(i), z.block(i)
            p = prob[a, rows, :width].astype(F32)
            dp = dot_nt(grad[rows, lanes], rows_span(2, a, 0, width))
            product = p * dp
            ds = (product - p * jnp.sum(product, axis=1, keepdims=True)).astype(BF16)
            dscore[a, rows, :width] = ds
            store(0, a, i, dot(ds, rows_span(1, a, 0, width)) * factor)

        z.each_block(by_query)

        def by_key(j):
            start, cols = z.onward(j), z.block(j)
            store(1, a, j, dot_tn(dscore[a, start:, cols], rows_span(0, a, start, z.s)) * factor)
            store(2, a, j, dot_tn(prob[a, start:, cols], grad[start:, lanes]))

        z.each_block(by_key)
    for s in range(n):
        outs[s][...] = result[lax.rem(me + z.back_shifts[g][s], n)]


def attend_back(z, g, qkv, prob, grad, small):
    count = z.sizes[g]
    rows = z.back_rows(g)
    scratch = [
        pltpu.VMEM((z.n, rows, z.hd), BF16),
        pltpu.VMEM((count, z.s, z.s), BF16),
    ]
    return call(
        z,
        lambda z, *refs: attend_back_kernel(z, g, *refs),
        "attend_back_%d" % g,
        [SHAPE((rows, z.hd), BF16)] * z.n,
        [VM] * 3 + ([ANY] if g else [VM] * len(small)),
        [VM] * z.n,
        scratch,
        (qkv, prob, grad, *small),
        flops=count * z.s * z.s * z.hd * 8,
        nbytes=count * z.s * z.s * 8,
    )


def unpack_kernel(z, *refs):
    n, t = z.n, z.t
    ins, (proj, step, vecs) = refs[:n], refs[n:]
    me = lax.axis_index("context")
    parts = [ins[s][3 * z.sizes[0] * t :] for s in range(n)]
    total = jnp.zeros((t, z.ns), F32)
    steps = jnp.zeros((n * z.h, t), F32)
    for s in range(n):
        total = total + parts[s][:t].astype(F32)
        source = lax.rem(me + n - z.back_shifts[0][s], n)
        row, col = iota((n * z.h, z.r), 0), iota((n * z.h, z.r), 1)
        place = mat((row == source * z.h + col) & (col < z.h)).astype(BF16)
        steps = steps + dot(place, parts[s][t : t + z.r])
        vec = parts[s][t + z.rp :].astype(F32)
        vecs[source] = vec[: z.v] + vec[z.v :]
    proj[...] = total
    step[0] = steps


def unpack(z, parts):
    return call(
        z,
        unpack_kernel,
        "unpack",
        (SHAPE((z.t, z.ns), F32), SHAPE((1, z.n * z.h, z.t), F32), SHAPE((z.n, z.v, z.t), F32)),
        [VM] * z.n,
        [VM] * 3,
        [],
        parts,
    )


def choose_kernel(z, lengths, mine, theirs, vecs, b, c, weight, rate, loss):
    core = lax.axis_index("head")
    b[0] = jnp.where(core == 0, mine[...], theirs[...])
    c[0] = jnp.where(core == 0, theirs[...], mine[...])
    valid = lengths[0]
    for k in range(1, lengths.shape[0]):
        valid = valid + lengths[k]
    rates = jnp.zeros((1, z.t), F32)
    for j in range(z.n):
        weight[j] = vecs[j, : z.features]
        rates = rates + vecs[j, z.features : z.features + 1]
    losses = vecs[0, z.features + 1 : z.features + 2]
    loss[...] = jnp.sum(losses, axis=1, keepdims=True) / valid.astype(F32)
    rate[...] = rates[:, : z.n * z.h]


def choose(z, lengths, mine, theirs, vecs):
    return call(
        z,
        choose_kernel,
        "choose",
        (
            SHAPE((1, z.t, z.ns), F32),
            SHAPE((1, z.t, z.ns), F32),
            SHAPE((z.n, z.features, z.hd), F32),
            SHAPE((1, z.n * z.h), F32),
            SHAPE((1, 1), F32),
        ),
        [SM] + [VM] * 3,
        [VM] * 5,
        [],
        (lengths, mine, theirs, vecs),
    )


def finish_kernel(z, *refs):
    count = z.n * z.groups
    ins, out, refs = refs[:count], refs[count], refs[count + 1 :]
    held, (turned, sems) = refs[: z.groups], refs[z.groups :]
    me = lax.axis_index("context")
    mover = Copies(sems)
    for g in range(z.groups):
        for s in range(z.n):
            held[g][lax.rem(me + z.n - z.back_shifts[g][s], z.n)] = ins[g * z.n + s][: 3 * z.sizes[g] * z.t]
    stores = []
    for k in range(3):
        heads = [
            held[g][j, z.rows_of(g, k, a), :]
            for j in range(z.n)
            for g in range(z.groups)
            for a in range(z.sizes[g])
        ]
        turned[k] = jnp.swapaxes(jnp.stack(heads), 0, 1)
        stores.append(mover.start(turned.at[k], out.at[k, 0]))
    wait_all(stores)


def finish(z, parts):
    return call(
        z,
        finish_kernel,
        "finish",
        SHAPE((3, 1, z.t, z.hl, z.hd), BF16),
        [VM] * (z.n * z.groups),
        ANY,
        [
            *[pltpu.VMEM((z.n, 3 * k * z.t, z.hd), BF16) for k in z.sizes],
            pltpu.VMEM((3, z.t, z.hl, z.hd), BF16),
            pltpu.SemaphoreType.DMA((3,)),
        ],
        parts,
        nbytes=12 * z.t * z.hl * z.hd,
    )


def shift(x, axis, size, step):
    return lax.ppermute(x, axis, [(i, (i + step) % size) for i in range(size)])


def spread(parts, axis, shifts):
    return [parts[0]] + [shift(x, axis, len(parts), s) for x, s in zip(parts[1:], shifts[1:])]


def partners(x, axis, step):
    return lax.ppermute(x, axis, [(i, i ^ step) for i in range(lax.axis_size(axis))])


def local(qkv, ssd_b, ssd_c, step_size, decay_rate, value_weight, returns, step_labels, lengths):
    n = lax.axis_size("context")
    z = Sizes(n, qkv.shape[2], qkv.shape[3], qkv.shape[4], step_size.shape[2], ssd_b.shape[2])

    sends = prep(z, qkv, ssd_b, ssd_c, jnp.swapaxes(step_size, 1, 2), step_labels, returns)
    arrived = [spread(sends[g * n : (g + 1) * n], "context", z.shifts[g]) for g in range(z.groups)]
    mine, pay = pick(z, arrived[0])
    theirs = shift(mine, "head", 2, 1)
    attended = [attend(z, g, arrived[g]) for g in range(z.groups - 1)]
    terms, bc = decay(z, mine, theirs, pay, decay_rate.reshape(1, -1), value_weight.reshape(z.hl, z.hd))
    *last, saved, value = attend_and_ssd(z, arrived[-1], [x[1] for x in attended], terms, bc)
    attended.append(last)
    early = ssd_pre(z, 0, bc, saved)
    other, *early = lax.optimization_barrier((shift(value, "head", 2, 1), *early))
    for part in range(1, z.parts):
        early += ssd_pre(z, part, bc, saved)
    value = value + other
    values = [value] + [partners(value, "context", s) for s in range(1, n)]
    grad, keep, give, steps, vec = ssd_back(z, lengths, values, terms, bc, saved, early)
    finals, small = [], [keep, shift(give, "head", 2, 1), steps, vec]
    for g in range(z.groups):
        back = attend_back(z, g, attended[g][2], attended[g][0], grad, small)
        finals.append(spread(back, "context", z.back_shifts[g]))
        small = back[:1]
    proj, step_grad, vecs = unpack(z, finals[0])
    other = shift(proj, "head", 2, 1)
    step = 1
    while step < lax.axis_size("rollout"):
        vecs = vecs + partners(vecs, "rollout", step)
        step *= 2
    b_grad, c_grad, weight_grad, rate_grad, loss = choose(z, lengths, proj, other, vecs)
    qkv_grad = finish(z, [x for part in finals for x in part])
    return (
        loss.reshape(()),
        qkv_grad,
        b_grad,
        c_grad,
        jnp.swapaxes(step_grad, 1, 2),
        rate_grad.reshape(-1),
        weight_grad.reshape(-1),
    )


def solution(mesh):
    in_specs = (
        P(None, "rollout", "context", "head", None),
        P("rollout", "context", None),
        P("rollout", "context", None),
        P("rollout", "context", "head"),
        P("head"),
        P("head"),
        P("rollout", None),
        P("rollout", "context"),
        P(),
    )
    out_specs = (
        P(),
        P(None, "rollout", "context", "head", None),
        P("rollout", "context", None),
        P("rollout", "context", None),
        P("rollout", "context", "head"),
        P("head"),
        P("head"),
    )
    return jax.shard_map(local, mesh=mesh, in_specs=in_specs, out_specs=out_specs, check_vma=False)
```

```python
import functools
import math

import jax
import jax.numpy as jnp
from jax import lax
from jax.experimental import pallas as pl
from jax.experimental.pallas import tpu as pltpu
from jax.sharding import PartitionSpec as P

MASK_FILL = -1e30
NORM_EPS = 1e-05
HIGHEST = lax.Precision.HIGHEST
LOG2E = 1.4426950408889634
GROUPS = (2, 2)
VMEM_MIB = 24
F32 = jnp.float32
BF16 = jnp.bfloat16

ANY = pl.BlockSpec(memory_space=pl.ANY)
SHAPE = jax.ShapeDtypeStruct
VM = pl.BlockSpec(memory_space=pltpu.VMEM)
SM = pl.BlockSpec(memory_space=pltpu.SMEM)


def dot(a, b, precision=None):
    return jnp.dot(a, b, preferred_element_type=F32, precision=precision)


def dot_nt(a, b, precision=None):
    return lax.dot_general(a, b, (((1,), (1,)), ((), ())), preferred_element_type=F32, precision=precision)


def dot_tn(a, b, precision=None):
    return lax.dot_general(a, b, (((0,), (0,)), ((), ())), preferred_element_type=F32, precision=precision)


def iota(shape, dim):
    return lax.broadcasted_iota(jnp.int32, shape, dim)


def mat(cond):
    return jnp.where(cond, 1.0, 0.0).astype(F32)


class Sizes:
    def __init__(self, n, tokens, heads_local, head_dim, ssd_local, state):
        self.n, self.t, self.hl, self.hd, self.ns = n, tokens, heads_local, head_dim, state
        self.s = n * tokens
        self.a = heads_local // n
        self.sizes = GROUPS if sum(GROUPS) == self.a else (self.a,)
        self.first = [sum(self.sizes[:g]) for g in range(len(self.sizes))]
        self.groups = len(self.sizes)
        natural = list(range(n))
        half_first = sorted(natural, key=lambda s: (s != 0, s != n // 2, s))
        self.shifts = [natural for _ in self.sizes]
        self.back_shifts = [half_first for _ in self.sizes]
        self.h = ssd_local // n
        self.hl_ssd = ssd_local
        self.mp = heads_local * head_dim // ssd_local
        self.f = self.a * head_dim
        self.r = -(-(self.h + 1) // 8) * 8
        self.rp = -(-self.r // 16) * 16
        self.features = self.f // head_dim
        self.v = -(-(self.features + 2) // 8) * 8
        self.rows = min(256, self.s)
        self.blocks = self.s // self.rows
        self.static = self.blocks <= 2
        self.parts = 2 if self.static and n % 2 == 0 else 1
        self.per = n // self.parts
        self.up, self.down, self.mid = 0, self.s, 2 * self.s
        self.pay = self.mid + 8 * n
        self.rate = self.pay + self.r * n
        self.weight = self.rate + self.r
        self.term_rows = self.weight + 8
        self.pay_rows = tokens + 2 * self.rp

    def sent_rows(self, g):
        return 3 * self.sizes[g] * self.t + (0 if g else self.pay_rows)

    def back_rows(self, g):
        rows = 3 * self.sizes[g] * self.t
        if g == 0:
            rows += self.t + self.rp + 2 * self.v
        return rows

    def rows_of(self, g, k, a):
        first = (k * self.sizes[g] + a) * self.t
        return slice(first, first + self.t)

    def lanes(self, g):
        return pl.ds(self.first[g] * self.hd, self.sizes[g] * self.hd)

    def each_block(self, body):
        if self.static:
            for i in range(self.blocks):
                body(i)
        else:

            @pl.loop(0, self.blocks)
            def _(i):
                body(i)

    def upto(self, i):
        return (i + 1) * self.rows if self.static else self.s

    def onward(self, i):
        return i * self.rows if self.static else 0

    def each_chunk(self, body):
        if self.static:
            for c in range(self.n):
                body(c)
        else:

            @pl.loop(0, self.n)
            def _(c):
                body(c)

    def chunk(self, c, base=0):
        return pl.ds(base + c * self.t if isinstance(c, int) else pl.multiple_of(base + c * self.t, self.t), self.t)

    def small(self, c, base, rows):
        return pl.ds(base + c * rows if isinstance(c, int) else pl.multiple_of(base + c * rows, 8), rows)

    def block(self, i):
        return pl.ds(i * self.rows if self.static else pl.multiple_of(i * self.rows, self.rows), self.rows)


def call(z, kernel, name, out_shape, in_specs, out_specs, scratch, args, flops=0, nbytes=0):
    return pl.pallas_call(
        functools.partial(kernel, z),
        name=name,
        out_shape=out_shape,
        in_specs=in_specs,
        out_specs=out_specs,
        scratch_shapes=scratch,
        compiler_params=pltpu.CompilerParams(vmem_limit_bytes=(VMEM_MIB if z.static else 56) * 1024 * 1024),
        cost_estimate=pl.CostEstimate(flops=flops, bytes_accessed=nbytes, transcendentals=0),
    )(*args)


def in_hbm(x):
    return pltpu.with_memory_space_constraint(x, pltpu.HBM)


class Copies:
    def __init__(self, sems):
        self.sems, self.count = sems, 0

    def start(self, source, target):
        one = pltpu.make_async_copy(source, target, self.sems.at[self.count])
        self.count += 1
        one.start()
        return one


def wait_all(copies):
    for one in copies:
        one.wait()


def split3(x):
    high = x.astype(BF16)
    rest = x - high.astype(F32)
    middle = rest.astype(BF16)
    return high, middle, (rest - middle.astype(F32)).astype(BF16)


def split2_dot(x, exact):
    high, low = split3(x)[:2]
    return dot(high, exact) + dot(low, exact)


def prep_kernel(z, qkv, b_in, c_in, step_in, labels_in, table_in, *refs):
    outs, refs = refs[: z.n * z.groups], refs[z.n * z.groups :]
    held, (parts, b, c, step, labels, table, sems) = refs[: z.groups], refs[z.groups :]
    me, core = lax.axis_index("context"), lax.axis_index("head")
    mover = Copies(sems)
    tiny = [
        mover.start(b_in.at[0], b),
        mover.start(c_in.at[0], c),
        mover.start(step_in.at[0], step),
        mover.start(labels_in, labels),
        mover.start(table_in, table),
    ]
    loads = [mover.start(qkv.at[k, 0], parts.at[k]) for k in range(3)]
    wait_all(tiny)
    onehot = mat(iota((table.shape[1], z.t), 0) == labels[...])
    target = dot(table[...], onehot, HIGHEST)
    mine = jnp.where(core == 0, b[...], c[...])
    end = 3 * z.sizes[0] * z.t
    for j in range(z.n):
        row = iota((z.r, z.hl_ssd), 0)
        pick = mat((iota((z.r, z.hl_ssd), 1) == j * z.h + row) & (row < z.h))
        pay = dot(pick, step[...], HIGHEST)
        pay = jnp.where(iota((z.r, z.t), 0) == z.h, target, pay)
        held[0][j, end : end + z.t] = mine
        held[0][j, end + z.t :] = jnp.zeros((2 * z.rp, z.t), BF16)
        for i, term in enumerate(split3(pay)[:2]):
            start = end + z.t + i * z.rp
            held[0][j, start : start + z.r] = term
    for k in range(3):
        loads[k].wait()
        turned = jnp.swapaxes(parts[k], 0, 1)
        for g in range(z.groups):
            for j in range(z.n):
                for a in range(z.sizes[g]):
                    held[g][j, z.rows_of(g, k, a), :] = turned[j * z.a + z.first[g] + a]
    for g in range(z.groups):
        for s in range(z.n):
            outs[g * z.n + s][...] = held[g][lax.rem(me + z.shifts[g][s], z.n)]


def prep(z, qkv, b, c, step, labels, table):
    args = [in_hbm(x) for x in (qkv, b, c, step, labels, table)]
    return call(
        z,
        prep_kernel,
        "prep",
        [SHAPE((z.sent_rows(g), z.hd), BF16) for g in range(z.groups) for _ in range(z.n)],
        [ANY] * 6,
        [VM] * (z.n * z.groups),
        [
            *[pltpu.VMEM((z.n, z.sent_rows(g), z.hd), BF16) for g in range(z.groups)],
            pltpu.VMEM((3, z.t, z.hl, z.hd), BF16),
            pltpu.VMEM((z.t, z.ns), BF16),
            pltpu.VMEM((z.t, z.ns), BF16),
            pltpu.VMEM(step.shape[1:], F32),
            pltpu.VMEM(labels.shape, jnp.int32),
            pltpu.VMEM(table.shape, F32),
            pltpu.SemaphoreType.DMA((8,)),
        ],
        args,
        nbytes=qkv.size * 4,
    )


def pick_kernel(z, *refs):
    ins, (mine, pay) = refs[: z.n], refs[z.n :]
    me = lax.axis_index("context")
    first = 3 * z.sizes[0] * z.t
    for s in range(z.n):
        source = lax.rem(me + z.n - z.shifts[0][s], z.n)
        mine[source] = ins[s][first : first + z.t]
        start = first + z.t
        terms = [ins[s][start + k * z.rp : start + k * z.rp + z.r].astype(F32) for k in range(2)]
        pay[source] = terms[0] + terms[1]


def pick(z, ins):
    return call(
        z,
        pick_kernel,
        "pick",
        (SHAPE((z.n, z.t, z.ns), BF16), SHAPE((z.n, z.r, z.t), F32)),
        [VM] * z.n,
        [VM] * 2,
        [],
        ins,
    )


def decay_kernel(z, mine, theirs, pay, rate, weight, terms, bc):
    n, t = z.n, z.t
    me, core = lax.axis_index("context"), lax.axis_index("head")
    heads = z.hl_ssd
    row, col = iota((z.r, heads), 0), iota((z.r, heads), 1)
    pick = mat((col == me * z.h + row) & (row < z.h))
    terms[z.rate : z.rate + z.r, :t] = dot_nt(pick, jnp.broadcast_to(rate[...], (t, heads)), HIGHEST)
    pick = mat(iota((8, z.hl), 1) == me * z.a + iota((8, z.hl), 0))
    terms[z.weight : z.weight + 8, : z.hd] = dot(pick, weight[...].astype(F32))
    rates = jnp.broadcast_to(rate[...], (8, heads))
    rates = dot(rates, mat(iota((heads, z.f), 0) == me * z.h + iota((heads, z.f), 1) // z.mp), HIGHEST)
    rates = rates[0:1]
    for c in range(n):
        bc[c, 0] = jnp.where(core == 0, mine[c], theirs[c])
        bc[c, 1] = jnp.where(core == 0, theirs[c], mine[c])
        terms[z.pay + c * z.r : z.pay + (c + 1) * z.r, :t] = pay[c]
    causal = iota((t, t), 0) >= iota((t, t), 1)
    lower = mat(causal)
    spread_heads = mat(iota((z.r, z.f), 0) == iota((z.r, z.f), 1) // z.mp)

    def chunk(c):
        steps = terms[z.small(c, z.pay, z.r), :t]
        cum = dot(dot_nt(lower, steps, HIGHEST), spread_heads, HIGHEST) * (-rates)
        half = 0.5 * cum[t - 1 : t]
        terms[z.chunk(c, z.up), :] = jnp.exp(cum - half)
        terms[z.chunk(c, z.down), :] = jnp.exp(half - cum)
        terms[z.small(c, z.mid, 8), :] = jnp.broadcast_to(jnp.exp(half), (8, z.f))
        inner = split3(jnp.where(causal, dot_nt(bc[c, 1], bc[c, 0]), 0.0))
        bc[c, 2] = inner[0]
        bc[c, 3] = inner[1]

    z.each_chunk(chunk)


def decay(z, mine, theirs, pay, rate, weight):
    return call(
        z,
        decay_kernel,
        "decay",
        (SHAPE((z.term_rows, z.f), F32), SHAPE((z.n, 4, z.t, z.ns), BF16)),
        [VM] * 5,
        [VM] * 2,
        [],
        (mine, theirs, pay, rate, weight),
        nbytes=8 * z.s * z.f,
    )


def attend_kernel(z, g, *refs):
    n, t, count = z.n, z.t, z.sizes[g]
    ins, refs = refs[:n], refs[n:]
    prob, attended, held = refs
    me = lax.axis_index("context")
    for s in range(n):
        held[lax.rem(me + n - z.shifts[g][s], n)] = ins[s][: 3 * count * t]

    def rows_upto(k, a, width):
        return held[: width // t, z.rows_of(g, k, a), :].reshape(width, z.hd)

    def rows_block(k, a, i):
        per = z.rows // t
        return held[pl.ds(i * per, per), z.rows_of(g, k, a), :].reshape(z.rows, z.hd)

    factor = LOG2E / math.sqrt(z.hd)
    for a in range(count):

        def attend(i):
            width = z.upto(i)
            rows = z.block(i)
            scores = dot_nt(rows_block(0, a, i), rows_upto(1, a, width))
            keep = iota((z.rows, width), 1) <= i * z.rows + iota((z.rows, width), 0)
            scores = jnp.where(keep, scores, MASK_FILL)
            weight = jnp.exp2((scores - jnp.max(scores, axis=1, keepdims=True)) * factor)
            weight = (weight * (1.0 / jnp.sum(weight, axis=1, keepdims=True))).astype(BF16)
            prob[a, rows, :width] = weight
            attended[rows, a * z.hd : (a + 1) * z.hd] = dot(weight, rows_upto(2, a, width)).astype(BF16)

        z.each_block(attend)


def attend(z, g, ins):
    count = z.sizes[g]
    outs = (
        SHAPE((count, z.s, z.s), BF16),
        SHAPE((z.s, count * z.hd), BF16),
        SHAPE((z.n, 3 * count * z.t, z.hd), BF16),
    )
    return call(
        z,
        lambda z, *refs: attend_kernel(z, g, *refs),
        "attend_%d" % g,
        outs,
        [VM] * z.n,
        [VM] * 3,
        [],
        ins,
        flops=count * z.s * z.s * z.hd * 4,
        nbytes=count * z.s * z.s * 8,
    )


def ssd_kernel(z, *refs):
    n, t = z.n, z.t
    ins, refs = refs[: z.groups], refs[z.groups :]
    terms, bc, saved, value, state_low, adds = refs
    same_head = mat(iota((z.hd, z.hd), 0) // z.mp == iota((z.hd, z.hd), 1) // z.mp).astype(BF16)

    def enter(c):
        rows = z.chunk(c)
        attended = jnp.concatenate([one[rows, :] for one in ins], axis=1)
        high, low = split3(terms[z.chunk(c, z.down), :] * attended.astype(F32))[:2]
        saved[0, rows, :] = high
        saved[5, rows, :] = low
        adds[rows, :] = dot_tn(bc[c, 0], high) + dot_tn(bc[c, 0], low)

    z.each_chunk(enter)

    def step(c, state):
        m = terms[z.small(c, z.mid, 8), :][0:1]
        state = m * state
        high, low = split3(state)[:2]
        saved[3, z.chunk(c), :] = high
        state_low[z.chunk(c), :] = low
        return m * (state + adds[z.chunk(c), :])

    state = jnp.zeros((z.ns, z.f), F32)
    if z.static:
        for c in range(n):
            state = step(c, state)
    else:
        lax.fori_loop(0, n, step, state)

    def leave(c):
        rows = z.chunk(c)
        up = terms[z.chunk(c, z.up), :]
        left = [bc[c, k] for k in (2, 2, 3, 1, 1)]
        right = [saved[0, rows, :], saved[5, rows, :], saved[0, rows, :], saved[3, rows, :], state_low[rows, :]]
        y = up * dot(jnp.concatenate(left, axis=1), jnp.concatenate(right, axis=0))
        total = jnp.zeros((t, z.hd), F32)
        for a in range(z.a):
            part = slice(a * z.hd, (a + 1) * z.hd)
            ya = y[:, part]
            weight = terms[z.weight + a : z.weight + a + 1, : z.hd]
            scale = lax.rsqrt(split2_dot(ya * ya, same_head) * (1.0 / z.mp) + NORM_EPS)
            unit = ya * scale
            term = unit * weight
            total = total + term
            mean = split2_dot(term, same_head) * (1.0 / z.mp)
            saved[1, rows, part] = unit.astype(BF16)
            slope = split3(up[:, part] * scale * (weight - unit * mean))
            saved[2, rows, part] = slope[0]
            saved[4, rows, part] = slope[1]
        high, low = split3(total)[:2]
        ones = jnp.ones((8, z.hd), BF16)
        value[:, rows] = (dot_nt(ones, high) + dot_nt(ones, low))[0:1]

    z.each_chunk(leave)


def last_kernel(z, *refs):
    n, g = z.n, z.groups - 1
    ins, before, refs = refs[:n], refs[n : n + g], refs[n + g :]
    terms, bc, prob, attended, held, *rest = refs
    attend_kernel(z, g, *ins, prob, attended, held)
    ssd_kernel(z, *before, attended, terms, bc, *rest)


def attend_and_ssd(z, ins, before, terms, bc):
    count = z.sizes[-1]
    return call(
        z,
        last_kernel,
        "attend_and_ssd",
        (
            SHAPE((count, z.s, z.s), BF16),
            SHAPE((z.s, count * z.hd), BF16),
            SHAPE((z.n, 3 * count * z.t, z.hd), BF16),
            SHAPE((6, z.s, z.f), BF16),
            SHAPE((1, z.s), F32),
        ),
        [VM] * (z.n + z.groups + 1),
        [VM] * 5,
        [
            pltpu.VMEM((z.s, z.f), BF16),
            pltpu.VMEM((z.n * z.ns, z.f), F32),
        ],
        (*ins, *before, terms, bc),
        flops=z.s * z.f * z.ns * 20,
        nbytes=z.s * z.f * 32,
    )


def ssd_pre_kernel(z, part, bc, saved, w_sums, straddled, down_sums):
    t = z.t
    causal = iota((t, t), 0) >= iota((t, t), 1)
    per_head = mat(iota((z.f, t), 1) == iota((z.f, t), 0) // z.mp).astype(BF16)

    def chunk(c):
        rows, here = z.chunk(c), z.chunk(c - part * z.per)
        sc, sl, xc, xl = saved[2, rows, :], saved[4, rows, :], saved[0, rows, :], saved[5, rows, :]
        carried = dot(bc[c, 1], saved[3, rows, :])
        down_sums[here, :] = dot(((sc.astype(F32) + sl.astype(F32)) * carried).astype(BF16), per_head)
        inner = bc[c, 2].astype(F32)
        w_sum = jnp.zeros((t, t), F32)
        for k in range(z.h):
            first = k * z.mp // z.hd * z.hd
            mine = iota((t, z.hd), 1) // z.mp == k % (z.hd // z.mp)
            pair = slice(first, first + z.hd)
            x_head = jnp.where(mine, xc[:, pair], jnp.zeros((), BF16))
            x_low = jnp.where(mine, xl[:, pair], jnp.zeros((), BF16))
            left = jnp.concatenate([sc[:, pair], sl[:, pair], sc[:, pair]], axis=1)
            w = jnp.where(causal, dot_nt(left, jnp.concatenate([x_head, x_head, x_low], axis=1)), 0.0)
            w_sum += w
            straddled[here, k * t : (k + 1) * t] = (w * inner).astype(BF16)
        w_sums[here, :] = w_sum

    if z.parts > 1:
        for c in range(part * z.per, (part + 1) * z.per):
            chunk(c)
    else:
        z.each_chunk(chunk)


def ssd_pre(z, part, bc, saved):
    rows = z.per * z.t
    return call(
        z,
        lambda z, *refs: ssd_pre_kernel(z, part, *refs),
        "ssd_pre_%d" % part,
        (SHAPE((rows, z.t), F32), SHAPE((rows, z.h * z.t), BF16), SHAPE((rows, z.t), F32)),
        [VM] * 2,
        [VM] * 3,
        [],
        (bc, saved),
        flops=rows * z.f * z.ns * 20,
        nbytes=rows * z.f * 8,
    )


def ssd_back_kernel(z, *refs):
    n, t = z.n, z.t
    lengths, values, refs = refs[0], refs[1 : n + 1], refs[n + 1 :]
    terms, bc, saved, refs = *refs[:3], refs[3:]
    early, refs = refs[: 3 * z.parts], refs[3 * z.parts :]

    def made(kind, c):
        part = c // z.per if z.parts > 1 else 0
        return early[3 * part + kind][z.chunk(c - part * z.per), :]

    grads, keep_out, give_out, step_out, vec, refs = *refs[:5], refs[5:]
    d, adds, dstates, through, errors = refs
    me, core = lax.axis_index("context"), lax.axis_index("head")
    length = lengths[lax.axis_index("rollout")]
    value = values[0][...]
    for s in range(1, n):
        value = value + values[s][...]
    row_id, col_id = iota((t, t), 0), iota((t, t), 1)
    strict = row_id > col_id
    after = mat(col_id >= row_id).astype(BF16)
    before = mat(strict).astype(BF16)
    per_head = mat(iota((z.f, t), 1) == iota((z.f, t), 0) // z.mp).astype(BF16)
    per_row = mat(iota((z.h * t, t), 1) == iota((z.h * t, t), 0) // t).astype(BF16)
    vec[...] = jnp.zeros_like(vec)

    def pays(c):
        return terms[z.small(c, z.pay, z.r), :t]

    def enter(c):
        rows = z.chunk(c)
        if z.static:
            value_row = value[:, c * t : (c + 1) * t]
        else:
            value_row = jnp.zeros((1, t), F32)
            for j in range(n):
                value_row = jnp.where(c == j, value[:, j * t : (j + 1) * t], value_row)
        valid = c * t + iota((1, t), 1) < length
        error = jnp.where(valid, value_row - pays(c)[z.h : z.h + 1], 0.0)
        vec[z.features + 1 : z.features + 2, :] += 0.5 * error * error
        column = jnp.transpose(jnp.broadcast_to(error, (t, t)))
        errors[0, rows, :] = jnp.broadcast_to(error, (t, t))
        errors[1, rows, :] = column
        wide = jnp.concatenate([column] * (z.f // t), axis=1)
        dc = split3(wide * (saved[2, rows, :].astype(F32) + saved[4, rows, :].astype(F32)))[:2]
        d[0, rows, :] = dc[0]
        d[1, rows, :] = dc[1]
        adds[rows, :] = dot_tn(bc[c, 1], dc[0]) + dot_tn(bc[c, 1], dc[1])
        high, low = split3(error)[:2]
        pair = jnp.concatenate([high, low, jnp.zeros((6, t), BF16)], axis=0)
        weight_grad = dot(pair, saved[1, rows, :])
        weight_grad = weight_grad[0:1] + weight_grad[1:2]
        for a in range(z.features):
            vec[a : a + 1, :] += weight_grad[:, a * z.hd : (a + 1) * z.hd]

    z.each_chunk(enter)

    def carry(c, dstate):
        m = terms[z.small(c, z.mid, 8), :][0:1]
        rows = z.chunk(c)
        dstate = m * dstate
        dstates[rows, :] = dstate.astype(BF16)
        sums = jnp.sum(dstate * saved[3, rows, :].astype(F32), axis=0, keepdims=True)
        through[z.small(c, 0, 8), :] = jnp.broadcast_to(sums, (8, z.f))
        return m * (dstate + adds[rows, :])

    dstate = jnp.zeros((z.ns, z.f), F32)
    if z.static:
        for c in range(n - 1, -1, -1):
            dstate = carry(c, dstate)
    else:
        lax.fori_loop(0, n, lambda k, v: carry(n - 1 - k, v), dstate)

    def leave(c):
        rows = z.chunk(c)
        b, cp, inner = bc[c, 0], bc[c, 1], bc[c, 2]
        dc, dl = d[0, rows, :], d[1, rows, :]
        xc, state_in, dstate_in = saved[0, rows, :], saved[3, rows, :], dstates[rows, :]
        local = dot_tn(inner, dc) + dot_tn(inner, dl)
        outer = dot(b, dstate_in)
        grads[rows, :] = (terms[z.chunk(c, z.down), :] * (local + outer)).astype(BF16)
        grad_c = dot_nt(dc, state_in) + dot_nt(dl, state_in)
        grad_b = dot_nt(xc, dstate_in)
        down_sum = errors[1, rows, :] * made(2, c)
        up_sum = dot((xc.astype(F32) * outer).astype(BF16), per_head)
        straddle = dot(jnp.where(col_id >= row_id, errors[0, rows, :], 0.0).astype(BF16), made(1, c))
        straddle = jnp.concatenate(
            [jnp.where(strict, straddle[:, k * t : (k + 1) * t], 0.0).astype(BF16) for k in range(z.h)], axis=1
        )
        sums = [*split3(down_sum)[:2], *split3(up_sum)[:2]]
        gain = dot(
            jnp.concatenate([after, after, before, before], axis=1), jnp.concatenate(sums, axis=0)
        ) + dot(straddle, per_row)
        gain = gain + split2_dot(through[z.small(c, 0, 8), :], per_head)[0:1]
        w_low = (errors[1, rows, :] * made(0, c)).astype(BF16)
        grad_c += dot(w_low, b)
        grad_b += dot_tn(w_low, cp)
        keep_out[c] = jnp.where(core == 0, grad_b, grad_c)
        give_out[c] = jnp.where(core == 0, grad_c, grad_b).astype(BF16)
        gain_rows = jnp.transpose(gain)[: z.r]
        step_out[c] = -terms[z.rate : z.rate + z.r, :t] * gain_rows
        rate_part = jnp.sum(pays(c) * gain_rows, axis=1, keepdims=True)
        lane = (iota((z.r, t), 1) == me * z.h + iota((z.r, t), 0)) & (iota((z.r, t), 0) < z.h)
        vec[z.features : z.features + 1, :] -= jnp.sum(jnp.where(lane, rate_part, 0.0), axis=0, keepdims=True)

    z.each_chunk(leave)


def ssd_back(z, lengths, values, terms, bc, saved, early):
    outs = (
        SHAPE((z.s, z.f), BF16),
        SHAPE((z.n, z.t, z.ns), F32),
        SHAPE((z.n, z.t, z.ns), BF16),
        SHAPE((z.n, z.r, z.t), F32),
        SHAPE((z.v, z.t), F32),
    )
    scratch = [
        pltpu.VMEM((2, z.s, z.f), BF16),
        pltpu.VMEM((z.n * z.ns, z.f), F32),
        pltpu.VMEM((z.n * z.ns, z.f), BF16),
        pltpu.VMEM((z.n * 8, z.f), F32),
        pltpu.VMEM((2, z.s, z.t), F32),
    ]
    return call(
        z,
        ssd_back_kernel,
        "ssd_back",
        outs,
        [SM] + [VM] * (z.n + 3 + 3 * z.parts),
        [VM] * 5,
        scratch,
        (lengths, *values, terms, bc, saved, *early),
        flops=z.s * z.f * z.ns * 20,
        nbytes=z.s * z.f * 32,
    )


def attend_back_kernel(z, g, *refs):
    n, t, count = z.n, z.t, z.sizes[g]
    held, prob, grad_in, refs = *refs[:3], refs[3:]
    grad = grad_in.at[:, z.lanes(g)]
    if g == 0:
        keep, other, step, vec, refs = *refs[:4], refs[4:]
    else:
        refs = refs[1:]
    outs, refs = refs[:n], refs[n:]
    result, dscore = refs
    me = lax.axis_index("context")
    if g == 0:
        end = 3 * count * t
        for j in range(n):
            result[j, end : end + t] = (keep[j] + other[j].astype(F32)).astype(BF16)
            result[j, end + t :] = jnp.zeros((z.rp + 2 * z.v, t), BF16)
            result[j, end + t : end + t + z.r] = step[j].astype(BF16)
            result[j, end + t + z.rp :] = jnp.concatenate(split3(vec[...])[:2], axis=0)
    factor = 1.0 / math.sqrt(z.hd)
    per = z.rows // t

    def rows_span(k, a, first, last):
        return held[first // t : last // t, z.rows_of(g, k, a), :].reshape(last - first, z.hd)

    def store(k, a, i, x):
        result[pl.ds(i * per, per), z.rows_of(g, k, a), :] = x.astype(BF16).reshape(per, t, z.hd)

    for a in range(count):
        lanes = slice(a * z.hd, (a + 1) * z.hd)

        def by_query(i):
            width, rows = z.upto(i), z.block(i)
            p = prob[a, rows, :width].astype(F32)
            dp = dot_nt(grad[rows, lanes], rows_span(2, a, 0, width))
            product = p * dp
            ds = (product - p * jnp.sum(product, axis=1, keepdims=True)).astype(BF16)
            dscore[a, rows, :width] = ds
            store(0, a, i, dot(ds, rows_span(1, a, 0, width)) * factor)

        z.each_block(by_query)

        def by_key(j):
            start, cols = z.onward(j), z.block(j)
            store(1, a, j, dot_tn(dscore[a, start:, cols], rows_span(0, a, start, z.s)) * factor)
            store(2, a, j, dot_tn(prob[a, start:, cols], grad[start:, lanes]))

        z.each_block(by_key)
    for s in range(n):
        outs[s][...] = result[lax.rem(me + z.back_shifts[g][s], n)]


def attend_back(z, g, qkv, prob, grad, small):
    count = z.sizes[g]
    rows = z.back_rows(g)
    scratch = [
        pltpu.VMEM((z.n, rows, z.hd), BF16),
        pltpu.VMEM((count, z.s, z.s), BF16),
    ]
    return call(
        z,
        lambda z, *refs: attend_back_kernel(z, g, *refs),
        "attend_back_%d" % g,
        [SHAPE((rows, z.hd), BF16)] * z.n,
        [VM] * 3 + ([ANY] if g else [VM] * len(small)),
        [VM] * z.n,
        scratch,
        (qkv, prob, grad, *small),
        flops=count * z.s * z.s * z.hd * 8,
        nbytes=count * z.s * z.s * 8,
    )


def unpack_kernel(z, *refs):
    n, t = z.n, z.t
    ins, (proj, step, vecs) = refs[:n], refs[n:]
    me = lax.axis_index("context")
    parts = [ins[s][3 * z.sizes[0] * t :] for s in range(n)]
    total = jnp.zeros((t, z.ns), F32)
    steps = jnp.zeros((n * z.h, t), F32)
    for s in range(n):
        total = total + parts[s][:t].astype(F32)
        source = lax.rem(me + n - z.back_shifts[0][s], n)
        row, col = iota((n * z.h, z.r), 0), iota((n * z.h, z.r), 1)
        place = mat((row == source * z.h + col) & (col < z.h)).astype(BF16)
        steps = steps + dot(place, parts[s][t : t + z.r])
        vec = parts[s][t + z.rp :].astype(F32)
        vecs[source] = vec[: z.v] + vec[z.v :]
    proj[...] = total
    step[0] = steps


def unpack(z, parts):
    return call(
        z,
        unpack_kernel,
        "unpack",
        (SHAPE((z.t, z.ns), F32), SHAPE((1, z.n * z.h, z.t), F32), SHAPE((z.n, z.v, z.t), F32)),
        [VM] * z.n,
        [VM] * 3,
        [],
        parts,
    )


def choose_kernel(z, lengths, mine, theirs, *refs):
    vecs, (b, c, weight, rate, loss) = refs[:-5], refs[-5:]
    vecs = sum([one[...] for one in vecs[1:]], vecs[0][...])
    core = lax.axis_index("head")
    b[0] = jnp.where(core == 0, mine[...], theirs[...])
    c[0] = jnp.where(core == 0, theirs[...], mine[...])
    valid = lengths[0]
    for k in range(1, lengths.shape[0]):
        valid = valid + lengths[k]
    rates = jnp.zeros((1, z.t), F32)
    for j in range(z.n):
        weight[j] = vecs[j, : z.features]
        rates = rates + vecs[j, z.features : z.features + 1]
    losses = vecs[0, z.features + 1 : z.features + 2]
    loss[...] = jnp.sum(losses, axis=1, keepdims=True) / valid.astype(F32)
    rate[...] = rates[:, : z.n * z.h]


def choose(z, lengths, mine, theirs, vecs):
    return call(
        z,
        choose_kernel,
        "choose",
        (
            SHAPE((1, z.t, z.ns), F32),
            SHAPE((1, z.t, z.ns), F32),
            SHAPE((z.n, z.features, z.hd), F32),
            SHAPE((1, z.n * z.h), F32),
            SHAPE((1, 1), F32),
        ),
        [SM] + [VM] * (2 + len(vecs)),
        [VM] * 5,
        [],
        (lengths, mine, theirs, *vecs),
    )


def finish_kernel(z, *refs):
    count = z.n * z.groups
    ins, out, refs = refs[:count], refs[count], refs[count + 1 :]
    held, (turned, sems) = refs[: z.groups], refs[z.groups :]
    me = lax.axis_index("context")
    mover = Copies(sems)
    for g in range(z.groups):
        for s in range(z.n):
            held[g][lax.rem(me + z.n - z.back_shifts[g][s], z.n)] = ins[g * z.n + s][: 3 * z.sizes[g] * z.t]
    stores = []
    for k in range(3):
        heads = [
            held[g][j, z.rows_of(g, k, a), :]
            for j in range(z.n)
            for g in range(z.groups)
            for a in range(z.sizes[g])
        ]
        turned[k] = jnp.swapaxes(jnp.stack(heads), 0, 1)
        stores.append(mover.start(turned.at[k], out.at[k, 0]))
    wait_all(stores)


def finish(z, parts):
    return call(
        z,
        finish_kernel,
        "finish",
        SHAPE((3, 1, z.t, z.hl, z.hd), BF16),
        [VM] * (z.n * z.groups),
        ANY,
        [
            *[pltpu.VMEM((z.n, 3 * k * z.t, z.hd), BF16) for k in z.sizes],
            pltpu.VMEM((3, z.t, z.hl, z.hd), BF16),
            pltpu.SemaphoreType.DMA((3,)),
        ],
        parts,
        nbytes=12 * z.t * z.hl * z.hd,
    )


def shift(x, axis, size, step):
    return lax.ppermute(x, axis, [(i, (i + step) % size) for i in range(size)])


def spread(parts, axis, shifts):
    return [parts[0]] + [shift(x, axis, len(parts), s) for x, s in zip(parts[1:], shifts[1:])]


def partners(x, axis, step):
    return lax.ppermute(x, axis, [(i, i ^ step) for i in range(lax.axis_size(axis))])


def local(qkv, ssd_b, ssd_c, step_size, decay_rate, value_weight, returns, step_labels, lengths):
    n = lax.axis_size("context")
    z = Sizes(n, qkv.shape[2], qkv.shape[3], qkv.shape[4], step_size.shape[2], ssd_b.shape[2])

    sends = prep(z, qkv, ssd_b, ssd_c, jnp.swapaxes(step_size, 1, 2), step_labels, returns)
    arrived = [spread(sends[g * n : (g + 1) * n], "context", z.shifts[g]) for g in range(z.groups)]
    mine, pay = pick(z, arrived[0])
    theirs = shift(mine, "head", 2, 1)
    attended = [attend(z, g, arrived[g]) for g in range(z.groups - 1)]
    terms, bc = decay(z, mine, theirs, pay, decay_rate.reshape(1, -1), value_weight.reshape(z.hl, z.hd))
    *last, saved, value = attend_and_ssd(z, arrived[-1], [x[1] for x in attended], terms, bc)
    attended.append(last)
    early = ssd_pre(z, 0, bc, saved)
    other, *early = lax.optimization_barrier((shift(value, "head", 2, 1), *early))
    for part in range(1, z.parts):
        early += ssd_pre(z, part, bc, saved)
    value = value + other
    values = [value] + [partners(value, "context", s) for s in range(1, n)]
    grad, keep, give, steps, vec = ssd_back(z, lengths, values, terms, bc, saved, early)
    finals, small = [], [keep, shift(give, "head", 2, 1), steps, vec]
    for g in range(z.groups):
        back = attend_back(z, g, attended[g][2], attended[g][0], grad, small)
        finals.append(spread(back, "context", z.back_shifts[g]))
        small = back[:1]
    proj, step_grad, vecs = unpack(z, finals[0])
    other = shift(proj, "head", 2, 1)
    step = 1
    vecs = [vecs]
    while step < lax.axis_size("rollout"):
        total = sum(vecs[1:], vecs[0])
        vecs = [total, partners(total, "rollout", step)]
        step *= 2
    b_grad, c_grad, weight_grad, rate_grad, loss = choose(z, lengths, proj, other, vecs)
    qkv_grad = finish(z, [x for part in finals for x in part])
    return (
        loss.reshape(()),
        qkv_grad,
        b_grad,
        c_grad,
        jnp.swapaxes(step_grad, 1, 2),
        rate_grad.reshape(-1),
        weight_grad.reshape(-1),
    )


def solution(mesh):
    in_specs = (
        P(None, "rollout", "context", "head", None),
        P("rollout", "context", None),
        P("rollout", "context", None),
        P("rollout", "context", "head"),
        P("head"),
        P("head"),
        P("rollout", None),
        P("rollout", "context"),
        P(),
    )
    out_specs = (
        P(),
        P(None, "rollout", "context", "head", None),
        P("rollout", "context", None),
        P("rollout", "context", None),
        P("rollout", "context", "head"),
        P("head"),
        P("head"),
    )
    return jax.shard_map(local, mesh=mesh, in_specs=in_specs, out_specs=out_specs, check_vma=False)
```
